32 devices in a mesh: blk: 4 (over y, x), elem: 8 (over z, core).
Axes of the slice: x: 2, y: 2, z: 4, core: 2. Of those that a mesh axis runs over, the one named last changes fastest.
Arguments:
- state: float32 [256, 125, 16, 128], P('blk', None, 'elem'), may hold values from -18 to 18
- rhs: float32 [256, 125, 16, 128], P('blk', None, 'elem'), may hold values from -6 to 6
- to_modal: float32 [125, 125], replicated, may hold values from -1 to 2
- viscous_op: float32 [125, 125], replicated, may hold values from -0.5 to 0.5
- sweep_gain: float32 [256, 125, 125], P('blk'), may hold values from -1 to 1.2
- inv_blocks: float32 [256, 125, 125], P('blk'), may hold values from -0.125 to 0.125
Outputs:
- line_solution: float32 [256, 125, 16, 128], P(('blk', 'elem'))
The draws below stay inside these ranges and needn't reach their ends.
All inputs are finite; a program needn't handle non-finite values.
Results may differ from the reference program's by a relative error of at most 0.0003.
Values sent between devices are 32-bit elements; how exact they have to be, the bound alone decides.
No kernel may reach another device: no remote copies, remote signals or barrier semaphores. Data moves between devices by JAX's collectives and lax.ppermute only.
A program may use at most 128 MiB of HBM per device.

```python
import math
import jax
import jax.numpy as jnp
from jax import lax

ORDER = 4
NODES = 125
AX = 128
NAZ = 256
RAD = 16


def draw_state(key, part):
    first, second = jax.random.split(key)
    base = jnp.clip(jax.random.normal(first, (NAZ, NODES, RAD, AX), jnp.float32), -6.0, 6.0)
    spread = jnp.exp(jax.random.uniform(second, (NAZ, 1, RAD, AX), jnp.float32, math.log(0.1), math.log(3.0)))
    nodeid = jnp.arange(NODES).reshape(1, NODES, 1, 1)
    return base * jnp.where(nodeid >= ORDER ** 3, spread, 1.0)


def draw_to_modal(key, part):
    noise = jnp.clip(jax.random.normal(key, (NODES, NODES), jnp.float32), -6.0, 6.0)
    return jnp.eye(NODES, dtype=jnp.float32) + 0.3 / math.sqrt(NODES) * noise


def draw_sweep_gain(key, part):
    first, second, third, fourth, fifth, sixth = jax.random.split(jax.random.fold_in(key, 7), 6)
    upper = math.log(0.1)
    rates = jnp.exp(jax.random.uniform(first, (1, NODES, 1), jnp.float32, math.log(0.5 / NAZ), upper))
    factor = jax.random.uniform(second, (NAZ, 1, 1), jnp.float32, 0.5, 1.5)
    diagonal = jnp.exp(-rates * factor)
    order_nodes = jax.random.permutation(fourth, NODES).astype(jnp.int32)
    position = jnp.argsort(order_nodes).astype(jnp.int32)
    parity = position % 2
    mate_position = position + 1 - 2 * parity
    paired = mate_position < NODES
    mate_position = jnp.where(paired, mate_position, position)
    partner = order_nodes[mate_position]
    magnitude = jax.random.uniform(fifth, (NAZ, NODES), jnp.float32, 0.3, 1.2)
    turn_sign = jnp.where(jax.random.uniform(sixth, (NAZ, NODES), jnp.float32) < 0.5, -1.0, 1.0)
    pair_angle = (magnitude * turn_sign)[:, position // 2]
    pair_angle = jnp.where(paired[None, :], pair_angle, 0.0)
    row_sign = jnp.where(parity == 0, 1.0, -1.0).astype(jnp.float32)
    columns = jnp.arange(NODES).reshape(1, 1, NODES)
    rows = jnp.arange(NODES).reshape(1, NODES, 1)
    on_self = (columns == rows).astype(jnp.float32)
    on_mate = (columns == partner.reshape(1, NODES, 1)).astype(jnp.float32) * (1.0 - on_self)
    rotation = jnp.cos(pair_angle)[:, :, None] * on_self + (row_sign[None, :] * jnp.sin(pair_angle))[:, :, None] * on_mate
    noise = jnp.clip(jax.random.normal(third, (NAZ, NODES, NODES), jnp.float32), -4.0, 4.0)
    return 0.02 / math.sqrt(NODES) * noise + diagonal * rotation


def shard_levels(stream_key, shape, shards, low, largest):
    loudness = 1.0
    for dim, blocks in shards:
        steps = jax.random.uniform(jax.random.fold_in(jax.random.fold_in(stream_key, 6), dim), (blocks,), jnp.float32, low / len(shards), largest / len(shards))
        loudness = loudness * jnp.repeat(jnp.exp(steps), shape[dim] // blocks).reshape((-1,) + (1,) * (len(shape) - 1 - dim))
    return loudness


def gaussian(rng, shape, deviation, limit, shards=(), kind=jnp.bfloat16):
    array = jax.random.normal(rng, shape, jnp.float32) * deviation
    if len(shards) > 0:
        array = shard_levels(rng, shape, shards, -0.22, 0.18) * array
    return jnp.clip(array, min=-limit, max=limit).astype(kind)


def setup_inputs(seed: int = 0) -> dict:
    arg_keys = jax.random.split(jax.random.key(seed), 7)
    state = draw_state(jax.random.fold_in(arg_keys[6], 71), 0)
    rhs = gaussian(arg_keys[1], (NAZ, NODES, RAD, AX), 1.0, 6.0, ((0, 4), (2, 8)), jnp.float32)
    to_modal = draw_to_modal(jax.random.fold_in(arg_keys[6], 71), 0)
    viscous_op = gaussian(arg_keys[3], (NODES, NODES), NODES ** -0.5, 0.5, (), jnp.float32)
    sweep_gain = draw_sweep_gain(jax.random.fold_in(arg_keys[6], 71), 0)
    inv_blocks = gaussian(arg_keys[5], (NAZ, NODES, NODES), (NODES * 16) ** -0.5, 0.125, ((0, 4),), jnp.float32)
    return dict(state=state, rhs=rhs, to_modal=to_modal, viscous_op=viscous_op, sweep_gain=sweep_gain, inv_blocks=inv_blocks)


def reference(state, rhs, to_modal, viscous_op, sweep_gain, inv_blocks):
    highest = lax.Precision.HIGHEST
    modal = jnp.einsum('mn,knja->kmja', to_modal, state, precision=highest)
    squares = modal * modal
    upper = jnp.sum(squares[:, ORDER ** 3:], axis=1) / NODES
    energy = jnp.mean(squares, axis=1) + 1e-6
    sensor = upper / energy
    padded = jnp.pad(sensor, ((0, 0), (1, 1), (0, 0)))
    smooth = (4.0 * sensor + jnp.roll(sensor, 1, 0) + jnp.roll(sensor, -1, 0) + padded[:, 2:] + padded[:, :-2]) / 8.0
    viscous = jnp.einsum('mn,knja->kmja', viscous_op, state, precision=highest)
    force = rhs + smooth[:, None] * viscous
    coupled = jnp.einsum('kmn,knja->kmja', inv_blocks, force, precision=highest)

    def sweep_step(field, inputs):
        matrix, source = inputs
        field = jnp.einsum('mn,nja->mja', matrix, field, precision=highest) + source
        return field, field

    start = jnp.zeros(coupled.shape[1:], jnp.float32)
    cycle_end, _ = lax.scan(sweep_step, start, (sweep_gain, coupled))
    _, solved = lax.scan(sweep_step, cycle_end, (sweep_gain, coupled))
    return solved
```

```python
import functools

import jax
import jax.numpy as jnp
from jax import lax
from jax.experimental import pallas as pl
from jax.experimental.pallas import tpu as pltpu
from jax.sharding import PartitionSpec as P

ORDER = 4
F32 = jnp.float32
BF16 = jnp.bfloat16
VMEM_LIMIT = 36 * 1024 * 1024
TILE = 8
LANES = 128


def operand_left(a):
    high = a.astype(BF16)
    low = (a - high.astype(F32)).astype(BF16)
    return jnp.concatenate([jnp.concatenate([high, high], axis=1), jnp.concatenate([low, low], axis=1)], axis=0)


def operand_right(x):
    high = x.astype(BF16)
    return jnp.concatenate([high, (x - high.astype(F32)).astype(BF16)], axis=0)


def product(left, right):
    both = jnp.dot(left, right, preferred_element_type=F32)
    half = left.shape[0] // 2
    return both[:half] + both[half:]


def spec_any():
    return pl.BlockSpec(memory_space=pl.ANY)


def spec_vmem():
    return pl.BlockSpec(memory_space=pltpu.VMEM)


def spec_smem():
    return pl.BlockSpec(memory_space=pltpu.SMEM)


def call(kernel, name, outs, in_specs, out_specs, scratch, flops, nbytes, aliases=None):
    return pl.pallas_call(
        kernel,
        name=name,
        out_shape=outs,
        in_specs=in_specs,
        out_specs=out_specs,
        scratch_shapes=scratch,
        input_output_aliases=aliases or {},
        compiler_params=pltpu.CompilerParams(vmem_limit_bytes=VMEM_LIMIT),
        cost_estimate=pl.CostEstimate(flops=int(flops), bytes_accessed=int(nbytes), transcendentals=0),
    )


def f32(*shape):
    return jax.ShapeDtypeStruct(shape, F32)


def up(value, unit):
    return -(-value // unit) * unit


class Sizes:
    def __init__(self, state, segments, groups):
        count, self.nodes, self.rows, self.ax = state.shape
        self.count = count
        self.segments = segments
        self.groups = groups
        self.steps = count // segments
        self.cols = self.rows * self.ax
        self.height = self.nodes * self.rows
        self.pad = up(self.nodes, LANES)
        self.spill = up((self.pad - self.nodes) * self.rows, TILE)
        self.flops = 2 * 4 * self.pad * self.pad * self.cols

    def window(self, low, high):
        first = low * self.height // TILE * TILE
        return first, up(high * self.height, TILE) - first

    def message(self, count):
        return up(count * self.height, TILE)

    def rows_masked(self, x):
        cut = self.nodes // TILE * TILE
        rest = x[cut:]
        inside = lax.broadcasted_iota(jnp.int32, rest.shape, 0) < self.nodes - cut
        return jnp.concatenate([x[:cut], jnp.where(inside, rest, 0.0)], axis=0)

    def square(self, x):
        x = jnp.concatenate([x, jnp.zeros((self.nodes, self.pad - self.nodes), F32)], axis=1)
        return jnp.concatenate([x, jnp.zeros((self.pad - self.nodes, self.pad), F32)], axis=0)


def read_field(z, ref, lead, offset):
    parts = [ref[lead + (pl.ds(offset + j, z.pad, stride=z.rows), slice(None))] for j in range(z.rows)]
    return z.rows_masked(jnp.concatenate(parts, axis=1))


def read_exact(z, ref, lead, offset):
    parts = [ref[lead + (pl.ds(offset + j, z.nodes, stride=z.rows), slice(None))] for j in range(z.rows)]
    return jnp.concatenate(parts, axis=1)


def write_field(z, ref, lead, offset, value):
    for j in range(z.rows):
        rows = pl.ds(offset + j, z.nodes, stride=z.rows)
        ref[lead + (rows, slice(None))] = value[: z.nodes, j * z.ax : (j + 1) * z.ax]


def read_matrix(z, ref, k):
    return z.square(ref[:, k, :])


def sensor_call(z, state, to_modal, after, low, high):
    first, size = z.window(low, high)
    count = high - low

    def kernel(state_ref, modal_ref, *refs):
        sensor_ref, head_ref, tail_ref, buf, sem = refs[len(after) :]
        copies = [
            pltpu.make_async_copy(state_ref.at[e, pl.ds(first, size)], buf.at[e, pl.ds(0, size)], sem.at[e])
            for e in range(z.segments)
        ]
        for copy in copies:
            copy.start()
        matrix = operand_left(z.square(modal_ref[...]))
        for e in range(z.segments):
            copies[e].wait()
            for i in range(low, high):
                field = read_field(z, buf, (e,), i * z.height - first)
                modal = product(matrix, operand_right(field))
                squares = modal * modal
                lower = jnp.sum(squares[: ORDER**3], axis=0, keepdims=True)
                upper = jnp.sum(squares[ORDER**3 :], axis=0, keepdims=True)
                sensor = (upper / z.nodes) / ((lower + upper) / z.nodes + 1e-6)
                sensor_ref[i - low, e : e + 1, :] = sensor
                head_ref[i - low, e : e + 1, :] = sensor[:, : z.ax]
                tail_ref[i - low, e : e + 1, :] = sensor[:, z.cols - z.ax :]

    outs = [f32(count, z.segments, z.cols), f32(count, z.segments, z.ax), f32(count, z.segments, z.ax)]
    return call(
        kernel,
        f"sensor_{low}",
        outs,
        [spec_any(), spec_vmem()] + [spec_any()] * len(after),
        [spec_vmem()] * 3,
        [pltpu.VMEM((z.segments, size + z.spill, z.ax), F32), pltpu.SemaphoreType.DMA((z.segments,))],
        z.flops * count * z.segments,
        4 * z.segments * size * z.ax,
    )(state, to_modal, *after)


def smoothed(z, sensor, before, after, left, right):
    inner = sensor[:, : z.cols - z.ax]
    outer = sensor[:, z.ax :]
    from_left = jnp.concatenate([left, inner], axis=1)
    from_right = jnp.concatenate([outer, right], axis=1)
    return (4.0 * sensor + before + after + from_left + from_right) / 8.0


def sweep_call(z, chunk, whole, me, state, rhs, viscous, gain, inverse, sensors, lefts, rights, ring, carry, after):
    low, high = chunk
    with_first = high == z.steps
    first, size = z.window(low, high)
    count = high - low
    first0, size0 = z.window(0, 1)
    arrays = []

    def place(array):
        for n, known in enumerate(arrays):
            if known is array:
                return n
        arrays.append(array)
        return len(arrays) - 1

    steps = list(range(low, high)) + ([0] if with_first else [])
    plan = []
    for i in steps:
        beside = []
        for k in (i, (i - 1) % z.steps, (i + 1) % z.steps):
            beside.append((place(sensors[k][0]), sensors[k][1]))
        for side in (lefts, rights):
            beside.append((place(side[i][0]), side[i][1]))
        plan.append(beside)
    ring_places = [place(array) for array in ring] if with_first else []
    small = len(arrays)
    has_carry = carry is not None
    needs_gain = has_carry or count > 1
    sent = 1 if whole else z.segments
    message = z.message(count)

    def kernel(*refs):
        me_ref, state_ref, rhs_ref, viscous_ref, inverse_ref = refs[:5]
        refs = refs[5:]
        if needs_gain:
            gain_ref, refs = refs[0], refs[1:]
        small_refs, refs = refs[:small], refs[small:]
        if has_carry:
            carry_ref, refs = refs[0], refs[1:]
        refs = refs[len(after) :]
        out_refs, refs = refs[:sent], refs[sent:]
        end_ref, refs = refs[0], refs[1:]
        if with_first:
            start_ref, refs = refs[0], refs[1:]
        state_buf, rhs_buf, smooth_buf, stage, sem, out_sem = refs[:6]
        if with_first:
            state0, rhs0 = refs[6:]
        mine = me_ref[0]
        batch = 4 if z.segments % 4 == 0 else 1
        places = [e if whole else lax.rem(mine + e, z.segments) for e in range(z.segments)]
        copies = []
        for s, e in enumerate(places):
            moves = [
                (state_ref.at[e, pl.ds(first, size)], state_buf.at[s, pl.ds(0, size)]),
                (rhs_ref.at[e, pl.ds(first, size)], rhs_buf.at[s, pl.ds(0, size)]),
            ]
            if with_first:
                moves.append((state_ref.at[e, pl.ds(first0, size0)], state0.at[s, pl.ds(0, size0)]))
                moves.append((rhs_ref.at[e, pl.ds(first0, size0)], rhs0.at[s, pl.ds(0, size0)]))
            started = []
            for n, (source, target) in enumerate(moves):
                copy = pltpu.make_async_copy(source, target, sem.at[s, n])
                copy.start()
                started.append(copy)
            copies.append(started)
        for n, i in enumerate(steps):
            (a0, p0), (a1, p1), (a2, p2), (al, pL), (ar, pR) = plan[n]
            here = small_refs[a0][p0]
            before = small_refs[a1][p1]
            later = small_refs[a2][p2]
            if i == 0:
                before = jnp.concatenate([small_refs[ring_places[0]][...], before[: z.segments - 1]], axis=0)
            if i == z.steps - 1:
                later = jnp.concatenate([later[1:], small_refs[ring_places[1]][...]], axis=0)
            smooth_buf[n] = smoothed(z, here, before, later, small_refs[al][pL], small_refs[ar][pR])
        operator = operand_left(z.square(viscous_ref[...]))

        def source(field, force, matrix, smooth):
            force = force + smooth * product(operator, operand_right(field))
            return product(operand_left(matrix), operand_right(force))

        sends = []
        for s0 in range(0, z.segments, batch):
            group = range(s0, s0 + batch)
            for s in group:
                for copy in copies[s]:
                    copy.wait()
            fields = [carry_ref[places[s]] if has_carry else None for s in group]
            for n in range(count):
                offset = (low + n) * z.height - first
                for g, s in enumerate(group):
                    k = places[s] * z.steps + low + n
                    smooth = smooth_buf[n, pl.ds(places[s], 1), :]
                    value = source(
                        read_field(z, state_buf, (s,), offset),
                        read_field(z, rhs_buf, (s,), offset),
                        read_matrix(z, inverse_ref, k),
                        smooth,
                    )
                    if fields[g] is not None:
                        value = value + product(
                            operand_left(read_matrix(z, gain_ref, k)), operand_right(fields[g])
                        )
                    fields[g] = value
                    write_field(z, stage, (s,), n * z.height, value)
            for g, s in enumerate(group):
                target = out_refs[0].at[s] if whole else out_refs[s]
                copy = pltpu.make_async_copy(stage.at[s], target, out_sem.at[s])
                copy.start()
                sends.append(copy)
                end_ref[places[s]] = fields[g]
                if with_first:
                    smooth = smooth_buf[count, pl.ds(places[s], 1), :]
                    start_ref[places[s]] = source(
                        read_field(z, state0, (s,), -first0),
                        read_field(z, rhs0, (s,), -first0),
                        read_matrix(z, inverse_ref, places[s] * z.steps),
                        smooth,
                    )
        for copy in sends:
            copy.wait()

    field = f32(z.segments, z.pad, z.cols)
    outs = [f32(z.segments, message, z.ax)] if whole else [f32(message, z.ax) for _ in range(z.segments)]
    outs += [field] * (2 if with_first else 1)
    operands = [me, state, rhs, viscous, inverse] + ([gain] if needs_gain else [])
    in_specs = [spec_smem(), spec_any(), spec_any()] + [spec_vmem()] * (len(operands) - 3)
    operands += arrays + ([carry] if has_carry else []) + after
    in_specs += [spec_vmem()] * (small + (1 if has_carry else 0)) + [spec_any()] * len(after)
    out_specs = [spec_any()] * sent + [spec_vmem()] * (2 if with_first else 1)
    scratch = [
        pltpu.VMEM((z.segments, size + z.spill, z.ax), F32),
        pltpu.VMEM((z.segments, size + z.spill, z.ax), F32),
        pltpu.VMEM((len(steps), z.segments, z.cols), F32),
        pltpu.VMEM((z.segments, message, z.ax), F32),
        pltpu.SemaphoreType.DMA((z.segments, 4)),
        pltpu.SemaphoreType.DMA((z.segments,)),
    ]
    if with_first:
        scratch += [pltpu.VMEM((z.segments, size0 + z.spill, z.ax), F32)] * 2
    result = call(
        kernel,
        f"sweep_{low}",
        outs,
        in_specs,
        out_specs,
        scratch,
        z.flops * len(steps) * z.segments * 3,
        4 * z.segments * size * z.ax * 4,
    )(*operands)
    return result[:sent], result[sent:]


def maps_call(z, me, gain, after):
    def kernel(me_ref, gain_ref, *refs):
        own_ref, tail_ref, whole_ref, prefix_ref, group_ref = refs[len(after) :]
        mine = me_ref[0]

        def times(a, b):
            return product(operand_left(a), operand_right(b))

        own_ref[0] = read_matrix(z, gain_ref, mine * z.steps)
        values = [read_matrix(z, gain_ref, e * z.steps + 1) for e in range(z.segments)]
        for i in range(1, z.steps):
            for e in range(z.segments):
                if i > 1:
                    values[e] = times(read_matrix(z, gain_ref, e * z.steps + i), values[e])

                @pl.when(e == mine)
                def _(i=i, value=values[e]):
                    own_ref[i] = value

        for e in range(z.segments):
            tail_ref[e] = values[e]
            whole_ref[e] = times(values[e], read_matrix(z, gain_ref, e * z.steps))
        value = whole_ref[0]
        prefix_ref[0] = value
        for e in range(1, z.segments):
            prefix_ref[e] = value
            value = times(whole_ref[e], value)
        group_ref[...] = value

    square = (z.pad, z.pad)
    outs = [f32(z.steps, *square)] + [f32(z.segments, *square)] * 3 + [f32(*square)]
    return call(
        kernel,
        "maps",
        outs,
        [spec_smem(), spec_vmem()] + [spec_any()] * len(after),
        [spec_vmem()] * 5,
        [],
        z.flops * z.segments * (z.steps + 1) // 2,
        4 * z.segments * z.steps * z.pad * z.pad,
    )(me, gain, *after)


def chain_call(z, starts, ends, tails, wholes, group):
    def kernel(start_ref, end_ref, tail_ref, whole_ref, group_ref, before_ref, pack_ref):
        value = None
        for e in range(z.segments):
            shift = end_ref[e] + product(operand_left(tail_ref[e]), operand_right(start_ref[e]))
            if e > 0:
                before_ref[e] = value
                shift = shift + product(operand_left(whole_ref[e]), operand_right(value))
            else:
                before_ref[0] = jnp.zeros_like(shift)
            value = shift
        pack_ref[:, : z.cols] = value
        pack_ref[:, z.cols :] = group_ref[...]

    return call(
        kernel,
        "chain",
        [f32(z.segments, z.pad, z.cols), f32(z.pad, z.cols + z.pad)],
        [spec_vmem()] * 5,
        [spec_vmem()] * 2,
        [],
        z.flops * z.segments * 2,
        4 * z.segments * z.pad * z.cols * 4,
    )(starts, ends, tails, wholes, group)


def first_call(z, places, packs, before, prefix, gain, starts, held):
    message = z.message(1)

    def kernel(*refs):
        places_ref, refs = refs[0], refs[1:]
        pack_refs, refs = refs[: z.groups], refs[z.groups :]
        before_ref, prefix_ref, gain_ref, start_ref, _ = refs[:5]
        out_refs = refs[5 : 5 + z.segments]
        mine = places_ref[0]
        group = places_ref[1]
        value = jnp.zeros((z.pad, z.cols), F32)
        matrices = [operand_left(ref[:, z.cols :]) for ref in pack_refs]
        for t in range(2 * z.groups - 1, 0, -1):
            n = t % z.groups
            moved = product(matrices[n], operand_right(value)) + pack_refs[n][:, : z.cols]
            value = jnp.where(t <= z.groups + group, moved, 0.0)
        incoming = operand_right(value)
        for s in range(z.segments):
            e = lax.rem(mine + s, z.segments)
            arriving = jnp.where(e == 0, value, before_ref[e] + product(operand_left(prefix_ref[e]), incoming))
            matrix = operand_left(read_matrix(z, gain_ref, e * z.steps))
            solved = start_ref[e] + product(matrix, operand_right(arriving))
            write_field(z, out_refs[s], (), 0, solved)

    result = call(
        kernel,
        "first",
        [f32(message, z.ax) for _ in range(z.segments)] + [jax.ShapeDtypeStruct(held.shape, F32)],
        [spec_smem()] + [spec_vmem()] * (z.groups + 4) + [spec_any()],
        [spec_vmem()] * z.segments + [spec_any()],
        [],
        z.flops * (z.segments * 2 + 2 * z.groups),
        4 * z.segments * z.pad * z.cols * 4,
        {z.groups + 5: z.segments},
    )(places, *packs, before, prefix, gain, starts, held)
    return result[: z.segments], result[z.segments]


def finish_call(z, chunk, me, own, firsts, messages, out):
    low, high = chunk
    count = high - low
    radial = z.segments * z.rows
    tall = z.nodes * radial
    only_first = messages is None
    has_out = out is not None
    whole = not only_first and len(messages) == 1
    sent = 0 if only_first else len(messages)

    def kernel(*refs):
        me_ref, own_ref, refs = refs[0], refs[1], refs[2:]
        first_refs, refs = refs[: z.segments], refs[z.segments :]
        message_refs, refs = refs[:sent], refs[sent:]
        if has_out:
            refs = refs[1:]
        out_ref, stage, sem = refs
        mine = me_ref[0]
        matrices = None if only_first else [operand_left(own_ref[i]) for i in range(low, high)]
        for s in range(z.segments):
            src = lax.rem(mine - s + z.segments, z.segments)
            field = read_exact(z, first_refs[s], (), 0)
            if not only_first:
                empty = jnp.zeros((z.pad - z.nodes, z.cols), F32)
                parts = operand_right(jnp.concatenate([field, empty], axis=0))
            for n in range(count):
                if only_first:
                    value = field
                else:
                    ref, lead = (message_refs[0], (src,)) if whole else (message_refs[s], ())
                    value = product(matrices[n], parts)[: z.nodes] + read_exact(z, ref, lead, n * z.height)
                for j in range(z.rows):
                    rows = pl.ds(src * z.rows + j, z.nodes, stride=radial)
                    stage[n, rows, :] = value[:, j * z.ax : (j + 1) * z.ax]
        copies = []
        for n in range(count):
            copy = pltpu.make_async_copy(stage.at[n], out_ref.at[low + n], sem.at[n])
            copy.start()
            copies.append(copy)
        for copy in copies:
            copy.wait()

    operands = [me, own] + list(firsts) + ([] if only_first else list(messages))
    in_specs = [spec_smem()] + [spec_vmem()] * (len(operands) - 1)
    aliases = {}
    if has_out:
        aliases = {len(operands): 0}
        operands.append(out)
        in_specs.append(spec_any())
    return call(
        kernel,
        f"finish_{low}",
        f32(z.steps, tall, z.ax),
        in_specs,
        spec_any(),
        [pltpu.VMEM((count, tall, z.ax), F32), pltpu.SemaphoreType.DMA((count,))],
        z.flops * count * z.segments,
        4 * 2 * count * tall * z.ax,
        aliases,
    )(*operands)


def shift_by(array, axis, by):
    size = lax.axis_size(axis)
    return lax.ppermute(array, axis, [(i, (i + by) % size) for i in range(size)])


def neighbours(head, tail):
    size = lax.axis_size("elem")
    left = lax.ppermute(tail, "elem", [(i, i + 1) for i in range(size - 1)])
    right = lax.ppermute(head, "elem", [(i + 1, i) for i in range(size - 1)])
    return left, right


def exchange(z, messages):
    if len(messages) == 1:
        return [lax.all_to_all(messages[0], "elem", 0, 0, tiled=True)]
    order = sorted(range(1, z.segments), key=lambda s: abs(s - z.segments // 2))
    moved = {0: messages[0]}
    for s in order:
        moved[s] = shift_by(messages[s], "elem", s)
    return [moved[s] for s in range(z.segments)]


def chunks_of(steps):
    if steps >= 8:
        return [(1, 2), (2, 5), (5, steps)]
    return [(1, 2), (2, 3), (3, steps)]


def body(state, rhs, to_modal, viscous_op, sweep_gain, inv_blocks):
    segments = lax.axis_size("elem")
    groups = lax.axis_size("blk")
    z = Sizes(state, segments, groups)
    state = state.reshape(segments, z.steps * z.height, z.ax)
    rhs = rhs.reshape(segments, z.steps * z.height, z.ax)
    gain = jnp.transpose(sweep_gain, (1, 0, 2))
    inverse = jnp.transpose(inv_blocks, (1, 0, 2))
    here = lax.axis_index("elem").astype(jnp.int32)
    me = here.reshape(1)
    places = jnp.stack([here, lax.axis_index("blk").astype(jnp.int32)])
    sensors, lefts, rights = {}, {}, {}

    def sense(low, high, after):
        sensor, head, tail = sensor_call(z, state, to_modal, after, low, high)
        left, right = neighbours(head, tail)
        for i in range(low, high):
            sensors[i], lefts[i], rights[i] = (sensor, i - low), (left, i - low), (right, i - low)

    def sweep(chunk, whole, ring, carry, after):
        return sweep_call(
            z, chunk, whole, me, state, rhs, viscous_op, gain, inverse, sensors, lefts, rights, ring, carry, after
        )

    one, two, three = chunks_of(z.steps)
    sense(0, 3, [])
    messages_one, (carry,) = sweep(one, False, None, None, [])
    sense(3, z.steps, [carry])
    last, place = sensors[z.steps - 1]
    ring = [
        shift_by(last[place, segments - 1 :], "blk", 1),
        shift_by(sensors[0][0][0, :1], "blk", -1),
    ]
    messages_two, (carry,) = sweep(two, True, None, carry, [])
    received_one = exchange(z, messages_one)
    own, tails, wholes, prefix, group = maps_call(z, me, gain, [carry])
    messages_three, (carry, starts) = sweep(three, True, ring, carry, received_one[1:])
    before, pack = chain_call(z, starts, carry, tails, wholes, group)
    packs = [pack] + [shift_by(pack, "blk", s) for s in range(1, groups)]
    firsts, held = first_call(z, places, packs, before, prefix, gain, starts, messages_three[0])
    received_two = exchange(z, messages_two)
    firsts = exchange(z, firsts)
    received_three = exchange(z, [held])
    out = finish_call(z, (0, 1), me, own, firsts, None, None)
    for chunk, messages in ((one, received_one), (two, received_two), (three, received_three)):
        out = finish_call(z, chunk, me, own, firsts, messages, out)
    return out.reshape(z.steps, z.nodes, segments * z.rows, z.ax)


def solution(mesh):
    in_specs = (
        P("blk", None, "elem", None),
        P("blk", None, "elem", None),
        P(),
        P(),
        P("blk", None, None),
        P("blk", None, None),
    )
    out_specs = P(("blk", "elem"), None, None, None)
    return jax.shard_map(body, mesh=mesh, in_specs=in_specs, out_specs=out_specs, check_vma=False)
```

```python
import functools

import jax
import jax.numpy as jnp
from jax import lax
from jax.experimental import pallas as pl
from jax.experimental.pallas import tpu as pltpu
from jax.sharding import PartitionSpec as P

ORDER = 4
F32 = jnp.float32
BF16 = jnp.bfloat16
MIB = 1024 * 1024
TILE = 8
LANES = 128


def operand_left(a):
    high = a.astype(BF16)
    low = (a - high.astype(F32)).astype(BF16)
    return jnp.concatenate([jnp.concatenate([high, high], axis=1), jnp.concatenate([low, low], axis=1)], axis=0)


def operand_right(x):
    high = x.astype(BF16)
    return jnp.concatenate([high, (x - high.astype(F32)).astype(BF16)], axis=0)


def product(left, right):
    both = jnp.dot(left, right, preferred_element_type=F32)
    half = left.shape[0] // 2
    return both[:half] + both[half:]


def spec_any():
    return pl.BlockSpec(memory_space=pl.ANY)


def spec_hbm():
    return pl.BlockSpec(memory_space=pltpu.HBM)


def spec_vmem():
    return pl.BlockSpec(memory_space=pltpu.VMEM)


def spec_smem():
    return pl.BlockSpec(memory_space=pltpu.SMEM)


def call(kernel, name, outs, in_specs, out_specs, scratch, flops, nbytes, aliases=None, limit=24):
    return pl.pallas_call(
        kernel,
        name=name,
        out_shape=outs,
        in_specs=in_specs,
        out_specs=out_specs,
        scratch_shapes=scratch,
        input_output_aliases=aliases or {},
        compiler_params=pltpu.CompilerParams(vmem_limit_bytes=limit * MIB),
        cost_estimate=pl.CostEstimate(flops=int(flops), bytes_accessed=int(nbytes), transcendentals=0),
    )


def f32(*shape):
    return jax.ShapeDtypeStruct(shape, F32)


def up(value, unit):
    return -(-value // unit) * unit


class Sizes:
    def __init__(self, state, segments, groups):
        count, self.nodes, self.rows, self.ax = state.shape
        self.count = count
        self.segments = segments
        self.groups = groups
        self.steps = count // segments
        self.cols = self.rows * self.ax
        self.height = self.nodes * self.rows
        self.pad = up(self.nodes, LANES)
        self.spill = up((self.pad - self.nodes) * self.rows, TILE)
        self.flops = 2 * 4 * self.pad * self.pad * self.cols

    def window(self, low, high):
        first = low * self.height // TILE * TILE
        return first, up(high * self.height, TILE) - first

    def message(self, count):
        return up(count * self.height, TILE)

    def rows_masked(self, x):
        cut = self.nodes // TILE * TILE
        rest = x[cut:]
        inside = lax.broadcasted_iota(jnp.int32, rest.shape, 0) < self.nodes - cut
        return jnp.concatenate([x[:cut], jnp.where(inside, rest, 0.0)], axis=0)

    def square(self, x):
        x = jnp.concatenate([x, jnp.zeros((self.nodes, self.pad - self.nodes), F32)], axis=1)
        return jnp.concatenate([x, jnp.zeros((self.pad - self.nodes, self.pad), F32)], axis=0)


def read_field(z, ref, lead, offset):
    parts = [ref[lead + (pl.ds(offset + j, z.pad, stride=z.rows), slice(None))] for j in range(z.rows)]
    return z.rows_masked(jnp.concatenate(parts, axis=1))


def read_exact(z, ref, lead, offset):
    parts = [ref[lead + (pl.ds(offset + j, z.nodes, stride=z.rows), slice(None))] for j in range(z.rows)]
    return jnp.concatenate(parts, axis=1)


def write_field(z, ref, lead, offset, value):
    for j in range(z.rows):
        rows = pl.ds(offset + j, z.nodes, stride=z.rows)
        ref[lead + (rows, slice(None))] = value[: z.nodes, j * z.ax : (j + 1) * z.ax]


def read_matrix(z, ref, k):
    return z.square(ref[:, k, :])


def sensor_call(z, state, to_modal, after, low, high):
    first, size = z.window(low, high)
    count = high - low

    def kernel(state_ref, modal_ref, *refs):
        sensor_ref, head_ref, tail_ref, buf, sem = refs[len(after) :]
        copies = [
            pltpu.make_async_copy(state_ref.at[e, pl.ds(first, size)], buf.at[e, pl.ds(0, size)], sem.at[e])
            for e in range(z.segments)
        ]
        for copy in copies:
            copy.start()
        matrix = operand_left(z.square(modal_ref[...]))
        for e in range(z.segments):
            copies[e].wait()
            for i in range(low, high):
                field = read_field(z, buf, (e,), i * z.height - first)
                modal = product(matrix, operand_right(field))
                squares = modal * modal
                lower = jnp.sum(squares[: ORDER**3], axis=0, keepdims=True)
                upper = jnp.sum(squares[ORDER**3 :], axis=0, keepdims=True)
                sensor = (upper / z.nodes) / ((lower + upper) / z.nodes + 1e-6)
                sensor_ref[i - low, e : e + 1, :] = sensor
                head_ref[i - low, e : e + 1, :] = sensor[:, : z.ax]
                tail_ref[i - low, e : e + 1, :] = sensor[:, z.cols - z.ax :]

    outs = [f32(count, z.segments, z.cols), f32(count, z.segments, z.ax), f32(count, z.segments, z.ax)]
    return call(
        kernel,
        f"sensor_{low}",
        outs,
        [spec_hbm(), spec_vmem()] + [spec_any()] * len(after),
        [spec_vmem()] * 3,
        [pltpu.VMEM((z.segments, size + z.spill, z.ax), F32), pltpu.SemaphoreType.DMA((z.segments,))],
        z.flops * count * z.segments,
        4 * z.segments * size * z.ax,
        limit=56,
    )(state, to_modal, *after)


def smoothed(z, sensor, before, after, left, right):
    inner = sensor[:, : z.cols - z.ax]
    outer = sensor[:, z.ax :]
    from_left = jnp.concatenate([left, inner], axis=1)
    from_right = jnp.concatenate([outer, right], axis=1)
    return (4.0 * sensor + before + after + from_left + from_right) / 8.0


def sweep_call(z, chunk, state, rhs, viscous, gain, inverse, sensors, lefts, rights, ring, carry, after):
    low, high = chunk
    with_first = high == z.steps
    first, size = z.window(low, high)
    count = high - low
    first0, size0 = z.window(0, 1)
    arrays = []

    def place(array):
        for n, known in enumerate(arrays):
            if known is array:
                return n
        arrays.append(array)
        return len(arrays) - 1

    steps = list(range(low, high)) + ([0] if with_first else [])
    plan = []
    for i in steps:
        beside = []
        for k in (i, (i - 1) % z.steps, (i + 1) % z.steps):
            beside.append((place(sensors[k][0]), sensors[k][1]))
        for side in (lefts, rights):
            beside.append((place(side[i][0]), side[i][1]))
        plan.append(beside)
    ring_places = [place(array) for array in ring] if with_first else []
    small = len(arrays)
    has_carry = carry is not None
    needs_gain = has_carry or count > 1
    message = z.message(count)

    def kernel(*refs):
        state_ref, rhs_ref, viscous_ref, inverse_ref = refs[:4]
        refs = refs[4:]
        if needs_gain:
            gain_ref, refs = refs[0], refs[1:]
        small_refs, refs = refs[:small], refs[small:]
        if has_carry:
            carry_ref, refs = refs[0], refs[1:]
        refs = refs[len(after) :]
        out_ref, refs = refs[0], refs[1:]
        end_ref, refs = refs[0], refs[1:]
        if with_first:
            start_ref, refs = refs[0], refs[1:]
        state_buf, rhs_buf, smooth_buf, stage, sem, out_sem = refs[:6]
        if with_first:
            state0, rhs0 = refs[6:]
        batch = 4 if z.segments % 4 == 0 else 1
        copies = []
        for s in range(z.segments):
            moves = [
                (state_ref.at[s, pl.ds(first, size)], state_buf.at[s, pl.ds(0, size)]),
                (rhs_ref.at[s, pl.ds(first, size)], rhs_buf.at[s, pl.ds(0, size)]),
            ]
            if with_first:
                moves.append((state_ref.at[s, pl.ds(first0, size0)], state0.at[s, pl.ds(0, size0)]))
                moves.append((rhs_ref.at[s, pl.ds(first0, size0)], rhs0.at[s, pl.ds(0, size0)]))
            started = []
            for n, (source, target) in enumerate(moves):
                copy = pltpu.make_async_copy(source, target, sem.at[s, n])
                copy.start()
                started.append(copy)
            copies.append(started)
        for n, i in enumerate(steps):
            (a0, p0), (a1, p1), (a2, p2), (al, pL), (ar, pR) = plan[n]
            here = small_refs[a0][p0]
            before = small_refs[a1][p1]
            later = small_refs[a2][p2]
            if i == 0:
                before = jnp.concatenate([small_refs[ring_places[0]][...], before[: z.segments - 1]], axis=0)
            if i == z.steps - 1:
                later = jnp.concatenate([later[1:], small_refs[ring_places[1]][...]], axis=0)
            smooth_buf[n] = smoothed(z, here, before, later, small_refs[al][pL], small_refs[ar][pR])
        operator = operand_left(z.square(viscous_ref[...]))

        def source(field, force, matrix, smooth):
            force = force + smooth * product(operator, operand_right(field))
            return product(operand_left(matrix), operand_right(force))

        sends = []
        for s0 in range(0, z.segments, batch):
            group = range(s0, s0 + batch)
            for s in group:
                for copy in copies[s]:
                    copy.wait()
            fields = [carry_ref[s] if has_carry else None for s in group]
            for n in range(count):
                offset = (low + n) * z.height - first
                for g, s in enumerate(group):
                    k = s * z.steps + low + n
                    smooth = smooth_buf[n, s : s + 1, :]
                    value = source(
                        read_field(z, state_buf, (s,), offset),
                        read_field(z, rhs_buf, (s,), offset),
                        read_matrix(z, inverse_ref, k),
                        smooth,
                    )
                    if fields[g] is not None:
                        value = value + product(
                            operand_left(read_matrix(z, gain_ref, k)), operand_right(fields[g])
                        )
                    fields[g] = value
                    write_field(z, stage, (s,), n * z.height, value)
            for g, s in enumerate(group):
                copy = pltpu.make_async_copy(stage.at[s], out_ref.at[s], out_sem.at[s])
                copy.start()
                sends.append(copy)
                end_ref[s] = fields[g]
                if with_first:
                    smooth = smooth_buf[count, s : s + 1, :]
                    start_ref[s] = source(
                        read_field(z, state0, (s,), -first0),
                        read_field(z, rhs0, (s,), -first0),
                        read_matrix(z, inverse_ref, s * z.steps),
                        smooth,
                    )
        for copy in sends:
            copy.wait()

    field = f32(z.segments, z.pad, z.cols)
    outs = [f32(z.segments, message, z.ax)] + [field] * (2 if with_first else 1)
    operands = [state, rhs, viscous, inverse] + ([gain] if needs_gain else [])
    in_specs = [spec_hbm(), spec_hbm()] + [spec_vmem()] * (len(operands) - 2)
    operands += arrays + ([carry] if has_carry else []) + after
    in_specs += [spec_vmem()] * (small + (1 if has_carry else 0)) + [spec_any()] * len(after)
    out_specs = [spec_hbm()] + [spec_vmem()] * (2 if with_first else 1)
    scratch = [
        pltpu.VMEM((z.segments, size + z.spill, z.ax), F32),
        pltpu.VMEM((z.segments, size + z.spill, z.ax), F32),
        pltpu.VMEM((len(steps), z.segments, z.cols), F32),
        pltpu.VMEM((z.segments, message, z.ax), F32),
        pltpu.SemaphoreType.DMA((z.segments, 4)),
        pltpu.SemaphoreType.DMA((z.segments,)),
    ]
    if with_first:
        scratch += [pltpu.VMEM((z.segments, size0 + z.spill, z.ax), F32)] * 2
    result = call(
        kernel,
        f"sweep_{low}",
        outs,
        in_specs,
        out_specs,
        scratch,
        z.flops * len(steps) * z.segments * 3,
        4 * z.segments * size * z.ax * 4,
        limit=52,
    )(*operands)
    return result[0], result[1:]


def maps_call(z, me, gain, after):
    def kernel(me_ref, gain_ref, *refs):
        own_ref, tail_ref, whole_ref, prefix_ref, group_ref = refs[len(after) :]
        mine = me_ref[0]

        def times(a, b):
            return product(operand_left(a), operand_right(b))

        own_ref[0] = read_matrix(z, gain_ref, mine * z.steps)
        values = [read_matrix(z, gain_ref, e * z.steps + 1) for e in range(z.segments)]
        for i in range(1, z.steps):
            for e in range(z.segments):
                if i > 1:
                    values[e] = times(read_matrix(z, gain_ref, e * z.steps + i), values[e])

                @pl.when(e == mine)
                def _(i=i, value=values[e]):
                    own_ref[i] = value

        for e in range(z.segments):
            tail_ref[e] = values[e]
            whole_ref[e] = times(values[e], read_matrix(z, gain_ref, e * z.steps))
        value = whole_ref[0]
        prefix_ref[0] = value
        for e in range(1, z.segments):
            prefix_ref[e] = value
            value = times(whole_ref[e], value)
        group_ref[...] = value

    square = (z.pad, z.pad)
    outs = [f32(z.steps, *square)] + [f32(z.segments, *square)] * 3 + [f32(*square)]
    return call(
        kernel,
        "maps",
        outs,
        [spec_smem(), spec_vmem()] + [spec_any()] * len(after),
        [spec_vmem()] * 5,
        [],
        z.flops * z.segments * (z.steps + 1) // 2,
        4 * z.segments * z.steps * z.pad * z.pad,
    )(me, gain, *after)


def chain_call(z, starts, ends, tails, wholes, group):
    def kernel(start_ref, end_ref, tail_ref, whole_ref, group_ref, before_ref, pack_ref):
        value = None
        for e in range(z.segments):
            shift = end_ref[e] + product(operand_left(tail_ref[e]), operand_right(start_ref[e]))
            if e > 0:
                before_ref[e] = value
                shift = shift + product(operand_left(whole_ref[e]), operand_right(value))
            else:
                before_ref[0] = jnp.zeros_like(shift)
            value = shift
        pack_ref[:, : z.cols] = value
        pack_ref[:, z.cols :] = group_ref[...]

    return call(
        kernel,
        "chain",
        [f32(z.segments, z.pad, z.cols), f32(z.pad, z.cols + z.pad)],
        [spec_vmem()] * 5,
        [spec_vmem()] * 2,
        [],
        z.flops * z.segments * 2,
        4 * z.segments * z.pad * z.cols * 4,
    )(starts, ends, tails, wholes, group)


def first_call(z, places, packs, before, prefix, gain, starts, held):
    pairs = z.segments // 2
    message = z.message(1)

    def kernel(*refs):
        places_ref, refs = refs[0], refs[1:]
        pack_refs, refs = refs[: z.groups], refs[z.groups :]
        before_ref, prefix_ref, gain_ref, start_ref, _ = refs[:5]
        keep_ref, give_ref = refs[5:7]
        mine = places_ref[0]
        group = places_ref[1]
        value = jnp.zeros((z.pad, z.cols), F32)
        matrices = [operand_left(ref[:, z.cols :]) for ref in pack_refs]
        for t in range(2 * z.groups - 1, 0, -1):
            n = t % z.groups
            moved = product(matrices[n], operand_right(value)) + pack_refs[n][:, : z.cols]
            value = jnp.where(t <= z.groups + group, moved, 0.0)
        incoming = operand_right(value)
        side = lax.rem(mine, 2)
        for d in range(pairs):
            for ref, part in ((give_ref, 1 - side), (keep_ref, side)):
                e = lax.rem(mine - side + 2 * d, z.segments) + part
                arriving = jnp.where(e == 0, value, before_ref[e] + product(operand_left(prefix_ref[e]), incoming))
                matrix = operand_left(read_matrix(z, gain_ref, e * z.steps))
                solved = start_ref[e] + product(matrix, operand_right(arriving))
                write_field(z, ref, (d,), 0, solved)

    return call(
        kernel,
        "first",
        [f32(pairs, message, z.ax)] * 2 + [jax.ShapeDtypeStruct(held.shape, F32)],
        [spec_smem()] + [spec_vmem()] * (z.groups + 4) + [spec_hbm()],
        [spec_vmem()] * 2 + [spec_hbm()],
        [],
        z.flops * (z.segments * 2 + 2 * z.groups),
        4 * z.segments * z.pad * z.cols * 4,
        {z.groups + 5: 2},
    )(places, *packs, before, prefix, gain, starts, held)


def couple_call(z, keep, got):
    pairs = z.segments // 2
    message = z.message(1)

    def kernel(keep_ref, got_ref, *refs):
        for d in range(pairs):
            refs[d][0] = keep_ref[d]
            refs[d][1] = got_ref[d]

    return call(
        kernel,
        "couple",
        [f32(2, message, z.ax)] * pairs,
        [spec_vmem()] * 2,
        [spec_vmem()] * pairs,
        [],
        0,
        4 * 4 * pairs * message * z.ax,
    )(keep, got)


def open_call(z, me, firsts):
    radial = z.segments * z.rows
    tall = z.nodes * radial
    pairs = z.segments // 2

    def kernel(*refs):
        me_ref, refs = refs[0], refs[1:]
        first_refs, refs = refs[:pairs], refs[pairs:]
        out_ref, operand_ref, stage, sem = refs
        mine = me_ref[0]
        side = lax.rem(mine, 2)
        for d in range(pairs):
            for part in range(2):
                src = lax.rem(mine - side - 2 * d + z.segments, z.segments) + (side if part == 0 else 1 - side)
                field = read_exact(z, first_refs[d], (part,), 0)
                empty = jnp.zeros((z.pad - z.nodes, z.cols), F32)
                operand_ref[src] = operand_right(jnp.concatenate([field, empty], axis=0))
                for j in range(z.rows):
                    stage[pl.ds(src * z.rows + j, z.nodes, stride=radial), :] = field[:, j * z.ax : (j + 1) * z.ax]
        copy = pltpu.make_async_copy(stage, out_ref.at[0], sem)
        copy.start()
        copy.wait()

    return call(
        kernel,
        "finish_0",
        [f32(z.steps, tall, z.ax), jax.ShapeDtypeStruct((z.segments, 2 * z.pad, z.cols), BF16)],
        [spec_smem()] + [spec_vmem()] * pairs,
        [spec_hbm(), spec_vmem()],
        [pltpu.VMEM((tall, z.ax), F32), pltpu.SemaphoreType.DMA],
        0,
        4 * 2 * tall * z.ax,
    )(me, *firsts)


def finish_call(z, chunk, own, operands, messages, out):
    low, high = chunk
    count = high - low
    radial = z.segments * z.rows
    tall = z.nodes * radial
    message = z.message(count)

    def kernel(own_ref, operand_ref, message_ref, _, out_ref, buf, stage, sem, out_sem):
        copies = [pltpu.make_async_copy(message_ref.at[e], buf.at[e], sem.at[e]) for e in range(z.segments)]
        for copy in copies:
            copy.start()
        sends = []
        for n in range(count):
            matrix = operand_left(own_ref[low + n])
            for e in range(z.segments):
                if n == 0:
                    copies[e].wait()
                value = product(matrix, operand_ref[e])[: z.nodes] + read_exact(z, buf, (e,), n * z.height)
                for j in range(z.rows):
                    rows = pl.ds(e * z.rows + j, z.nodes, stride=radial)
                    stage[n, rows, :] = value[:, j * z.ax : (j + 1) * z.ax]
            copy = pltpu.make_async_copy(stage.at[n], out_ref.at[low + n], out_sem.at[n])
            copy.start()
            sends.append(copy)
        for copy in sends:
            copy.wait()

    return call(
        kernel,
        f"finish_{low}",
        f32(z.steps, tall, z.ax),
        [spec_vmem(), spec_vmem(), spec_hbm(), spec_hbm()],
        spec_hbm(),
        [
            pltpu.VMEM((z.segments, message, z.ax), F32),
            pltpu.VMEM((count, tall, z.ax), F32),
            pltpu.SemaphoreType.DMA((z.segments,)),
            pltpu.SemaphoreType.DMA((count,)),
        ],
        z.flops * count * z.segments,
        4 * 2 * count * tall * z.ax,
        {3: 0},
    )(own, operands, messages, out)


def shift_by(array, axis, by):
    size = lax.axis_size(axis)
    return lax.ppermute(array, axis, [(i, (i + by) % size) for i in range(size)])


def neighbours(head, tail):
    size = lax.axis_size("elem")
    left = lax.ppermute(tail, "elem", [(i, i + 1) for i in range(size - 1)])
    right = lax.ppermute(head, "elem", [(i + 1, i) for i in range(size - 1)])
    return left, right


def spread(messages):
    return lax.all_to_all(messages, "elem", 0, 0, tiled=True)


def chunks_of(steps):
    if steps >= 8:
        return [(1, 2), (2, 5), (5, steps)]
    return [(1, 2), (2, 3), (3, steps)]


def body(state, rhs, to_modal, viscous_op, sweep_gain, inv_blocks):
    segments = lax.axis_size("elem")
    groups = lax.axis_size("blk")
    z = Sizes(state, segments, groups)
    state = state.reshape(segments, z.steps * z.height, z.ax)
    rhs = rhs.reshape(segments, z.steps * z.height, z.ax)
    gain = jnp.transpose(sweep_gain, (1, 0, 2))
    inverse = jnp.transpose(inv_blocks, (1, 0, 2))
    here = lax.axis_index("elem").astype(jnp.int32)
    me = here.reshape(1)
    places = jnp.stack([here, lax.axis_index("blk").astype(jnp.int32)])
    sensors, lefts, rights = {}, {}, {}

    def sense(low, high, after):
        sensor, head, tail = sensor_call(z, state, to_modal, after, low, high)
        left, right = neighbours(head, tail)
        for i in range(low, high):
            sensors[i], lefts[i], rights[i] = (sensor, i - low), (left, i - low), (right, i - low)

    def sweep(chunk, ring, carry):
        return sweep_call(
            z, chunk, state, rhs, viscous_op, gain, inverse, sensors, lefts, rights, ring, carry, []
        )

    one, two, three = chunks_of(z.steps)
    sense(0, 3, [])
    messages_one, (carry,) = sweep(one, None, None)
    sense(3, z.steps, [carry])
    last, place = sensors[z.steps - 1]
    ring = [
        shift_by(last[place, segments - 1 :], "blk", 1),
        shift_by(sensors[0][0][0, :1], "blk", -1),
    ]
    messages_two, (carry,) = sweep(two, None, carry)
    own, tails, wholes, prefix, group = maps_call(z, me, gain, [carry])
    messages_three, (carry, starts) = sweep(three, ring, carry)
    before, pack = chain_call(z, starts, carry, tails, wholes, group)
    packs = [pack] + [shift_by(pack, "blk", s) for s in range(1, groups)]
    keep, give, held = first_call(z, places, packs, before, prefix, gain, starts, messages_three)
    got = lax.ppermute(give, "elem", [(i, i ^ 1) for i in range(segments)])
    firsts = couple_call(z, keep, got)
    firsts = [firsts[0]] + [shift_by(firsts[d], "elem", 2 * d) for d in range(1, segments // 2)]
    received_one = spread(messages_one)
    received_two = spread(messages_two)
    received_three = spread(held)
    out, operands = open_call(z, me, firsts)
    for chunk, messages in ((one, received_one), (two, received_two), (three, received_three)):
        out = finish_call(z, chunk, own, operands, messages, out)
    return out.reshape(z.steps, z.nodes, segments * z.rows, z.ax)


def solution(mesh):
    in_specs = (
        P("blk", None, "elem", None),
        P("blk", None, "elem", None),
        P(),
        P(),
        P("blk", None, None),
        P("blk", None, None),
    )
    out_specs = P(("blk", "elem"), None, None, None)
    return jax.shard_map(body, mesh=mesh, in_specs=in_specs, out_specs=out_specs, check_vma=False)
```

```python
import functools

import jax
import jax.numpy as jnp
from jax import lax
from jax.experimental import pallas as pl
from jax.experimental.pallas import tpu as pltpu
from jax.sharding import PartitionSpec as P

ORDER = 4
F32 = jnp.float32
BF16 = jnp.bfloat16
VMEM_LIMIT = 57 * 1024 * 1024
TILE = 8
LANES = 128


def operand_left(a):
    high = a.astype(BF16)
    low = (a - high.astype(F32)).astype(BF16)
    return jnp.concatenate([jnp.concatenate([high, high], axis=1), jnp.concatenate([low, low], axis=1)], axis=0)


def operand_right(x):
    high = x.astype(BF16)
    return jnp.concatenate([high, (x - high.astype(F32)).astype(BF16)], axis=0)


def product(left, right):
    both = jnp.dot(left, right, preferred_element_type=F32)
    half = left.shape[0] // 2
    return both[:half] + both[half:]


def spec_any():
    return pl.BlockSpec(memory_space=pl.ANY)


def spec_hbm():
    return pl.BlockSpec(memory_space=pltpu.HBM)


def spec_vmem():
    return pl.BlockSpec(memory_space=pltpu.VMEM)


def spec_smem():
    return pl.BlockSpec(memory_space=pltpu.SMEM)


def call(kernel, name, outs, in_specs, out_specs, scratch, flops, nbytes, aliases=None):
    return pl.pallas_call(
        kernel,
        name=name,
        out_shape=outs,
        in_specs=in_specs,
        out_specs=out_specs,
        scratch_shapes=scratch,
        input_output_aliases=aliases or {},
        compiler_params=pltpu.CompilerParams(vmem_limit_bytes=VMEM_LIMIT),
        cost_estimate=pl.CostEstimate(flops=int(flops), bytes_accessed=int(nbytes), transcendentals=0),
    )


def f32(*shape):
    return jax.ShapeDtypeStruct(shape, F32)


def up(value, unit):
    return -(-value // unit) * unit


class Sizes:
    def __init__(self, state, segments, groups):
        count, self.nodes, self.rows, self.ax = state.shape
        self.count = count
        self.segments = segments
        self.groups = groups
        self.steps = count // segments
        self.cols = self.rows * self.ax
        self.height = self.nodes * self.rows
        self.pad = up(self.nodes, LANES)
        self.spill = up((self.pad - self.nodes) * self.rows, TILE)
        self.flops = 2 * 4 * self.pad * self.pad * self.cols

    def window(self, low, high):
        first = low * self.height // TILE * TILE
        return first, up(high * self.height, TILE) - first

    def message(self, count):
        return up(count * self.height, TILE)

    def rows_masked(self, x):
        cut = self.nodes // TILE * TILE
        rest = x[cut:]
        inside = lax.broadcasted_iota(jnp.int32, rest.shape, 0) < self.nodes - cut
        return jnp.concatenate([x[:cut], jnp.where(inside, rest, 0.0)], axis=0)

    def square(self, x):
        x = jnp.concatenate([x, jnp.zeros((self.nodes, self.pad - self.nodes), F32)], axis=1)
        return jnp.concatenate([x, jnp.zeros((self.pad - self.nodes, self.pad), F32)], axis=0)


def read_field(z, ref, lead, offset):
    parts = [ref[lead + (pl.ds(offset + j, z.pad, stride=z.rows), slice(None))] for j in range(z.rows)]
    return z.rows_masked(jnp.concatenate(parts, axis=1))


def read_exact(z, ref, lead, offset):
    parts = [ref[lead + (pl.ds(offset + j, z.nodes, stride=z.rows), slice(None))] for j in range(z.rows)]
    return jnp.concatenate(parts, axis=1)


def write_field(z, ref, lead, offset, value):
    for j in range(z.rows):
        rows = pl.ds(offset + j, z.nodes, stride=z.rows)
        ref[lead + (rows, slice(None))] = value[: z.nodes, j * z.ax : (j + 1) * z.ax]


def read_matrix(z, ref, k):
    return z.square(ref[:, k, :])


def sensor_call(z, state, to_modal, after, earlier, low, high):
    first, size = z.window(low, high)
    count = high - low
    before = sum(array.shape[0] for array in earlier)

    def kernel(state_ref, modal_ref, *refs):
        earlier_refs, refs = refs[: len(earlier)], refs[len(earlier) :]
        sensor_ref, head_ref, tail_ref, buf, sem = refs[len(after) :]
        copies = [
            pltpu.make_async_copy(state_ref.at[e, pl.ds(first, size)], buf.at[e, pl.ds(0, size)], sem.at[e])
            for e in range(z.segments)
        ]
        for copy in copies:
            copy.start()
        place = 0
        for ref in earlier_refs:
            for n in range(ref.shape[0]):
                head_ref[place] = ref[n, :, : z.ax]
                tail_ref[place] = ref[n, :, z.cols - z.ax :]
                place += 1
        matrix = operand_left(z.square(modal_ref[...]))
        for e in range(z.segments):
            copies[e].wait()
            for i in range(low, high):
                field = read_field(z, buf, (e,), i * z.height - first)
                modal = product(matrix, operand_right(field))
                squares = modal * modal
                lower = jnp.sum(squares[: ORDER**3], axis=0, keepdims=True)
                upper = jnp.sum(squares[ORDER**3 :], axis=0, keepdims=True)
                sensor = (upper / z.nodes) / ((lower + upper) / z.nodes + 1e-6)
                n = i - low
                sensor_ref[n, e : e + 1, :] = sensor
                head_ref[before + n, e : e + 1, :] = sensor[:, : z.ax]
                tail_ref[before + n, e : e + 1, :] = sensor[:, z.cols - z.ax :]

    outs = [f32(count, z.segments, z.cols)] + [f32(before + count, z.segments, z.ax)] * 2
    return call(
        kernel,
        f"sensor_{low}",
        outs,
        [spec_hbm()] + [spec_vmem()] * (1 + len(earlier)) + [spec_any()] * len(after),
        [spec_vmem()] * 3,
        [pltpu.VMEM((z.segments, size + z.spill, z.ax), F32), pltpu.SemaphoreType.DMA((z.segments,))],
        z.flops * count * z.segments,
        4 * z.segments * size * z.ax,
    )(state, to_modal, *earlier, *after)


def smoothed(z, sensor, before, after, left, right):
    inner = sensor[:, : z.cols - z.ax]
    outer = sensor[:, z.ax :]
    from_left = jnp.concatenate([left, inner], axis=1)
    from_right = jnp.concatenate([outer, right], axis=1)
    return (4.0 * sensor + before + after + from_left + from_right) / 8.0


def sweep_call(z, chunk, state, rhs, viscous, gain, inverse, sensors, lefts, rights, ring, carry, held):
    low, high = chunk
    with_first = high == z.steps
    first, size = z.window(low, high)
    count = high - low
    first0, size0 = z.window(0, 1)
    arrays = []

    def place(array):
        for n, known in enumerate(arrays):
            if known is array:
                return n
        arrays.append(array)
        return len(arrays) - 1

    steps = list(range(low, high)) + ([0] if with_first else [])
    plan = []
    for i in steps:
        beside = []
        for k in (i, (i - 1) % z.steps, (i + 1) % z.steps):
            beside.append((place(sensors[k][0]), sensors[k][1]))
        for side in (lefts, rights):
            beside.append((place(side[i][0]), side[i][1]))
        plan.append(beside)
    ring_places = [place(array) for array in ring] if with_first else []
    small = len(arrays)
    has_carry = carry is not None
    needs_gain = has_carry or count > 1
    message = z.message(count)

    def kernel(*refs):
        state_ref, rhs_ref, viscous_ref, inverse_ref = refs[:4]
        refs = refs[4:]
        if needs_gain:
            gain_ref, refs = refs[0], refs[1:]
        small_refs, refs = refs[:small], refs[small:]
        if has_carry:
            carry_ref, refs = refs[0], refs[1:]
        if held is not None:
            refs = refs[1:]
        out_ref, refs = refs[0], refs[1:]
        end_ref, refs = refs[0], refs[1:]
        if with_first:
            start_ref, refs = refs[0], refs[1:]
        if held is not None:
            refs = refs[1:]
        state_buf, rhs_buf, inverse_buf, gain_buf, smooth_buf, stage, sem, matrix_sem, out_sem = refs[:9]
        if with_first:
            state0, rhs0 = refs[9:]
        batch = next(n for n in (4, 8, z.segments) if z.segments % n == 0 and n * z.steps % TILE == 0)
        copies = []
        for s in range(z.segments):
            if s % batch == 0:
                part = pl.ds(s * z.steps, batch * z.steps)
                sources = [(inverse_ref, inverse_buf)] + ([(gain_ref, gain_buf)] if needs_gain else [])
                pieces = []
                for n, (source, target) in enumerate(sources):
                    copy = pltpu.make_async_copy(source.at[:, part], target.at[:, part], matrix_sem.at[s, n])
                    copy.start()
                    pieces.append(copy)
                copies.append(pieces)
            else:
                copies.append([])
            moves = [
                (state_ref.at[s, pl.ds(first, size)], state_buf.at[s, pl.ds(0, size)]),
                (rhs_ref.at[s, pl.ds(first, size)], rhs_buf.at[s, pl.ds(0, size)]),
            ]
            if with_first:
                moves.append((state_ref.at[s, pl.ds(first0, size0)], state0.at[s, pl.ds(0, size0)]))
                moves.append((rhs_ref.at[s, pl.ds(first0, size0)], rhs0.at[s, pl.ds(0, size0)]))
            started = []
            for n, (source, target) in enumerate(moves):
                copy = pltpu.make_async_copy(source, target, sem.at[s, n])
                copy.start()
                started.append(copy)
            copies[s] += started
        for n, i in enumerate(steps):
            (a0, p0), (a1, p1), (a2, p2), (al, pL), (ar, pR) = plan[n]
            here = small_refs[a0][p0]
            before = small_refs[a1][p1]
            later = small_refs[a2][p2]
            if i == 0:
                before = jnp.concatenate([small_refs[ring_places[0]][...], before[: z.segments - 1]], axis=0)
            if i == z.steps - 1:
                later = jnp.concatenate([later[1:], small_refs[ring_places[1]][...]], axis=0)
            smooth_buf[n] = smoothed(z, here, before, later, small_refs[al][pL], small_refs[ar][pR])
        operator = operand_left(z.square(viscous_ref[...]))

        def source(field, force, matrix, smooth):
            force = force + smooth * product(operator, operand_right(field))
            return product(operand_left(matrix), operand_right(force))

        sends = []
        for s0 in range(0, z.segments, batch):
            group = range(s0, s0 + batch)
            for s in group:
                for copy in copies[s]:
                    copy.wait()
            fields = [carry_ref[s] if has_carry else None for s in group]
            for n in range(count):
                offset = (low + n) * z.height - first
                for g, s in enumerate(group):
                    k = s * z.steps + low + n
                    smooth = smooth_buf[n, s : s + 1, :]
                    value = source(
                        read_field(z, state_buf, (s,), offset),
                        read_field(z, rhs_buf, (s,), offset),
                        read_matrix(z, inverse_buf, k),
                        smooth,
                    )
                    if fields[g] is not None:
                        value = value + product(
                            operand_left(read_matrix(z, gain_buf, k)), operand_right(fields[g])
                        )
                    fields[g] = value
                    write_field(z, stage, (s,), n * z.height, value)
            for g, s in enumerate(group):
                copy = pltpu.make_async_copy(stage.at[s], out_ref.at[s], out_sem.at[s])
                copy.start()
                sends.append(copy)
                end_ref[s] = fields[g]
                if with_first:
                    smooth = smooth_buf[count, s : s + 1, :]
                    start_ref[s] = source(
                        read_field(z, state0, (s,), -first0),
                        read_field(z, rhs0, (s,), -first0),
                        read_matrix(z, inverse_buf, s * z.steps),
                        smooth,
                    )
        for copy in sends:
            copy.wait()

    field = f32(z.segments, z.pad, z.cols)
    outs = [f32(z.segments, message, z.ax)] + [field] * (2 if with_first else 1)
    operands = [state, rhs, viscous, inverse] + ([gain] if needs_gain else [])
    in_specs = [spec_hbm(), spec_hbm(), spec_vmem()] + [spec_hbm()] * (len(operands) - 3)
    operands += arrays + ([carry] if has_carry else [])
    in_specs += [spec_vmem()] * (small + (1 if has_carry else 0))
    aliases = {}
    out_specs = [spec_hbm()] + [spec_vmem()] * (2 if with_first else 1)
    if held is not None:
        aliases = {len(operands): len(outs)}
        operands.append(held)
        in_specs.append(spec_hbm())
        outs.append(f32(*held.shape))
        out_specs.append(spec_hbm())
    scratch = [
        pltpu.VMEM((z.segments, size + z.spill, z.ax), F32),
        pltpu.VMEM((z.segments, size + z.spill, z.ax), F32),
        pltpu.VMEM(inverse.shape, F32),
        pltpu.VMEM(gain.shape, F32),
        pltpu.VMEM((len(steps), z.segments, z.cols), F32),
        pltpu.VMEM((z.segments, message, z.ax), F32),
        pltpu.SemaphoreType.DMA((z.segments, 4)),
        pltpu.SemaphoreType.DMA((z.segments, 2)),
        pltpu.SemaphoreType.DMA((z.segments,)),
    ]
    if with_first:
        scratch += [pltpu.VMEM((z.segments, size0 + z.spill, z.ax), F32)] * 2
    result = call(
        kernel,
        f"sweep_{low}",
        outs,
        in_specs,
        out_specs,
        scratch,
        z.flops * len(steps) * z.segments * 3,
        4 * z.segments * size * z.ax * 4,
        aliases,
    )(*operands)
    return result[0], result[1:]


def maps_call(z, me, gain, after):
    def kernel(me_ref, gain_ref, *refs):
        own_ref, head_ref, tail_ref, whole_ref, prefix_ref, group_ref = refs[len(after) :]
        mine = me_ref[0]

        def times(a, b):
            return product(operand_left(a), operand_right(b))

        own_ref[0] = read_matrix(z, gain_ref, mine * z.steps)
        values = [read_matrix(z, gain_ref, e * z.steps + 1) for e in range(z.segments)]
        for i in range(1, z.steps):
            for e in range(z.segments):
                if i > 1:
                    values[e] = times(read_matrix(z, gain_ref, e * z.steps + i), values[e])

                @pl.when(e == mine)
                def _(i=i, value=values[e]):
                    own_ref[i] = value

        for e in range(z.segments):
            head_ref[e] = read_matrix(z, gain_ref, e * z.steps)
            tail_ref[e] = values[e]
            whole_ref[e] = times(values[e], head_ref[e])
        value = whole_ref[0]
        prefix_ref[0] = value
        for e in range(1, z.segments):
            prefix_ref[e] = value
            value = times(whole_ref[e], value)
        group_ref[...] = value

    square = (z.pad, z.pad)
    outs = [f32(z.steps, *square)] + [f32(z.segments, *square)] * 4 + [f32(*square)]
    return call(
        kernel,
        "maps",
        outs,
        [spec_smem(), spec_vmem()] + [spec_any()] * len(after),
        [spec_vmem()] * 6,
        [],
        z.flops * z.segments * (z.steps + 1) // 2,
        4 * z.segments * z.steps * z.pad * z.pad,
    )(me, gain, *after)


def chain_call(z, starts, ends, tails, wholes, group):
    def kernel(start_ref, end_ref, tail_ref, whole_ref, group_ref, before_ref, pack_ref):
        value = None
        for e in range(z.segments):
            shift = end_ref[e] + product(operand_left(tail_ref[e]), operand_right(start_ref[e]))
            if e > 0:
                before_ref[e] = value
                shift = shift + product(operand_left(whole_ref[e]), operand_right(value))
            else:
                before_ref[0] = jnp.zeros_like(shift)
            value = shift
        pack_ref[:, : z.cols] = value
        pack_ref[:, z.cols :] = group_ref[...]

    return call(
        kernel,
        "chain",
        [f32(z.segments, z.pad, z.cols), f32(z.pad, z.cols + z.pad)],
        [spec_vmem()] * 5,
        [spec_vmem()] * 2,
        [],
        z.flops * z.segments * 2,
        4 * z.segments * z.pad * z.cols * 4,
    )(starts, ends, tails, wholes, group)


def first_call(z, places, packs, before, prefix, heads, starts):
    pairs = z.segments // 2
    message = z.message(1)

    def kernel(*refs):
        places_ref, refs = refs[0], refs[1:]
        pack_refs, refs = refs[: z.groups], refs[z.groups :]
        before_ref, prefix_ref, head_ref, start_ref, keep_ref, give_ref = refs
        mine = places_ref[0]
        group = places_ref[1]
        value = jnp.zeros((z.pad, z.cols), F32)
        matrices = [operand_left(ref[:, z.cols :]) for ref in pack_refs]
        for t in range(2 * z.groups - 1, 0, -1):
            n = t % z.groups
            moved = product(matrices[n], operand_right(value)) + pack_refs[n][:, : z.cols]
            value = jnp.where(t <= z.groups + group, moved, 0.0)
        incoming = operand_right(value)
        side = lax.rem(mine, 2)
        for d in range(pairs):
            for ref, part in ((give_ref, 1 - side), (keep_ref, side)):
                e = lax.rem(mine - side + 2 * d, z.segments) + part
                arriving = jnp.where(e == 0, value, before_ref[e] + product(operand_left(prefix_ref[e]), incoming))
                matrix = operand_left(head_ref[e])
                solved = start_ref[e] + product(matrix, operand_right(arriving))
                write_field(z, ref, (d,), 0, solved)

    return call(
        kernel,
        "first",
        [f32(pairs, message, z.ax)] * 2,
        [spec_smem()] + [spec_vmem()] * (z.groups + 4),
        [spec_vmem()] * 2,
        [],
        z.flops * (z.segments * 2 + 2 * z.groups),
        4 * z.segments * z.pad * z.cols * 4,
    )(places, *packs, before, prefix, heads, starts)


def couple_call(z, keep, got, held):
    pairs = z.segments // 2
    message = z.message(1)

    def kernel(keep_ref, got_ref, _, *refs):
        for d in range(pairs):
            refs[d][0] = keep_ref[d]
            refs[d][1] = got_ref[d]

    return call(
        kernel,
        "couple",
        [f32(2, message, z.ax)] * pairs + [f32(*held.shape)],
        [spec_vmem()] * 2 + [spec_hbm()],
        [spec_vmem()] * pairs + [spec_hbm()],
        [],
        0,
        4 * 4 * pairs * message * z.ax,
        {2: pairs},
    )(keep, got, held)


def open_call(z, me, firsts):
    radial = z.segments * z.rows
    tall = z.nodes * radial
    pairs = z.segments // 2

    def kernel(*refs):
        me_ref, refs = refs[0], refs[1:]
        first_refs, refs = refs[:pairs], refs[pairs:]
        out_ref, operand_ref, stage, sem = refs
        mine = me_ref[0]
        side = lax.rem(mine, 2)
        for d in range(pairs):
            for part in range(2):
                src = lax.rem(mine - side - 2 * d + z.segments, z.segments) + (side if part == 0 else 1 - side)
                field = read_exact(z, first_refs[d], (part,), 0)
                empty = jnp.zeros((z.pad - z.nodes, z.cols), F32)
                operand_ref[src] = operand_right(jnp.concatenate([field, empty], axis=0))
                for j in range(z.rows):
                    stage[pl.ds(src * z.rows + j, z.nodes, stride=radial), :] = field[:, j * z.ax : (j + 1) * z.ax]
        copy = pltpu.make_async_copy(stage, out_ref.at[0], sem)
        copy.start()
        copy.wait()

    return call(
        kernel,
        "finish_0",
        [f32(z.steps, tall, z.ax), jax.ShapeDtypeStruct((z.segments, 2 * z.pad, z.cols), BF16)],
        [spec_smem()] + [spec_vmem()] * pairs,
        [spec_hbm(), spec_vmem()],
        [pltpu.VMEM((tall, z.ax), F32), pltpu.SemaphoreType.DMA],
        0,
        4 * 2 * tall * z.ax,
    )(me, *firsts)


def finish_call(z, chunk, own, operands, messages, out):
    low, high = chunk
    count = high - low
    radial = z.segments * z.rows
    tall = z.nodes * radial
    message = z.message(count)

    def kernel(own_ref, operand_ref, message_ref, _, out_ref, buf, stage, sem, out_sem):
        copies = [pltpu.make_async_copy(message_ref.at[e], buf.at[e], sem.at[e]) for e in range(z.segments)]
        for copy in copies:
            copy.start()
        sends = []
        for n in range(count):
            matrix = operand_left(own_ref[low + n])
            for e in range(z.segments):
                if n == 0:
                    copies[e].wait()
                value = product(matrix, operand_ref[e])[: z.nodes] + read_exact(z, buf, (e,), n * z.height)
                for j in range(z.rows):
                    rows = pl.ds(e * z.rows + j, z.nodes, stride=radial)
                    stage[n, rows, :] = value[:, j * z.ax : (j + 1) * z.ax]
            copy = pltpu.make_async_copy(stage.at[n], out_ref.at[low + n], out_sem.at[n])
            copy.start()
            sends.append(copy)
        for copy in sends:
            copy.wait()

    return call(
        kernel,
        f"finish_{low}",
        f32(z.steps, tall, z.ax),
        [spec_vmem(), spec_vmem(), spec_hbm(), spec_hbm()],
        spec_hbm(),
        [
            pltpu.VMEM((z.segments, message, z.ax), F32),
            pltpu.VMEM((count, tall, z.ax), F32),
            pltpu.SemaphoreType.DMA((z.segments,)),
            pltpu.SemaphoreType.DMA((count,)),
        ],
        z.flops * count * z.segments,
        4 * 2 * count * tall * z.ax,
        {3: 0},
    )(own, operands, messages, out)


def shift_by(array, axis, by):
    size = lax.axis_size(axis)
    return lax.ppermute(array, axis, [(i, (i + by) % size) for i in range(size)])


def neighbours(head, tail):
    size = lax.axis_size("elem")
    left = lax.ppermute(tail, "elem", [(i, i + 1) for i in range(size - 1)])
    right = lax.ppermute(head, "elem", [(i + 1, i) for i in range(size - 1)])
    return left, right


def spread(messages):
    return lax.all_to_all(messages, "elem", 0, 0, tiled=True)


def chunks_of(steps):
    if steps >= 8:
        return [(1, 3), (3, 6), (6, steps)]
    return [(1, 2), (2, 3), (3, steps)]


def body(state, rhs, to_modal, viscous_op, sweep_gain, inv_blocks):
    segments = lax.axis_size("elem")
    groups = lax.axis_size("blk")
    z = Sizes(state, segments, groups)
    state = state.reshape(segments, z.steps * z.height, z.ax)
    rhs = rhs.reshape(segments, z.steps * z.height, z.ax)
    gain = jnp.transpose(sweep_gain, (1, 0, 2))
    inverse = jnp.transpose(inv_blocks, (1, 0, 2))
    here = lax.axis_index("elem").astype(jnp.int32)
    me = here.reshape(1)
    places = jnp.stack([here, lax.axis_index("blk").astype(jnp.int32)])
    sensors, lefts, rights = {}, {}, {}

    def sense(low, high, after, earlier=()):
        sensor, head, tail = sensor_call(z, state, to_modal, after, earlier, low, high)
        for i in range(low, high):
            sensors[i] = (sensor, i - low)
        return sensor, head, tail

    def edges(low, high, head, tail):
        left, right = neighbours(head, tail)
        for i in range(low, high):
            lefts[i], rights[i] = (left, i - low), (right, i - low)

    def sweep(chunk, ring, carry, held):
        return sweep_call(
            z, chunk, state, rhs, viscous_op, gain, inverse, sensors, lefts, rights, ring, carry, held
        )

    one, two, three = chunks_of(z.steps)
    opening, head, tail = sense(0, 3, [])
    edges(0, 3, head, tail)
    known = 3
    earlier = []
    if one[1] >= known:
        more, _, _ = sense(known, one[1] + 1, [opening])
        earlier = [more]
        known = one[1] + 1
    messages_one, (carry,) = sweep(one, None, None, None)
    last, head, tail = sense(known, z.steps, [carry], earlier)
    edges(3, z.steps, head, tail)
    ring = [
        shift_by(last[z.steps - 1 - known, segments - 1 :], "blk", 1),
        shift_by(opening[0, :1], "blk", -1),
    ]
    own, heads, tails, wholes, prefix, group = maps_call(z, me, gain, [carry])
    messages_two, (carry,) = sweep(two, None, carry, None)
    messages_three, (carry, starts, messages_two) = sweep(three, ring, carry, messages_two)
    before, pack = chain_call(z, starts, carry, tails, wholes, group)
    packs = [pack] + [shift_by(pack, "blk", s) for s in range(1, groups)]
    keep, give = first_call(z, places, packs, before, prefix, heads, starts)
    got = lax.ppermute(give, "elem", [(i, i ^ 1) for i in range(segments)])
    *firsts, messages_three = couple_call(z, keep, got, messages_three)
    firsts = [firsts[0]] + [shift_by(firsts[d], "elem", 2 * d) for d in range(1, segments // 2)]
    received_one = spread(messages_one)
    received_two = spread(messages_two)
    received_three = spread(messages_three)
    out, operands = open_call(z, me, firsts)
    for chunk, messages in ((one, received_one), (two, received_two), (three, received_three)):
        out = finish_call(z, chunk, own, operands, messages, out)
    return out.reshape(z.steps, z.nodes, segments * z.rows, z.ax)


def solution(mesh):
    in_specs = (
        P("blk", None, "elem", None),
        P("blk", None, "elem", None),
        P(),
        P(),
        P("blk", None, None),
        P("blk", None, None),
    )
    out_specs = P(("blk", "elem"), None, None, None)
    return jax.shard_map(body, mesh=mesh, in_specs=in_specs, out_specs=out_specs, check_vma=False)
```

```python
import functools

import jax
import jax.numpy as jnp
from jax import lax
from jax.experimental import pallas as pl
from jax.experimental.pallas import tpu as pltpu
from jax.sharding import PartitionSpec as P

ORDER = 4
F32 = jnp.float32
BF16 = jnp.bfloat16
MIB = 1024 * 1024
TILE = 8
LANES = 128


def operand_left(a):
    high = a.astype(BF16)
    low = (a - high.astype(F32)).astype(BF16)
    return jnp.concatenate([jnp.concatenate([high, high], axis=1), jnp.concatenate([low, low], axis=1)], axis=0)


def operand_right(x):
    high = x.astype(BF16)
    return jnp.concatenate([high, (x - high.astype(F32)).astype(BF16)], axis=0)


def product(left, right):
    both = jnp.dot(left, right, preferred_element_type=F32)
    half = left.shape[0] // 2
    return both[:half] + both[half:]


def spec_any():
    return pl.BlockSpec(memory_space=pl.ANY)


def spec_hbm():
    return pl.BlockSpec(memory_space=pltpu.HBM)


def spec_vmem():
    return pl.BlockSpec(memory_space=pltpu.VMEM)


def spec_smem():
    return pl.BlockSpec(memory_space=pltpu.SMEM)


def call(kernel, name, outs, in_specs, out_specs, scratch, flops, nbytes, aliases=None, limit=57):
    return pl.pallas_call(
        kernel,
        name=name,
        out_shape=outs,
        in_specs=in_specs,
        out_specs=out_specs,
        scratch_shapes=scratch,
        input_output_aliases=aliases or {},
        compiler_params=pltpu.CompilerParams(vmem_limit_bytes=limit * MIB),
        cost_estimate=pl.CostEstimate(flops=int(flops), bytes_accessed=int(nbytes), transcendentals=0),
    )


def f32(*shape):
    return jax.ShapeDtypeStruct(shape, F32)


def up(value, unit):
    return -(-value // unit) * unit


class Sizes:
    def __init__(self, state, segments, groups):
        count, self.nodes, self.rows, self.ax = state.shape
        self.count = count
        self.segments = segments
        self.groups = groups
        self.steps = count // segments
        self.cols = self.rows * self.ax
        self.height = self.nodes * self.rows
        self.pad = up(self.nodes, LANES)
        self.spill = up((self.pad - self.nodes) * self.rows, TILE)
        self.flops = 2 * 4 * self.pad * self.pad * self.cols

    def window(self, low, high):
        first = low * self.height // TILE * TILE
        return first, up(high * self.height, TILE) - first

    def message(self, count):
        return up(count * self.height, TILE)

    def rows_masked(self, x):
        cut = self.nodes // TILE * TILE
        rest = x[cut:]
        inside = lax.broadcasted_iota(jnp.int32, rest.shape, 0) < self.nodes - cut
        return jnp.concatenate([x[:cut], jnp.where(inside, rest, 0.0)], axis=0)

    def square(self, x):
        x = jnp.concatenate([x, jnp.zeros((self.nodes, self.pad - self.nodes), F32)], axis=1)
        return jnp.concatenate([x, jnp.zeros((self.pad - self.nodes, self.pad), F32)], axis=0)


def read_field(z, ref, lead, offset):
    parts = [ref[lead + (pl.ds(offset + j, z.pad, stride=z.rows), slice(None))] for j in range(z.rows)]
    return z.rows_masked(jnp.concatenate(parts, axis=1))


def read_exact(z, ref, lead, offset):
    parts = [ref[lead + (pl.ds(offset + j, z.nodes, stride=z.rows), slice(None))] for j in range(z.rows)]
    return jnp.concatenate(parts, axis=1)


def write_field(z, ref, lead, offset, value):
    for j in range(z.rows):
        rows = pl.ds(offset + j, z.nodes, stride=z.rows)
        ref[lead + (rows, slice(None))] = value[: z.nodes, j * z.ax : (j + 1) * z.ax]


def read_matrix(z, ref, k):
    return z.square(ref[:, k, :])


def sensor_call(z, state, to_modal):
    batch = 4 if z.segments % 4 == 0 else 1
    tall = z.steps * z.height

    def kernel(state_ref, modal_ref, sensor_ref, head_ref, tail_ref, buf, modal_buf, sem, modal_sem):
        modal_copy = pltpu.make_async_copy(modal_ref, modal_buf, modal_sem)
        modal_copy.start()
        copies = [
            pltpu.make_async_copy(state_ref.at[e], buf.at[e, pl.ds(0, tall)], sem.at[e]) for e in range(z.segments)
        ]
        for copy in copies:
            copy.start()
        modal_copy.wait()
        matrix = operand_left(z.square(modal_buf[...]))
        for e0 in range(0, z.segments, batch):
            for e in range(e0, e0 + batch):
                copies[e].wait()
            for e in range(e0, e0 + batch):
                for i in range(z.steps):
                    modal = product(matrix, operand_right(read_field(z, buf, (e,), i * z.height)))
                    squares = modal * modal
                    lower = jnp.sum(squares[: ORDER**3], axis=0, keepdims=True)
                    upper = jnp.sum(squares[ORDER**3 :], axis=0, keepdims=True)
                    sensor = (upper / z.nodes) / ((lower + upper) / z.nodes + 1e-6)
                    sensor_ref[i, e : e + 1, :] = sensor
                    head_ref[i, e : e + 1, :] = sensor[:, : z.ax]
                    tail_ref[i, e : e + 1, :] = sensor[:, z.cols - z.ax :]

    outs = [f32(z.steps, z.segments, z.cols)] + [f32(z.steps, z.segments, z.ax)] * 2
    return call(
        kernel,
        "sensor",
        outs,
        [spec_hbm()] * 2,
        [spec_vmem()] * 3,
        [
            pltpu.VMEM((z.segments, tall + z.spill, z.ax), F32),
            pltpu.VMEM((z.nodes, z.nodes), F32),
            pltpu.SemaphoreType.DMA((z.segments,)),
            pltpu.SemaphoreType.DMA,
        ],
        z.flops * z.steps * z.segments,
        4 * z.segments * tall * z.ax,
    )(state, to_modal)


def smoothed(z, sensor, before, after, left, right):
    inner = sensor[:, : z.cols - z.ax]
    outer = sensor[:, z.ax :]
    from_left = jnp.concatenate([left, inner], axis=1)
    from_right = jnp.concatenate([outer, right], axis=1)
    return (4.0 * sensor + before + after + from_left + from_right) / 8.0


def sweep_call(z, chunk, mode, me, state, rhs, viscous, gain, inverse, sensors, lefts, rights, ring, carry, after):
    low, high = chunk
    opened = mode == "open"
    first, size = z.window(low, high)
    count = high - low
    first0, size0 = z.window(0, 1)
    steps = list(range(low, high)) + ([0] if opened else [])
    has_carry = carry is not None
    needs_gain = has_carry or count > 1
    message = z.message(count + (1 if opened else 0))
    edge_outs = low == 1
    pairs = z.segments // 2
    batch = next(n for n in (4, 8, z.segments) if z.segments % n == 0 and n * z.steps % TILE == 0)

    def kernel(*refs):
        me_ref, state_ref, rhs_ref, viscous_ref, inverse_ref, gain_ref, sensor_ref, left_ref, right_ref = refs[:9]
        refs = refs[9:]
        if opened:
            before_ref, behind_ref, refs = refs[0], refs[1], refs[2:]
        if has_carry:
            carry_ref, refs = refs[0], refs[1:]
        refs = refs[len(after) :]
        if mode == "pairs":
            keep_ref, give_ref, refs = refs[0], refs[1], refs[2:]
        else:
            out_ref, refs = refs[0], refs[1:]
        end_ref, refs = refs[0], refs[1:]
        if opened:
            start_ref, refs = refs[0], refs[1:]
        if edge_outs:
            low_ref, high_ref, refs = refs[0], refs[1], refs[2:]
        state_buf, rhs_buf, inverse_buf, gain_buf, viscous_buf, smooth_buf, stage, sem, matrix_sem, out_sem = refs[:10]
        if opened:
            state0, rhs0 = refs[10:]
        viscous_copy = pltpu.make_async_copy(viscous_ref, viscous_buf, out_sem.at[0])
        viscous_copy.start()
        copies = [[] for _ in range(z.segments)]
        for s0 in range(0, z.segments, batch):
            for s in range(s0, s0 + batch):
                moves = [
                    (state_ref.at[s, pl.ds(first, size)], state_buf.at[s, pl.ds(0, size)]),
                    (rhs_ref.at[s, pl.ds(first, size)], rhs_buf.at[s, pl.ds(0, size)]),
                ]
                if opened:
                    moves.append((state_ref.at[s, pl.ds(first0, size0)], state0.at[s, pl.ds(0, size0)]))
                    moves.append((rhs_ref.at[s, pl.ds(first0, size0)], rhs0.at[s, pl.ds(0, size0)]))
                for n, (source, target) in enumerate(moves):
                    copies[s].append(pltpu.make_async_copy(source, target, sem.at[s, n]))
            part = pl.ds(s0 * z.steps, batch * z.steps)
            sources = [(inverse_ref, inverse_buf)] + ([(gain_ref, gain_buf)] if needs_gain else [])
            for n, (source, target) in enumerate(sources):
                copies[s0].append(pltpu.make_async_copy(source.at[:, part], target.at[:, part], matrix_sem.at[s0, n]))
            for s in range(s0, s0 + batch):
                for copy in copies[s]:
                    copy.start()
        for n, i in enumerate(steps):
            before = sensor_ref[(i - 1) % z.steps]
            later = sensor_ref[(i + 1) % z.steps]
            if i == 0:
                before = jnp.concatenate([before_ref[...], before[: z.segments - 1]], axis=0)
            if i == z.steps - 1:
                later = jnp.concatenate([later[1:], behind_ref[...]], axis=0)
            smooth_buf[n] = smoothed(z, sensor_ref[i], before, later, left_ref[i], right_ref[i])
        if edge_outs:
            low_ref[...] = sensor_ref[0, :1]
            high_ref[...] = sensor_ref[z.steps - 1, z.segments - 1 :]
        viscous_copy.wait()
        operator = operand_left(z.square(viscous_buf[...]))
        sends = []
        for s0 in range(0, z.segments, batch):
            group = range(s0, s0 + batch)
            for s in group:
                for copy in copies[s]:
                    copy.wait()
            fields = [carry_ref[s] if has_carry else None for s in group]
            for n, i in enumerate(steps):
                bufs = (state0, rhs0, -first0) if i == 0 else (state_buf, rhs_buf, i * z.height - first)
                moved = [product(operator, operand_right(read_field(z, bufs[0], (s,), bufs[2]))) for s in group]
                forces = [
                    operand_right(read_field(z, bufs[1], (s,), bufs[2]) + smooth_buf[n, s : s + 1, :] * value)
                    for s, value in zip(group, moved)
                ]
                values = [
                    product(operand_left(read_matrix(z, inverse_buf, s * z.steps + i)), force)
                    for s, force in zip(group, forces)
                ]
                if i == 0:
                    for s, value in zip(group, values):
                        start_ref[s] = value
                    continue
                if fields[0] is not None:
                    swept = [
                        product(operand_left(read_matrix(z, gain_buf, s * z.steps + i)), operand_right(field))
                        for s, field in zip(group, fields)
                    ]
                    values = [value + more for value, more in zip(values, swept)]
                fields = values
                for s, value in zip(group, values):
                    write_field(z, stage, (s,), n * z.height, value)
            for s, value in zip(group, fields):
                end_ref[s] = value
                if mode != "pairs":
                    copy = pltpu.make_async_copy(stage.at[s], out_ref.at[s], out_sem.at[s])
                    copy.start()
                    sends.append(copy)
                    continue
                side = lax.rem(me_ref[0], 2)
                place = lax.rem(s // 2 - me_ref[0] // 2 + pairs, pairs)
                own = side == s % 2

                @pl.when(own)
                def _(s=s, place=place):
                    pltpu.make_async_copy(stage.at[s], keep_ref.at[place], out_sem.at[s]).start()

                @pl.when(jnp.logical_not(own))
                def _(s=s, place=place):
                    pltpu.make_async_copy(stage.at[s], give_ref.at[place], out_sem.at[s]).start()

                sends.append(pltpu.make_async_copy(stage.at[s], keep_ref.at[place], out_sem.at[s]))
        for copy in sends:
            copy.wait()

    field = f32(z.segments, z.pad, z.cols)
    outs = [f32(pairs, message, z.ax)] * 2 if mode == "pairs" else [f32(z.segments, message, z.ax)]
    out_specs = [spec_hbm()] * len(outs)
    more = [field] * (2 if opened else 1) + ([f32(1, z.cols)] * 2 if edge_outs else [])
    operands = [me, state, rhs, viscous, inverse, gain, sensors, lefts, rights]
    in_specs = [spec_smem()] + [spec_hbm()] * 5 + [spec_vmem()] * 3
    extra = (list(ring) if opened else []) + ([carry] if has_carry else [])
    scratch = [
        pltpu.VMEM((z.segments, size + z.spill, z.ax), F32),
        pltpu.VMEM((z.segments, size + z.spill, z.ax), F32),
        pltpu.VMEM(inverse.shape, F32),
        pltpu.VMEM(gain.shape, F32),
        pltpu.VMEM(viscous.shape, F32),
        pltpu.VMEM((len(steps), z.segments, z.cols), F32),
        pltpu.VMEM((z.segments, message, z.ax), F32),
        pltpu.SemaphoreType.DMA((z.segments, 4)),
        pltpu.SemaphoreType.DMA((z.segments, 2)),
        pltpu.SemaphoreType.DMA((z.segments,)),
    ]
    if opened:
        scratch += [pltpu.VMEM((z.segments, size0 + z.spill, z.ax), F32)] * 2
    return call(
        kernel,
        f"sweep_{low}",
        outs + more,
        in_specs + [spec_vmem()] * len(extra) + [spec_any()] * len(after),
        out_specs + [spec_vmem()] * len(more),
        scratch,
        z.flops * len(steps) * z.segments * 3,
        4 * z.segments * size * z.ax * 4,
    )(*operands, *extra, *after)


def maps_call(z, me, gain, after):
    def kernel(me_ref, gain_ref, *refs):
        own_ref, head_ref, tail_ref, whole_ref, prefix_ref, group_ref, gain_buf, kept, sem = refs[len(after) :]
        copy = pltpu.make_async_copy(gain_ref, gain_buf, sem)
        copy.start()
        copy.wait()

        def times(a, b):
            return product(operand_left(a), operand_right(b))

        values = [read_matrix(z, gain_buf, e * z.steps + 1) for e in range(z.segments)]
        for i in range(1, z.steps):
            if i > 1:
                values = [
                    times(read_matrix(z, gain_buf, e * z.steps + i), values[e]) for e in range(z.segments)
                ]
            for e in range(z.segments):
                kept[e, i] = values[e]
        heads = [read_matrix(z, gain_buf, e * z.steps) for e in range(z.segments)]
        for e in range(z.segments):
            kept[e, 0] = heads[e]
            head_ref[e] = heads[e]
            tail_ref[e] = values[e]
            whole_ref[e] = times(values[e], heads[e])
        own_ref[...] = kept[me_ref[0]]
        value = whole_ref[0]
        prefix_ref[0] = value
        for e in range(1, z.segments):
            prefix_ref[e] = value
            value = times(whole_ref[e], value)
        group_ref[...] = value

    square = (z.pad, z.pad)
    outs = [f32(z.steps, *square)] + [f32(z.segments, *square)] * 4 + [f32(*square)]
    return call(
        kernel,
        "maps",
        outs,
        [spec_smem(), spec_hbm()] + [spec_any()] * len(after),
        [spec_vmem()] * 6,
        [
            pltpu.VMEM(gain.shape, F32),
            pltpu.VMEM((z.segments, z.steps) + square, F32),
            pltpu.SemaphoreType.DMA,
        ],
        z.flops * z.segments * (z.steps + 1) // 2,
        4 * z.segments * z.steps * z.pad * z.pad,
    )(me, gain, *after)


def chain_call(z, starts, ends, tails, wholes, group):
    def kernel(start_ref, end_ref, tail_ref, whole_ref, group_ref, before_ref, pack_ref):
        value = None
        for e in range(z.segments):
            shift = end_ref[e] + product(operand_left(tail_ref[e]), operand_right(start_ref[e]))
            if e > 0:
                before_ref[e] = value
                shift = shift + product(operand_left(whole_ref[e]), operand_right(value))
            else:
                before_ref[0] = jnp.zeros_like(shift)
            value = shift
        pack_ref[:, : z.cols] = value
        pack_ref[:, z.cols :] = group_ref[...]

    return call(
        kernel,
        "chain",
        [f32(z.segments, z.pad, z.cols), f32(z.pad, z.cols + z.pad)],
        [spec_vmem()] * 5,
        [spec_vmem()] * 2,
        [],
        z.flops * z.segments * 2,
        4 * z.segments * z.pad * z.cols * 4,
    )(starts, ends, tails, wholes, group)


def first_call(z, places, packs, before, prefix, heads, starts, messages, place):
    offset = place * z.height
    base = offset // TILE * TILE
    size = messages.shape[1] - base

    def kernel(*refs):
        places_ref, refs = refs[0], refs[1:]
        pack_refs, refs = refs[: z.groups], refs[z.groups :]
        before_ref, prefix_ref, head_ref, start_ref, message_ref, out_ref, stage, sem = refs
        copies = [
            pltpu.make_async_copy(message_ref.at[e, pl.ds(base, size)], stage.at[e], sem.at[e])
            for e in range(z.segments)
        ]
        for copy in copies:
            copy.start()
        group = places_ref[1]
        value = jnp.zeros((z.pad, z.cols), F32)
        matrices = [operand_left(ref[:, z.cols :]) for ref in pack_refs]
        for t in range(2 * z.groups - 1, 0, -1):
            n = t % z.groups
            moved = product(matrices[n], operand_right(value)) + pack_refs[n][:, : z.cols]
            value = jnp.where(t <= z.groups + group, moved, 0.0)
        incoming = operand_right(value)
        arriving = [value] + [
            before_ref[e] + product(operand_left(prefix_ref[e]), incoming) for e in range(1, z.segments)
        ]
        solved = [
            start_ref[e] + product(operand_left(head_ref[e]), operand_right(arriving[e])) for e in range(z.segments)
        ]
        sends = []
        for e in range(z.segments):
            copies[e].wait()
            write_field(z, stage, (e,), offset - base, solved[e])
            copy = pltpu.make_async_copy(stage.at[e], out_ref.at[e, pl.ds(base, size)], sem.at[e])
            copy.start()
            sends.append(copy)
        for copy in sends:
            copy.wait()

    return call(
        kernel,
        "first",
        f32(*messages.shape),
        [spec_smem()] + [spec_vmem()] * (z.groups + 4) + [spec_hbm()],
        spec_hbm(),
        [pltpu.VMEM((z.segments, size, z.ax), F32), pltpu.SemaphoreType.DMA((z.segments,))],
        z.flops * (z.segments * 2 + 2 * z.groups),
        4 * z.segments * z.pad * z.cols * 4,
        {z.groups + 5: 0},
    )(places, *packs, before, prefix, heads, starts, messages)


def couple_call(z, keep, got):
    pairs, message, _ = keep.shape

    def kernel(*refs):
        sources, refs = refs[:2], refs[2:]
        outs, sem = refs[:pairs], refs[pairs]
        copies = []
        for d in range(pairs):
            for n in range(2):
                copies.append(pltpu.make_async_copy(sources[n].at[d], outs[d].at[n], sem.at[d, n]))
        for copy in copies:
            copy.start()
        for copy in copies:
            copy.wait()

    return call(
        kernel,
        "couple",
        [f32(2, message, z.ax)] * pairs,
        [spec_hbm()] * 2,
        [spec_hbm()] * pairs,
        [pltpu.SemaphoreType.DMA((pairs, 2))],
        0,
        4 * 4 * pairs * message * z.ax,
    )(keep, got)


def finish_call(z, chunk, mode, me, own, messages, place, operands, out):
    low, high = chunk
    count = high - low
    radial = z.segments * z.rows
    tall = z.nodes * radial
    opened = mode == "open"
    paired = mode == "pairs"
    pairs = z.segments // 2
    if paired:
        message = messages[0].shape[1]
    else:
        message = messages.shape[1]
        messages = [messages]
    steps = list(range(low, high)) + ([0] if opened else [])

    def kernel(*refs):
        me_ref, own_ref, refs = refs[0], refs[1], refs[2:]
        message_refs, refs = refs[: len(messages)], refs[len(messages) :]
        if opened:
            out_ref, operand_ref, refs = refs[0], refs[1], refs[2:]
        else:
            operand_ref, _, out_ref, refs = refs[0], refs[1], refs[2], refs[3:]
        buf, own_buf, operand_buf, stage, sem, in_sem, out_sem = refs
        copies = []
        own_copy = pltpu.make_async_copy(own_ref, own_buf, in_sem.at[0])
        own_copy.start()
        if not opened:
            operand_copy = pltpu.make_async_copy(operand_ref, operand_buf, in_sem.at[1])
            operand_copy.start()
        if paired:
            mine = me_ref[0]
            side = lax.rem(mine, 2)
            for d in range(pairs):
                pair = lax.rem(mine // 2 - d + pairs, pairs) * 2
                for n in range(2):
                    e = pair + (side if n == 0 else 1 - side)
                    copies.append(pltpu.make_async_copy(message_refs[d].at[n], buf.at[e], sem.at[2 * d + n]))
        else:
            copies = [pltpu.make_async_copy(message_refs[0].at[e], buf.at[e], sem.at[e]) for e in range(z.segments)]
        for copy in copies:
            copy.start()
        own_copy.wait()
        if not opened:
            operand_copy.wait()
        for copy in copies:
            copy.wait()
        sends = []

        def put(n, i, e, value):
            for j in range(z.rows):
                rows = pl.ds(e * z.rows + j, z.nodes, stride=radial)
                stage[n, rows, :] = value[: z.nodes, j * z.ax : (j + 1) * z.ax]

        def send(n, i):
            copy = pltpu.make_async_copy(stage.at[n], out_ref.at[i], out_sem.at[n])
            copy.start()
            sends.append(copy)

        if opened:
            for e in range(z.segments):
                field = read_exact(z, buf, (e,), count * z.height)
                empty = jnp.zeros((z.pad - z.nodes, z.cols), F32)
                operand_buf[e] = operand_right(jnp.concatenate([field, empty], axis=0))
                put(count, 0, e, field)
            send(count, 0)
            operand_copy = pltpu.make_async_copy(operand_buf, operand_ref, in_sem.at[1])
            operand_copy.start()
            sends.append(operand_copy)
        for n in range(count):
            matrix = operand_left(own_buf[low + n])
            for e in range(z.segments):
                value = product(matrix, operand_buf[e])[: z.nodes]
                put(n, low + n, e, value + read_exact(z, buf, (e,), (place + n) * z.height))
            send(n, low + n)
        for copy in sends:
            copy.wait()

    result = f32(z.steps, tall, z.ax)
    operand_shape = (z.segments, 2 * z.pad, z.cols)
    inputs = [me, own] + list(messages)
    in_specs = [spec_smem()] + [spec_hbm()] * (len(inputs) - 1)
    aliases = {}
    if opened:
        outs = [result, jax.ShapeDtypeStruct(operand_shape, BF16)]
        out_specs = [spec_hbm()] * 2
    else:
        inputs += [operands, out]
        in_specs += [spec_hbm()] * 2
        aliases = {len(inputs) - 1: 0}
        outs = result
        out_specs = spec_hbm()
    return call(
        kernel,
        f"finish_{low}",
        outs,
        in_specs,
        out_specs,
        [
            pltpu.VMEM((z.segments, message, z.ax), F32),
            pltpu.VMEM((z.steps, z.pad, z.pad), F32),
            pltpu.VMEM(operand_shape, BF16),
            pltpu.VMEM((len(steps), tall, z.ax), F32),
            pltpu.SemaphoreType.DMA((z.segments,)),
            pltpu.SemaphoreType.DMA((2,)),
            pltpu.SemaphoreType.DMA((len(steps),)),
        ],
        z.flops * count * z.segments,
        4 * 2 * count * tall * z.ax,
        aliases,
    )(*inputs)


def shift_by(array, axis, by):
    size = lax.axis_size(axis)
    return lax.ppermute(array, axis, [(i, (i + by) % size) for i in range(size)])


def neighbours(head, tail):
    size = lax.axis_size("elem")
    left = lax.ppermute(tail, "elem", [(i, i + 1) for i in range(size - 1)])
    right = lax.ppermute(head, "elem", [(i + 1, i) for i in range(size - 1)])
    return left, right


def spread(messages):
    return lax.all_to_all(messages, "elem", 0, 0, tiled=True)


def chunks_of(steps):
    if steps >= 8:
        return [(1, 3), (3, 5), (5, steps)]
    return [(1, 2), (2, 3), (3, steps)]


def body(state, rhs, to_modal, viscous_op, sweep_gain, inv_blocks):
    segments = lax.axis_size("elem")
    groups = lax.axis_size("blk")
    z = Sizes(state, segments, groups)
    state = state.reshape(segments, z.steps * z.height, z.ax)
    rhs = rhs.reshape(segments, z.steps * z.height, z.ax)
    gain = jnp.transpose(sweep_gain, (1, 0, 2))
    inverse = jnp.transpose(inv_blocks, (1, 0, 2))
    here = lax.axis_index("elem").astype(jnp.int32)
    me = here.reshape(1)
    places = jnp.stack([here, lax.axis_index("blk").astype(jnp.int32)])
    one, two, three = chunks_of(z.steps)
    sensors, head, tail = sensor_call(z, state, to_modal)
    lefts, rights = neighbours(head, tail)

    def sweep(chunk, mode, ring, carry, after):
        return sweep_call(
            z, chunk, mode, me, state, rhs, viscous_op, gain, inverse, sensors, lefts, rights, ring, carry, after
        )

    messages_one, carry, low, high = sweep(one, "all", None, None, [])
    ring = [shift_by(high, "blk", 1), shift_by(low, "blk", -1)]
    own, heads, tails, wholes, prefix, group = maps_call(z, me, gain, [carry])
    keep, give, carry = sweep(two, "pairs", None, carry, [group])
    messages_three, carry, starts = sweep(three, "open", ring, carry, [])
    before, pack = chain_call(z, starts, carry, tails, wholes, group)
    packs = [pack] + [shift_by(pack, "blk", s) for s in range(1, groups)]
    place = three[1] - three[0]
    messages_three = first_call(z, places, packs, before, prefix, heads, starts, messages_three, place)
    got = lax.ppermute(give, "elem", [(i, i ^ 1) for i in range(segments)])
    coupled = couple_call(z, keep, got)
    coupled = [coupled[0]] + [shift_by(coupled[d], "elem", 2 * d) for d in range(1, segments // 2)]
    received_one = spread(messages_one)
    received_three = spread(messages_three)
    out, operands = finish_call(z, three, "open", me, own, received_three, 0, None, None)
    out = finish_call(z, one, "all", me, own, received_one, 0, operands, out)
    out = finish_call(z, two, "pairs", me, own, coupled, 0, operands, out)
    return out.reshape(z.steps, z.nodes, segments * z.rows, z.ax)


def solution(mesh):
    in_specs = (
        P("blk", None, "elem", None),
        P("blk", None, "elem", None),
        P(),
        P(),
        P("blk", None, None),
        P("blk", None, None),
    )
    out_specs = P(("blk", "elem"), None, None, None)
    return jax.shard_map(body, mesh=mesh, in_specs=in_specs, out_specs=out_specs, check_vma=False)
```

```python
import functools

import jax
import jax.numpy as jnp
from jax import lax
from jax.experimental import pallas as pl
from jax.experimental.pallas import tpu as pltpu
from jax.sharding import PartitionSpec as P

ORDER = 4
F32 = jnp.float32
BF16 = jnp.bfloat16
MIB = 1024 * 1024
TILE = 8
LANES = 128


def operand_left(a):
    high = a.astype(BF16)
    low = (a - high.astype(F32)).astype(BF16)
    return jnp.concatenate([jnp.concatenate([high, high], axis=1), jnp.concatenate([low, low], axis=1)], axis=0)


def operand_right(x):
    high = x.astype(BF16)
    return jnp.concatenate([high, (x - high.astype(F32)).astype(BF16)], axis=0)


def product(left, right):
    both = jnp.dot(left, right, preferred_element_type=F32)
    half = left.shape[0] // 2
    return both[:half] + both[half:]


def spec_any():
    return pl.BlockSpec(memory_space=pl.ANY)


def spec_hbm():
    return pl.BlockSpec(memory_space=pltpu.HBM)


def spec_vmem():
    return pl.BlockSpec(memory_space=pltpu.VMEM)


def spec_smem():
    return pl.BlockSpec(memory_space=pltpu.SMEM)


def call(kernel, name, outs, in_specs, out_specs, scratch, flops, nbytes, aliases=None, limit=57):
    return pl.pallas_call(
        kernel,
        name=name,
        out_shape=outs,
        in_specs=in_specs,
        out_specs=out_specs,
        scratch_shapes=scratch,
        input_output_aliases=aliases or {},
        compiler_params=pltpu.CompilerParams(vmem_limit_bytes=limit * MIB),
        cost_estimate=pl.CostEstimate(flops=int(flops), bytes_accessed=int(nbytes), transcendentals=0),
    )


def f32(*shape):
    return jax.ShapeDtypeStruct(shape, F32)


def up(value, unit):
    return -(-value // unit) * unit


class Sizes:
    def __init__(self, state, segments, groups):
        count, self.nodes, self.rows, self.ax = state.shape
        self.count = count
        self.segments = segments
        self.groups = groups
        self.steps = count // segments
        self.cols = self.rows * self.ax
        self.height = self.nodes * self.rows
        self.pad = up(self.nodes, LANES)
        self.spill = up((self.pad - self.nodes) * self.rows, TILE)
        self.flops = 2 * 4 * self.pad * self.pad * self.cols

    def window(self, low, high):
        first = low * self.height // TILE * TILE
        return first, up(high * self.height, TILE) - first

    def message(self, count):
        return up(count * self.height, TILE)

    def rows_masked(self, x):
        cut = self.nodes // TILE * TILE
        rest = x[cut:]
        inside = lax.broadcasted_iota(jnp.int32, rest.shape, 0) < self.nodes - cut
        return jnp.concatenate([x[:cut], jnp.where(inside, rest, 0.0)], axis=0)

    def square(self, x):
        x = jnp.concatenate([x, jnp.zeros((self.nodes, self.pad - self.nodes), F32)], axis=1)
        return jnp.concatenate([x, jnp.zeros((self.pad - self.nodes, self.pad), F32)], axis=0)


def read_field(z, ref, lead, offset):
    parts = [ref[lead + (pl.ds(offset + j, z.pad, stride=z.rows), slice(None))] for j in range(z.rows)]
    return z.rows_masked(jnp.concatenate(parts, axis=1))


def read_exact(z, ref, lead, offset):
    parts = [ref[lead + (pl.ds(offset + j, z.nodes, stride=z.rows), slice(None))] for j in range(z.rows)]
    return jnp.concatenate(parts, axis=1)


def write_field(z, ref, lead, offset, value):
    for j in range(z.rows):
        rows = pl.ds(offset + j, z.nodes, stride=z.rows)
        ref[lead + (rows, slice(None))] = value[: z.nodes, j * z.ax : (j + 1) * z.ax]


def read_matrix(z, ref, k):
    return z.square(ref[:, k, :])


def sensor_call(z, state, to_modal):
    batch = 4 if z.segments % 4 == 0 else 1
    tall = z.steps * z.height

    def kernel(state_ref, modal_ref, sensor_ref, head_ref, tail_ref, buf, modal_buf, sem, modal_sem):
        modal_copy = pltpu.make_async_copy(modal_ref, modal_buf, modal_sem)
        modal_copy.start()
        copies = [
            pltpu.make_async_copy(state_ref.at[e], buf.at[e, pl.ds(0, tall)], sem.at[e]) for e in range(z.segments)
        ]
        for copy in copies:
            copy.start()
        modal_copy.wait()
        matrix = operand_left(z.square(modal_buf[...]))
        for e0 in range(0, z.segments, batch):
            for e in range(e0, e0 + batch):
                copies[e].wait()
            for e in range(e0, e0 + batch):
                for i in range(z.steps):
                    modal = product(matrix, operand_right(read_field(z, buf, (e,), i * z.height)))
                    squares = modal * modal
                    lower = jnp.sum(squares[: ORDER**3], axis=0, keepdims=True)
                    upper = jnp.sum(squares[ORDER**3 :], axis=0, keepdims=True)
                    sensor = (upper / z.nodes) / ((lower + upper) / z.nodes + 1e-6)
                    sensor_ref[i, e : e + 1, :] = sensor
                    head_ref[i, e : e + 1, :] = sensor[:, : z.ax]
                    tail_ref[i, e : e + 1, :] = sensor[:, z.cols - z.ax :]

    outs = [f32(z.steps, z.segments, z.cols)] + [f32(z.steps, z.segments, z.ax)] * 2
    return call(
        kernel,
        "sensor",
        outs,
        [spec_hbm()] * 2,
        [spec_vmem()] * 3,
        [
            pltpu.VMEM((z.segments, tall + z.spill, z.ax), F32),
            pltpu.VMEM((z.nodes, z.nodes), F32),
            pltpu.SemaphoreType.DMA((z.segments,)),
            pltpu.SemaphoreType.DMA,
        ],
        z.flops * z.steps * z.segments,
        4 * z.segments * tall * z.ax,
    )(state, to_modal)


def smoothed(z, sensor, before, after, left, right):
    inner = sensor[:, : z.cols - z.ax]
    outer = sensor[:, z.ax :]
    from_left = jnp.concatenate([left, inner], axis=1)
    from_right = jnp.concatenate([outer, right], axis=1)
    return (4.0 * sensor + before + after + from_left + from_right) / 8.0


def sweep_call(z, chunk, paired, me, state, rhs, viscous, gain, inverse, sensors, lefts, rights, ring, carry, after):
    low, high = chunk
    opened = high == z.steps
    first, size = z.window(low, high)
    count = high - low
    first0, size0 = z.window(0, 1)
    steps = list(range(low, high)) + ([0] if opened else [])
    has_carry = carry is not None
    gains = list(range(low if has_carry else low + 1, high))
    rest = count - paired
    message = z.message(rest + (1 if opened else 0))
    paired_message = z.message(paired)
    edge_outs = low == 1
    pairs = z.segments // 2
    last, last_size = z.window(low - 2, low - 1)
    batch = next(n for n in (4, 8, z.segments) if z.segments % n == 0 and n * z.steps % TILE == 0)
    narrow = low == 1

    def kernel(*refs):
        me_ref, state_ref, rhs_ref, viscous_ref, inverse_ref, gain_ref, sensor_ref, left_ref, right_ref = refs[:9]
        refs = refs[9:]
        if opened:
            before_ref, behind_ref, refs = refs[0], refs[1], refs[2:]
        if has_carry:
            carry_ref, refs = refs[0], refs[1:]
        refs = refs[len(after) :]
        out_ref, refs = refs[0], refs[1:]
        if paired:
            keep_ref, give_ref, refs = refs[0], refs[1], refs[2:]
        if opened:
            end_ref, start_ref, refs = refs[0], refs[1], refs[2:]
        if edge_outs:
            low_ref, high_ref, refs = refs[0], refs[1], refs[2:]
        state_buf, rhs_buf, inverse_buf, gain_buf, viscous_buf, smooth_buf, stage, sem, matrix_sem, out_sem = refs[:10]
        refs = refs[10:]
        if opened:
            state0, rhs0, refs = refs[0], refs[1], refs[2:]
        if paired:
            pair_stage, pair_sem, refs = refs[0], refs[1], refs[2:]
        if has_carry:
            carry_buf = refs[0]
        viscous_copy = pltpu.make_async_copy(viscous_ref, viscous_buf, out_sem.at[0])
        viscous_copy.start()
        copies = [[] for _ in range(z.segments)]
        for s0 in range(0, z.segments, batch):
            for s in range(s0, s0 + batch):
                moves = [
                    (state_ref.at[s, pl.ds(first, size)], state_buf.at[s, pl.ds(0, size)]),
                    (rhs_ref.at[s, pl.ds(first, size)], rhs_buf.at[s, pl.ds(0, size)]),
                ]
                if opened:
                    moves.append((state_ref.at[s, pl.ds(first0, size0)], state0.at[s, pl.ds(0, size0)]))
                    moves.append((rhs_ref.at[s, pl.ds(first0, size0)], rhs0.at[s, pl.ds(0, size0)]))
                if has_carry:
                    moves.append((carry_ref.at[s, pl.ds(last, last_size)], carry_buf.at[s, pl.ds(0, last_size)]))
                if narrow:
                    for source, target, needed in ((inverse_ref, inverse_buf, steps), (gain_ref, gain_buf, gains)):
                        if needed:
                            part = pl.ds(s * z.steps + needed[0], len(needed))
                            moves.append((source.at[:, part], target.at[:, part]))
                for n, (source, target) in enumerate(moves):
                    copies[s].append(pltpu.make_async_copy(source, target, sem.at[s, n]))
            if not narrow:
                part = pl.ds(s0 * z.steps, batch * z.steps)
                for n, (source, target) in enumerate(((inverse_ref, inverse_buf), (gain_ref, gain_buf))):
                    copy = pltpu.make_async_copy(source.at[:, part], target.at[:, part], matrix_sem.at[s0, n])
                    copies[s0].append(copy)
            for s in range(s0, s0 + batch):
                for copy in copies[s]:
                    copy.start()
        for n, i in enumerate(steps):
            before = sensor_ref[(i - 1) % z.steps]
            later = sensor_ref[(i + 1) % z.steps]
            if i == 0:
                before = jnp.concatenate([before_ref[...], before[: z.segments - 1]], axis=0)
            if i == z.steps - 1:
                later = jnp.concatenate([later[1:], behind_ref[...]], axis=0)
            smooth_buf[n] = smoothed(z, sensor_ref[i], before, later, left_ref[i], right_ref[i])
        if edge_outs:
            low_ref[...] = sensor_ref[0, :1]
            high_ref[...] = sensor_ref[z.steps - 1, z.segments - 1 :]
        viscous_copy.wait()
        operator = operand_left(z.square(viscous_buf[...]))
        sends = []

        def send_pairs(s):
            side = lax.rem(me_ref[0], 2)
            place = lax.rem(s // 2 - me_ref[0] // 2 + pairs, pairs)
            own = side == s % 2

            @pl.when(own)
            def _():
                pltpu.make_async_copy(pair_stage.at[s], keep_ref.at[place], pair_sem.at[s]).start()

            @pl.when(jnp.logical_not(own))
            def _():
                pltpu.make_async_copy(pair_stage.at[s], give_ref.at[place], pair_sem.at[s]).start()

            sends.append(pltpu.make_async_copy(pair_stage.at[s], keep_ref.at[place], pair_sem.at[s]))

        for s0 in range(0, z.segments, batch):
            group = range(s0, s0 + batch)
            for s in group:
                for copy in copies[s]:
                    copy.wait()
            sources = []
            for n, i in enumerate(steps):
                bufs = (state0, rhs0, -first0) if i == 0 else (state_buf, rhs_buf, i * z.height - first)
                moved = [product(operator, operand_right(read_field(z, bufs[0], (s,), bufs[2]))) for s in group]
                forces = [
                    operand_right(read_field(z, bufs[1], (s,), bufs[2]) + smooth_buf[n, s : s + 1, :] * value)
                    for s, value in zip(group, moved)
                ]
                sources.append(forces)
            for n, i in enumerate(steps):
                sources[n] = [
                    product(operand_left(read_matrix(z, inverse_buf, s * z.steps + i)), force)
                    for s, force in zip(group, sources[n])
                ]
            fields = None
            if has_carry:
                fields = [read_field(z, carry_buf, (s,), (low - 2) * z.height - last) for s in group]
            for n, i in enumerate(steps):
                values = sources[n]
                if i == 0:
                    for s, value in zip(group, values):
                        start_ref[s] = value
                    continue
                if fields is not None:
                    swept = [
                        product(operand_left(read_matrix(z, gain_buf, s * z.steps + i)), operand_right(field))
                        for s, field in zip(group, fields)
                    ]
                    values = [value + more for value, more in zip(values, swept)]
                fields = values
                for s, value in zip(group, values):
                    if n >= rest:
                        write_field(z, pair_stage, (s,), (n - rest) * z.height, value)
                    else:
                        write_field(z, stage, (s,), n * z.height, value)
            for s, value in zip(group, fields):
                if opened:
                    end_ref[s] = value
                copy = pltpu.make_async_copy(stage.at[s], out_ref.at[s], out_sem.at[s])
                copy.start()
                sends.append(copy)
            if paired:
                for s in group:
                    send_pairs(s)
        for copy in sends:
            copy.wait()

    field = f32(z.segments, z.pad, z.cols)
    outs = [f32(z.segments, message, z.ax)] + [f32(pairs, paired_message, z.ax)] * (2 if paired else 0)
    out_specs = [spec_hbm()] * len(outs)
    more = [field] * (2 if opened else 0) + ([f32(1, z.cols)] * 2 if edge_outs else [])
    operands = [me, state, rhs, viscous, inverse, gain, sensors, lefts, rights]
    in_specs = [spec_smem()] + [spec_hbm()] * 5 + [spec_vmem()] * 3
    extra = list(ring) if opened else []
    extra_specs = [spec_vmem()] * len(extra)
    if has_carry:
        extra.append(carry)
        extra_specs.append(spec_hbm())
    scratch = [
        pltpu.VMEM((z.segments, size + z.spill, z.ax), F32),
        pltpu.VMEM((z.segments, size + z.spill, z.ax), F32),
        pltpu.VMEM(inverse.shape, F32),
        pltpu.VMEM(gain.shape, F32),
        pltpu.VMEM(viscous.shape, F32),
        pltpu.VMEM((len(steps), z.segments, z.cols), F32),
        pltpu.VMEM((z.segments, message, z.ax), F32),
        pltpu.SemaphoreType.DMA((z.segments, 7)),
        pltpu.SemaphoreType.DMA((z.segments, 2)),
        pltpu.SemaphoreType.DMA((z.segments,)),
    ]
    if opened:
        scratch += [pltpu.VMEM((z.segments, size0 + z.spill, z.ax), F32)] * 2
    if paired:
        scratch += [pltpu.VMEM((z.segments, paired_message, z.ax), F32), pltpu.SemaphoreType.DMA((z.segments,))]
    if has_carry:
        scratch.append(pltpu.VMEM((z.segments, last_size + z.spill, z.ax), F32))
    return call(
        kernel,
        f"sweep_{low}",
        outs + more,
        in_specs + extra_specs + [spec_any()] * len(after),
        out_specs + [spec_vmem()] * len(more),
        scratch,
        z.flops * len(steps) * z.segments * 3,
        4 * z.segments * size * z.ax * 4,
        limit=54,
    )(*operands, *extra, *after)


def maps_call(z, me, gain, after):
    def kernel(me_ref, gain_ref, *refs):
        own_ref, head_ref, tail_ref, whole_ref, prefix_ref, group_ref, gain_buf, kept, sem = refs[len(after) :]
        copy = pltpu.make_async_copy(gain_ref, gain_buf, sem)
        copy.start()
        copy.wait()

        def times(a, b):
            return product(operand_left(a), operand_right(b))

        values = [read_matrix(z, gain_buf, e * z.steps + 1) for e in range(z.segments)]
        for i in range(1, z.steps):
            if i > 1:
                values = [
                    times(read_matrix(z, gain_buf, e * z.steps + i), values[e]) for e in range(z.segments)
                ]
            for e in range(z.segments):
                kept[e, i] = values[e]
        heads = [read_matrix(z, gain_buf, e * z.steps) for e in range(z.segments)]
        for e in range(z.segments):
            kept[e, 0] = heads[e]
            head_ref[e] = heads[e]
            tail_ref[e] = values[e]
            whole_ref[e] = times(values[e], heads[e])
        own_ref[...] = kept[me_ref[0]]
        value = whole_ref[0]
        prefix_ref[0] = value
        for e in range(1, z.segments):
            prefix_ref[e] = value
            value = times(whole_ref[e], value)
        group_ref[...] = value

    square = (z.pad, z.pad)
    outs = [f32(z.steps, *square)] + [f32(z.segments, *square)] * 4 + [f32(*square)]
    return call(
        kernel,
        "maps",
        outs,
        [spec_smem(), spec_hbm()] + [spec_any()] * len(after),
        [spec_vmem()] * 6,
        [
            pltpu.VMEM(gain.shape, F32),
            pltpu.VMEM((z.segments, z.steps) + square, F32),
            pltpu.SemaphoreType.DMA,
        ],
        z.flops * z.segments * (z.steps + 1) // 2,
        4 * z.segments * z.steps * z.pad * z.pad,
    )(me, gain, *after)


def chain_call(z, starts, ends, tails, wholes, group):
    def kernel(start_ref, end_ref, tail_ref, whole_ref, group_ref, before_ref, pack_ref):
        value = None
        for e in range(z.segments):
            shift = end_ref[e] + product(operand_left(tail_ref[e]), operand_right(start_ref[e]))
            if e > 0:
                before_ref[e] = value
                shift = shift + product(operand_left(whole_ref[e]), operand_right(value))
            else:
                before_ref[0] = jnp.zeros_like(shift)
            value = shift
        pack_ref[:, : z.cols] = value
        pack_ref[:, z.cols :] = group_ref[...]

    return call(
        kernel,
        "chain",
        [f32(z.segments, z.pad, z.cols), f32(z.pad, z.cols + z.pad)],
        [spec_vmem()] * 5,
        [spec_vmem()] * 2,
        [],
        z.flops * z.segments * 2,
        4 * z.segments * z.pad * z.cols * 4,
    )(starts, ends, tails, wholes, group)


def first_call(z, places, packs, before, prefix, heads, starts, messages, place):
    offset = place * z.height
    base = offset // TILE * TILE
    size = messages.shape[1] - base

    def kernel(*refs):
        places_ref, refs = refs[0], refs[1:]
        pack_refs, refs = refs[: z.groups], refs[z.groups :]
        before_ref, prefix_ref, head_ref, start_ref, message_ref, out_ref, stage, sem = refs
        copies = [
            pltpu.make_async_copy(message_ref.at[e, pl.ds(base, size)], stage.at[e], sem.at[e])
            for e in range(z.segments)
        ]
        for copy in copies:
            copy.start()
        group = places_ref[1]
        value = jnp.zeros((z.pad, z.cols), F32)
        matrices = [operand_left(ref[:, z.cols :]) for ref in pack_refs]
        for t in range(2 * z.groups - 1, 0, -1):
            n = t % z.groups
            moved = product(matrices[n], operand_right(value)) + pack_refs[n][:, : z.cols]
            value = jnp.where(t <= z.groups + group, moved, 0.0)
        incoming = operand_right(value)
        arriving = [value] + [
            before_ref[e] + product(operand_left(prefix_ref[e]), incoming) for e in range(1, z.segments)
        ]
        solved = [
            start_ref[e] + product(operand_left(head_ref[e]), operand_right(arriving[e])) for e in range(z.segments)
        ]
        sends = []
        for e in range(z.segments):
            copies[e].wait()
            write_field(z, stage, (e,), offset - base, solved[e])
            copy = pltpu.make_async_copy(stage.at[e], out_ref.at[e, pl.ds(base, size)], sem.at[e])
            copy.start()
            sends.append(copy)
        for copy in sends:
            copy.wait()

    return call(
        kernel,
        "first",
        f32(*messages.shape),
        [spec_smem()] + [spec_vmem()] * (z.groups + 4) + [spec_hbm()],
        spec_hbm(),
        [pltpu.VMEM((z.segments, size, z.ax), F32), pltpu.SemaphoreType.DMA((z.segments,))],
        z.flops * (z.segments * 2 + 2 * z.groups),
        4 * z.segments * z.pad * z.cols * 4,
        {z.groups + 5: 0},
    )(places, *packs, before, prefix, heads, starts, messages)


def couple_call(z, keep, got):
    pairs, message, _ = keep.shape

    def kernel(*refs):
        sources, refs = refs[:2], refs[2:]
        outs, buf, sem = refs[:pairs], refs[pairs], refs[pairs + 1]
        loads = [
            [pltpu.make_async_copy(sources[n].at[d], buf.at[d, n], sem.at[d, n]) for n in range(2)]
            for d in range(pairs)
        ]
        for load in loads:
            for copy in load:
                copy.start()
        stores = []
        for d in range(pairs):
            for copy in loads[d]:
                copy.wait()
            copy = pltpu.make_async_copy(buf.at[d], outs[d], sem.at[d, 0])
            copy.start()
            stores.append(copy)
        for copy in stores:
            copy.wait()

    return call(
        kernel,
        "couple",
        [f32(2, message, z.ax)] * pairs,
        [spec_hbm()] * 2,
        [spec_hbm()] * pairs,
        [pltpu.VMEM((pairs, 2, message, z.ax), F32), pltpu.SemaphoreType.DMA((pairs, 2))],
        0,
        4 * 4 * pairs * message * z.ax,
    )(keep, got)


def gate_call(held, after):
    def kernel(*refs):
        pass

    return call(
        kernel,
        "gate",
        f32(*held.shape),
        [spec_hbm()] + [spec_any()] * len(after),
        spec_hbm(),
        [],
        0,
        0,
        {0: 0},
    )(held, *after)


def open_call(z, one, two, own, received_one, received_two):
    radial = z.segments * z.rows
    tall = z.nodes * radial
    operand_shape = (z.segments, 2 * z.pad, z.cols)
    low, middle, high = one[0], two[0], two[1]
    messages = (received_one, received_two)

    def kernel(own_ref, one_ref, two_ref, out_ref, operand_ref, own_buf, one_buf, two_buf, stage, sem, own_sem, out_sem):
        own_copy = pltpu.make_async_copy(own_ref, own_buf, own_sem)
        own_copy.start()
        copies = []
        for n, (source, target) in enumerate(((two_ref, two_buf), (one_ref, one_buf))):
            copies.append(
                [pltpu.make_async_copy(source.at[e], target.at[e], sem.at[e, n]) for e in range(z.segments)]
            )
            for copy in copies[n]:
                copy.start()
        sends = []

        def put(i, e, value):
            for j in range(z.rows):
                rows = pl.ds(e * z.rows + j, z.nodes, stride=radial)
                stage[i, rows, :] = value[: z.nodes, j * z.ax : (j + 1) * z.ax]

        def send(i):
            copy = pltpu.make_async_copy(stage.at[i], out_ref.at[i], out_sem.at[i])
            copy.start()
            sends.append(copy)

        for e in range(z.segments):
            copies[0][e].wait()
            field = read_exact(z, two_buf, (e,), (high - middle) * z.height)
            empty = jnp.zeros((z.pad - z.nodes, z.cols), F32)
            operand_ref[e] = operand_right(jnp.concatenate([field, empty], axis=0))
            put(0, e, field)
        send(0)
        own_copy.wait()
        for i in list(range(middle, high)) + list(range(low, middle)):
            if i == low:
                for copy in copies[1]:
                    copy.wait()
            buf, offset = (two_buf, i - middle) if i >= middle else (one_buf, i - low)
            matrix = operand_left(own_buf[i])
            for e in range(z.segments):
                value = product(matrix, operand_ref[e])[: z.nodes]
                put(i, e, value + read_exact(z, buf, (e,), offset * z.height))
            send(i)
        for copy in sends:
            copy.wait()

    return call(
        kernel,
        "finish_0",
        [f32(z.steps, tall, z.ax), jax.ShapeDtypeStruct(operand_shape, BF16)],
        [spec_hbm()] * 3,
        [spec_hbm(), spec_vmem()],
        [
            pltpu.VMEM((z.steps, z.pad, z.pad), F32),
            pltpu.VMEM(received_one.shape, F32),
            pltpu.VMEM(received_two.shape, F32),
            pltpu.VMEM((high, tall, z.ax), F32),
            pltpu.SemaphoreType.DMA((z.segments, 2)),
            pltpu.SemaphoreType.DMA,
            pltpu.SemaphoreType.DMA((high,)),
        ],
        z.flops * (high - 1) * z.segments,
        4 * 2 * high * tall * z.ax,
    )(own, *messages)


def finish_call(z, chunk, me, own, messages, operands, out):
    low, high = chunk
    count = high - low
    radial = z.segments * z.rows
    tall = z.nodes * radial
    pairs = z.segments // 2
    paired = len(messages) > 1
    message = messages[0].shape[1]

    def kernel(me_ref, own_ref, operand_ref, *refs):
        message_refs, refs = refs[: len(messages)], refs[len(messages) :]
        _, out_ref, buf, own_buf, operand_buf, stage, sem, in_sem, out_sem = refs
        own_copy = pltpu.make_async_copy(own_ref.at[pl.ds(low, count)], own_buf, in_sem.at[0])
        operand_copy = pltpu.make_async_copy(operand_ref, operand_buf, in_sem.at[1])
        own_copy.start()
        operand_copy.start()
        copies = []
        if paired:
            mine = me_ref[0]
            side = lax.rem(mine, 2)
            for d in range(pairs):
                pair = lax.rem(mine // 2 - d + pairs, pairs) * 2
                for n in range(2):
                    e = pair + (side if n == 0 else 1 - side)
                    copies.append(pltpu.make_async_copy(message_refs[d].at[n], buf.at[e], sem.at[2 * d + n]))
        else:
            copies = [pltpu.make_async_copy(message_refs[0].at[e], buf.at[e], sem.at[e]) for e in range(z.segments)]
        for copy in copies:
            copy.start()
        own_copy.wait()
        operand_copy.wait()
        if paired:
            for copy in copies:
                copy.wait()
        sends = []
        for n in range(count):
            matrix = operand_left(own_buf[n])
            for e in range(z.segments):
                if n == 0 and not paired:
                    copies[e].wait()
                value = product(matrix, operand_buf[e])[: z.nodes] + read_exact(z, buf, (e,), n * z.height)
                for j in range(z.rows):
                    rows = pl.ds(e * z.rows + j, z.nodes, stride=radial)
                    stage[n, rows, :] = value[:, j * z.ax : (j + 1) * z.ax]
            copy = pltpu.make_async_copy(stage.at[n], out_ref.at[low + n], out_sem.at[n])
            copy.start()
            sends.append(copy)
        for copy in sends:
            copy.wait()

    inputs = [me, own, operands] + list(messages) + [out]
    return call(
        kernel,
        f"finish_{low}",
        f32(z.steps, tall, z.ax),
        [spec_smem()] + [spec_hbm()] * (len(inputs) - 1),
        spec_hbm(),
        [
            pltpu.VMEM((z.segments, message, z.ax), F32),
            pltpu.VMEM((count, z.pad, z.pad), F32),
            pltpu.VMEM(operands.shape, BF16),
            pltpu.VMEM((count, tall, z.ax), F32),
            pltpu.SemaphoreType.DMA((z.segments,)),
            pltpu.SemaphoreType.DMA((2,)),
            pltpu.SemaphoreType.DMA((count,)),
        ],
        z.flops * count * z.segments,
        4 * 2 * count * tall * z.ax,
        {len(inputs) - 1: 0},
    )(*inputs)


def shift_by(array, axis, by):
    size = lax.axis_size(axis)
    return lax.ppermute(array, axis, [(i, (i + by) % size) for i in range(size)])


def neighbours(head, tail):
    size = lax.axis_size("elem")
    left = lax.ppermute(tail, "elem", [(i, i + 1) for i in range(size - 1)])
    right = lax.ppermute(head, "elem", [(i + 1, i) for i in range(size - 1)])
    return left, right


def spread(messages):
    return lax.all_to_all(messages, "elem", 0, 0, tiled=True)


def chunks_of(steps):
    if steps >= 8:
        return (1, 4), (4, steps), 1
    return (1, 2), (2, steps), 1


def body(state, rhs, to_modal, viscous_op, sweep_gain, inv_blocks):
    segments = lax.axis_size("elem")
    groups = lax.axis_size("blk")
    z = Sizes(state, segments, groups)
    state = state.reshape(segments, z.steps * z.height, z.ax)
    rhs = rhs.reshape(segments, z.steps * z.height, z.ax)
    gain = jnp.transpose(sweep_gain, (1, 0, 2))
    inverse = jnp.transpose(inv_blocks, (1, 0, 2))
    here = lax.axis_index("elem").astype(jnp.int32)
    me = here.reshape(1)
    places = jnp.stack([here, lax.axis_index("blk").astype(jnp.int32)])
    one, two, paired = chunks_of(z.steps)
    sensors, head, tail = sensor_call(z, state, to_modal)
    lefts, rights = neighbours(head, tail)

    def sweep(chunk, paired, ring, carry, after):
        return sweep_call(
            z, chunk, paired, me, state, rhs, viscous_op, gain, inverse, sensors, lefts, rights, ring, carry, after
        )

    messages_one, low, high = sweep(one, 0, None, None, [])
    ring = [shift_by(high, "blk", 1), shift_by(low, "blk", -1)]
    own, heads, tails, wholes, prefix, group = maps_call(z, me, gain, [messages_one])
    messages_two, keep, give, ends, starts = sweep(two, paired, ring, messages_one, [group])
    before, pack = chain_call(z, starts, ends, tails, wholes, group)
    packs = [pack] + [shift_by(pack, "blk", s) for s in range(1, groups)]
    middle = two[1] - paired
    messages_two = first_call(z, places, packs, before, prefix, heads, starts, messages_two, middle - two[0])
    got = lax.ppermute(give, "elem", [(i, i ^ 1) for i in range(segments)])
    coupled = couple_call(z, keep, got)
    coupled = [coupled[0]] + [shift_by(coupled[d], "elem", 2 * d) for d in range(1, segments // 2)]
    received_one = spread(messages_one)
    received_two = spread(gate_call(messages_two, [received_one, coupled[0]]))
    out, operands = open_call(z, one, (two[0], middle), own, received_one, received_two)
    out = finish_call(z, (middle, two[1]), me, own, coupled, operands, out)
    return out.reshape(z.steps, z.nodes, segments * z.rows, z.ax)


def solution(mesh):
    in_specs = (
        P("blk", None, "elem", None),
        P("blk", None, "elem", None),
        P(),
        P(),
        P("blk", None, None),
        P("blk", None, None),
    )
    out_specs = P(("blk", "elem"), None, None, None)
    return jax.shard_map(body, mesh=mesh, in_specs=in_specs, out_specs=out_specs, check_vma=False)
```

```python
import functools

import jax
import jax.numpy as jnp
from jax import lax
from jax.experimental import pallas as pl
from jax.experimental.pallas import tpu as pltpu
from jax.sharding import PartitionSpec as P

ORDER = 4
F32 = jnp.float32
BF16 = jnp.bfloat16
MIB = 1024 * 1024
TILE = 8
LANES = 128


def operand_left(a):
    high = a.astype(BF16)
    low = (a - high.astype(F32)).astype(BF16)
    return jnp.concatenate([jnp.concatenate([high, high], axis=1), jnp.concatenate([low, low], axis=1)], axis=0)


def operand_right(x):
    high = x.astype(BF16)
    return jnp.concatenate([high, (x - high.astype(F32)).astype(BF16)], axis=0)


def product(left, right):
    both = jnp.dot(left, right, preferred_element_type=F32)
    half = left.shape[0] // 2
    return both[:half] + both[half:]


def spec_any():
    return pl.BlockSpec(memory_space=pl.ANY)


def spec_hbm():
    return pl.BlockSpec(memory_space=pltpu.HBM)


def spec_vmem():
    return pl.BlockSpec(memory_space=pltpu.VMEM)


def spec_smem():
    return pl.BlockSpec(memory_space=pltpu.SMEM)


def call(kernel, name, outs, in_specs, out_specs, scratch, flops, nbytes, aliases=None, limit=57):
    return pl.pallas_call(
        kernel,
        name=name,
        out_shape=outs,
        in_specs=in_specs,
        out_specs=out_specs,
        scratch_shapes=scratch,
        input_output_aliases=aliases or {},
        compiler_params=pltpu.CompilerParams(vmem_limit_bytes=limit * MIB),
        cost_estimate=pl.CostEstimate(flops=int(flops), bytes_accessed=int(nbytes), transcendentals=0),
    )


def f32(*shape):
    return jax.ShapeDtypeStruct(shape, F32)


def up(value, unit):
    return -(-value // unit) * unit


class Sizes:
    def __init__(self, state, segments, groups):
        count, self.nodes, self.rows, self.ax = state.shape
        self.count = count
        self.segments = segments
        self.groups = groups
        self.steps = count // segments
        self.cols = self.rows * self.ax
        self.height = self.nodes * self.rows
        self.pad = up(self.nodes, LANES)
        self.spill = up((self.pad - self.nodes) * self.rows, TILE)
        self.flops = 2 * 4 * self.pad * self.pad * self.cols

    def window(self, low, high):
        first = low * self.height // TILE * TILE
        return first, up(high * self.height, TILE) - first

    def message(self, count):
        return up(count * self.height, TILE)

    def rows_masked(self, x):
        cut = self.nodes // TILE * TILE
        rest = x[cut:]
        inside = lax.broadcasted_iota(jnp.int32, rest.shape, 0) < self.nodes - cut
        return jnp.concatenate([x[:cut], jnp.where(inside, rest, 0.0)], axis=0)

    def square(self, x):
        x = jnp.concatenate([x, jnp.zeros((self.nodes, self.pad - self.nodes), F32)], axis=1)
        return jnp.concatenate([x, jnp.zeros((self.pad - self.nodes, self.pad), F32)], axis=0)


def read_field(z, ref, lead, offset):
    parts = [ref[lead + (pl.ds(offset + j, z.pad, stride=z.rows), slice(None))] for j in range(z.rows)]
    return z.rows_masked(jnp.concatenate(parts, axis=1))


def read_exact(z, ref, lead, offset):
    parts = [ref[lead + (pl.ds(offset + j, z.nodes, stride=z.rows), slice(None))] for j in range(z.rows)]
    return jnp.concatenate(parts, axis=1)


def write_field(z, ref, lead, offset, value):
    for j in range(z.rows):
        rows = pl.ds(offset + j, z.nodes, stride=z.rows)
        ref[lead + (rows, slice(None))] = value[: z.nodes, j * z.ax : (j + 1) * z.ax]


def read_matrix(z, ref, k):
    return z.square(ref[:, k, :])


def send_pair(z, mine, e, stage, keep_ref, give_ref, sem):
    pairs = z.segments // 2
    place = lax.rem(e // 2 - mine // 2 + pairs, pairs)
    own = lax.rem(mine, 2) == e % 2

    @pl.when(own)
    def _():
        pltpu.make_async_copy(stage.at[e], keep_ref.at[place], sem.at[e]).start()

    @pl.when(jnp.logical_not(own))
    def _():
        pltpu.make_async_copy(stage.at[e], give_ref.at[place], sem.at[e]).start()

    return pltpu.make_async_copy(stage.at[e], keep_ref.at[place], sem.at[e])


def load_pairs(z, mine, sources, buf, sem):
    pairs = z.segments // 2
    side = lax.rem(mine, 2)
    copies = []
    for d in range(pairs):
        pair = lax.rem(mine // 2 - d + pairs, pairs) * 2
        for n in range(2):
            e = pair + (side if n == 0 else 1 - side)
            copies.append(pltpu.make_async_copy(sources[d].at[n], buf.at[e], sem.at[2 * d + n]))
    return copies


def sensor_call(z, state, to_modal):
    batch = 4 if z.segments % 4 == 0 else 1
    tall = z.steps * z.height

    def kernel(state_ref, modal_ref, sensor_ref, head_ref, tail_ref, buf, modal_buf, sem, modal_sem):
        modal_copy = pltpu.make_async_copy(modal_ref, modal_buf, modal_sem)
        modal_copy.start()
        copies = [
            pltpu.make_async_copy(state_ref.at[e], buf.at[e, pl.ds(0, tall)], sem.at[e]) for e in range(z.segments)
        ]
        for copy in copies:
            copy.start()
        modal_copy.wait()
        matrix = operand_left(z.square(modal_buf[...]))
        for e0 in range(0, z.segments, batch):
            for e in range(e0, e0 + batch):
                copies[e].wait()
            for e in range(e0, e0 + batch):
                for i in range(z.steps):
                    modal = product(matrix, operand_right(read_field(z, buf, (e,), i * z.height)))
                    squares = modal * modal
                    lower = jnp.sum(squares[: ORDER**3], axis=0, keepdims=True)
                    upper = jnp.sum(squares[ORDER**3 :], axis=0, keepdims=True)
                    sensor = (upper / z.nodes) / ((lower + upper) / z.nodes + 1e-6)
                    sensor_ref[i, e : e + 1, :] = sensor
                    head_ref[i, e : e + 1, :] = sensor[:, : z.ax]
                    tail_ref[i, e : e + 1, :] = sensor[:, z.cols - z.ax :]

    outs = [f32(z.steps, z.segments, z.cols)] + [f32(z.steps, z.segments, z.ax)] * 2
    return call(
        kernel,
        "sensor",
        outs,
        [spec_hbm()] * 2,
        [spec_vmem()] * 3,
        [
            pltpu.VMEM((z.segments, tall + z.spill, z.ax), F32),
            pltpu.VMEM((z.nodes, z.nodes), F32),
            pltpu.SemaphoreType.DMA((z.segments,)),
            pltpu.SemaphoreType.DMA,
        ],
        z.flops * z.steps * z.segments,
        4 * z.segments * tall * z.ax,
        limit=57,
    )(state, to_modal)


def smoothed(z, sensor, before, after, left, right):
    inner = sensor[:, : z.cols - z.ax]
    outer = sensor[:, z.ax :]
    from_left = jnp.concatenate([left, inner], axis=1)
    from_right = jnp.concatenate([outer, right], axis=1)
    return (4.0 * sensor + before + after + from_left + from_right) / 8.0


def sweep_call(z, chunk, parts, me, state, rhs, viscous, gain, inverse, sensors, lefts, rights, ring, carry, after):
    low, high = chunk
    opened = high == z.steps
    first, size = z.window(low, high)
    count = high - low
    first0, size0 = z.window(0, 1)
    steps = list(range(low, high)) + ([0] if opened else [])
    has_carry = carry is not None
    gains = list(range(low if has_carry else low + 1, high))
    messages = [z.message(stop - start) for start, stop in parts or [chunk]]
    edge_outs = low == 1
    pairs = z.segments // 2
    last, last_size = z.window(low - 2, low - 1)
    batch = next(n for n in (4, 8, z.segments) if z.segments % n == 0 and n * z.steps % TILE == 0)
    narrow = low == 1

    if parts:
        outs = [f32(pairs, message, z.ax) for message in messages for _ in range(2)]
    else:
        outs = [f32(z.segments, messages[0], z.ax)]

    def kernel(*refs):
        me_ref, state_ref, rhs_ref, viscous_ref, inverse_ref, gain_ref, sensor_ref, left_ref, right_ref = refs[:9]
        refs = refs[9:]
        if opened:
            before_ref, behind_ref, refs = refs[0], refs[1], refs[2:]
        if has_carry:
            carry_ref, refs = refs[0], refs[1:]
        refs = refs[len(after) :]
        out_refs, refs = refs[: len(outs)], refs[len(outs) :]
        if opened:
            end_ref, start_ref, refs = refs[0], refs[1], refs[2:]
        if edge_outs:
            low_ref, high_ref, refs = refs[0], refs[1], refs[2:]
        state_buf, rhs_buf, inverse_buf, gain_buf, viscous_buf, smooth_buf, sem, matrix_sem, out_sem = refs[:9]
        stages, refs = refs[9 : 9 + len(messages)], refs[9 + len(messages) :]
        if opened:
            state0, rhs0, refs = refs[0], refs[1], refs[2:]
        if has_carry:
            carry_buf = refs[0]
        viscous_copy = pltpu.make_async_copy(viscous_ref, viscous_buf, out_sem.at[0, 0])
        viscous_copy.start()
        copies = [[] for _ in range(z.segments)]
        for s0 in range(0, z.segments, batch):
            for s in range(s0, s0 + batch):
                moves = [
                    (state_ref.at[s, pl.ds(first, size)], state_buf.at[s, pl.ds(0, size)]),
                    (rhs_ref.at[s, pl.ds(first, size)], rhs_buf.at[s, pl.ds(0, size)]),
                ]
                if opened:
                    moves.append((state_ref.at[s, pl.ds(first0, size0)], state0.at[s, pl.ds(0, size0)]))
                    moves.append((rhs_ref.at[s, pl.ds(first0, size0)], rhs0.at[s, pl.ds(0, size0)]))
                if has_carry:
                    moves.append((carry_ref.at[s, pl.ds(last, last_size)], carry_buf.at[s, pl.ds(0, last_size)]))
                if narrow:
                    for source, target, needed in ((inverse_ref, inverse_buf, steps), (gain_ref, gain_buf, gains)):
                        if needed:
                            part = pl.ds(s * z.steps + needed[0], len(needed))
                            moves.append((source.at[:, part], target.at[:, part]))
                for n, (source, target) in enumerate(moves):
                    copies[s].append(pltpu.make_async_copy(source, target, sem.at[s, n]))
            if not narrow:
                part = pl.ds(s0 * z.steps, batch * z.steps)
                for n, (source, target) in enumerate(((inverse_ref, inverse_buf), (gain_ref, gain_buf))):
                    copy = pltpu.make_async_copy(source.at[:, part], target.at[:, part], matrix_sem.at[s0, n])
                    copies[s0].append(copy)
            for s in range(s0, s0 + batch):
                for copy in copies[s]:
                    copy.start()
        for n, i in enumerate(steps):
            before = sensor_ref[(i - 1) % z.steps]
            later = sensor_ref[(i + 1) % z.steps]
            if i == 0:
                before = jnp.concatenate([before_ref[...], before[: z.segments - 1]], axis=0)
            if i == z.steps - 1:
                later = jnp.concatenate([later[1:], behind_ref[...]], axis=0)
            smooth_buf[n] = smoothed(z, sensor_ref[i], before, later, left_ref[i], right_ref[i])
        if edge_outs:
            low_ref[...] = sensor_ref[0, :1]
            high_ref[...] = sensor_ref[z.steps - 1, z.segments - 1 :]
        viscous_copy.wait()
        operator = operand_left(z.square(viscous_buf[...]))
        sends = []

        for s0 in range(0, z.segments, batch):
            group = range(s0, s0 + batch)
            for s in group:
                for copy in copies[s]:
                    copy.wait()
            sources = []
            for n, i in enumerate(steps):
                bufs = (state0, rhs0, -first0) if i == 0 else (state_buf, rhs_buf, i * z.height - first)
                moved = [product(operator, operand_right(read_field(z, bufs[0], (s,), bufs[2]))) for s in group]
                forces = [
                    operand_right(read_field(z, bufs[1], (s,), bufs[2]) + smooth_buf[n, s : s + 1, :] * value)
                    for s, value in zip(group, moved)
                ]
                sources.append(forces)
            for n, i in enumerate(steps):
                sources[n] = [
                    product(operand_left(read_matrix(z, inverse_buf, s * z.steps + i)), force)
                    for s, force in zip(group, sources[n])
                ]
            fields = None
            if has_carry:
                fields = [read_field(z, carry_buf, (s,), (low - 2) * z.height - last) for s in group]
            for n, i in enumerate(steps):
                values = sources[n]
                if i == 0:
                    for s, value in zip(group, values):
                        start_ref[s] = value
                    continue
                if fields is not None:
                    swept = [
                        product(operand_left(read_matrix(z, gain_buf, s * z.steps + i)), operand_right(field))
                        for s, field in zip(group, fields)
                    ]
                    values = [value + more for value, more in zip(values, swept)]
                fields = values
                for s, value in zip(group, values):
                    for (start, stop), stage in zip(parts or [chunk], stages):
                        if start <= i < stop:
                            write_field(z, stage, (s,), (i - start) * z.height, value)
            for s, value in zip(group, fields):
                if opened:
                    end_ref[s] = value
                if not parts:
                    copy = pltpu.make_async_copy(stages[0].at[s], out_refs[0].at[s], out_sem.at[0, s])
                    copy.start()
                    sends.append(copy)
            for p, stage in enumerate(stages if parts else []):
                for s in group:
                    keep_ref, give_ref = out_refs[2 * p], out_refs[2 * p + 1]
                    sends.append(send_pair(z, me_ref[0], s, stage, keep_ref, give_ref, out_sem.at[p]))
        for copy in sends:
            copy.wait()

    field = f32(z.segments, z.pad, z.cols)
    out_specs = [spec_hbm()] * len(outs)
    more = [field] * (2 if opened else 0) + ([f32(1, z.cols)] * 2 if edge_outs else [])
    operands = [me, state, rhs, viscous, inverse, gain, sensors, lefts, rights]
    in_specs = [spec_smem()] + [spec_hbm()] * 5 + [spec_vmem()] * 3
    extra = list(ring) if opened else []
    extra_specs = [spec_vmem()] * len(extra)
    if has_carry:
        extra.append(carry)
        extra_specs.append(spec_hbm())
    scratch = [
        pltpu.VMEM((z.segments, size + z.spill, z.ax), F32),
        pltpu.VMEM((z.segments, size + z.spill, z.ax), F32),
        pltpu.VMEM(inverse.shape, F32),
        pltpu.VMEM(gain.shape, F32),
        pltpu.VMEM(viscous.shape, F32),
        pltpu.VMEM((len(steps), z.segments, z.cols), F32),
        pltpu.SemaphoreType.DMA((z.segments, 7)),
        pltpu.SemaphoreType.DMA((z.segments, 2)),
        pltpu.SemaphoreType.DMA((len(messages), z.segments)),
    ]
    scratch += [pltpu.VMEM((z.segments, message, z.ax), F32) for message in messages]
    if opened:
        scratch += [pltpu.VMEM((z.segments, size0 + z.spill, z.ax), F32)] * 2
    if has_carry:
        scratch.append(pltpu.VMEM((z.segments, last_size + z.spill, z.ax), F32))
    return call(
        kernel,
        f"sweep_{low}",
        outs + more,
        in_specs + extra_specs + [spec_any()] * len(after),
        out_specs + [spec_vmem()] * len(more),
        scratch,
        z.flops * len(steps) * z.segments * 3,
        4 * z.segments * size * z.ax * 4,
        limit=54,
    )(*operands, *extra, *after)


def maps_call(z, me, gain, after):
    def kernel(me_ref, gain_ref, *refs):
        own_ref, head_ref, tail_ref, whole_ref, prefix_ref, group_ref, gain_buf, kept, sem = refs[len(after) :]
        copy = pltpu.make_async_copy(gain_ref, gain_buf, sem)
        copy.start()
        copy.wait()

        def times(a, b):
            return product(operand_left(a), operand_right(b))

        values = [read_matrix(z, gain_buf, e * z.steps + 1) for e in range(z.segments)]
        for i in range(1, z.steps):
            if i > 1:
                values = [
                    times(read_matrix(z, gain_buf, e * z.steps + i), values[e]) for e in range(z.segments)
                ]
            for e in range(z.segments):
                kept[e, i] = values[e]
        heads = [read_matrix(z, gain_buf, e * z.steps) for e in range(z.segments)]
        for e in range(z.segments):
            kept[e, 0] = heads[e]
            head_ref[e] = heads[e]
            tail_ref[e] = values[e]
            whole_ref[e] = times(values[e], heads[e])
        own_ref[...] = kept[me_ref[0]]
        value = whole_ref[0]
        prefix_ref[0] = value
        for e in range(1, z.segments):
            prefix_ref[e] = value
            value = times(whole_ref[e], value)
        group_ref[...] = value

    square = (z.pad, z.pad)
    outs = [f32(z.steps, *square)] + [f32(z.segments, *square)] * 4 + [f32(*square)]
    return call(
        kernel,
        "maps",
        outs,
        [spec_smem(), spec_hbm()] + [spec_any()] * len(after),
        [spec_vmem()] * 6,
        [
            pltpu.VMEM(gain.shape, F32),
            pltpu.VMEM((z.segments, z.steps) + square, F32),
            pltpu.SemaphoreType.DMA,
        ],
        z.flops * z.segments * (z.steps + 1) // 2,
        4 * z.segments * z.steps * z.pad * z.pad,
    )(me, gain, *after)


def chain_call(z, starts, ends, tails, wholes, group):
    def kernel(start_ref, end_ref, tail_ref, whole_ref, group_ref, before_ref, pack_ref):
        value = None
        for e in range(z.segments):
            shift = end_ref[e] + product(operand_left(tail_ref[e]), operand_right(start_ref[e]))
            if e > 0:
                before_ref[e] = value
                shift = shift + product(operand_left(whole_ref[e]), operand_right(value))
            else:
                before_ref[0] = jnp.zeros_like(shift)
            value = shift
        pack_ref[:, : z.cols] = value
        pack_ref[:, z.cols :] = group_ref[...]

    return call(
        kernel,
        "chain",
        [f32(z.segments, z.pad, z.cols), f32(z.pad, z.cols + z.pad)],
        [spec_vmem()] * 5,
        [spec_vmem()] * 2,
        [],
        z.flops * z.segments * 2,
        4 * z.segments * z.pad * z.cols * 4,
    )(starts, ends, tails, wholes, group)


def first_call(z, places, packs, before, prefix, heads, starts):
    rows = z.message(1)
    pairs = z.segments // 2

    def kernel(*refs):
        places_ref, refs = refs[0], refs[1:]
        pack_refs, refs = refs[: z.groups], refs[z.groups :]
        before_ref, prefix_ref, head_ref, start_ref, keep_ref, give_ref, stage, sem = refs
        mine = places_ref[0]
        group = places_ref[1]
        value = jnp.zeros((z.pad, z.cols), F32)
        matrices = [operand_left(ref[:, z.cols :]) for ref in pack_refs]
        for t in range(2 * z.groups - 1, 0, -1):
            n = t % z.groups
            moved = product(matrices[n], operand_right(value)) + pack_refs[n][:, : z.cols]
            value = jnp.where(t <= z.groups + group, moved, 0.0)
        incoming = operand_right(value)
        arriving = [value] + [
            before_ref[e] + product(operand_left(prefix_ref[e]), incoming) for e in range(1, z.segments)
        ]
        solved = [
            start_ref[e] + product(operand_left(head_ref[e]), operand_right(arriving[e])) for e in range(z.segments)
        ]
        for e in range(z.segments):
            write_field(z, stage, (e,), 0, solved[e])
        sends = [send_pair(z, mine, e, stage, keep_ref, give_ref, sem) for e in range(z.segments)]
        for copy in sends:
            copy.wait()

    return call(
        kernel,
        "first",
        [f32(pairs, rows, z.ax)] * 2,
        [spec_smem()] + [spec_vmem()] * (z.groups + 4),
        [spec_hbm()] * 2,
        [pltpu.VMEM((z.segments, rows, z.ax), F32), pltpu.SemaphoreType.DMA((z.segments,))],
        z.flops * (z.segments * 2 + 2 * z.groups),
        4 * z.segments * z.pad * z.cols * 4,
    )(places, *packs, before, prefix, heads, starts)


def couple_call(z, keep, got):
    pairs, message, _ = keep.shape

    def kernel(*refs):
        sources, refs = refs[:2], refs[2:]
        outs, buf, sem = refs[:pairs], refs[pairs], refs[pairs + 1]
        loads = [
            [pltpu.make_async_copy(sources[n].at[d], buf.at[d, n], sem.at[d, n]) for n in range(2)]
            for d in range(pairs)
        ]
        for load in loads:
            for copy in load:
                copy.start()
        stores = []
        for d in range(pairs):
            for copy in loads[d]:
                copy.wait()
            copy = pltpu.make_async_copy(buf.at[d], outs[d], sem.at[d, 0])
            copy.start()
            stores.append(copy)
        for copy in stores:
            copy.wait()

    return call(
        kernel,
        "couple",
        [f32(2, message, z.ax)] * pairs,
        [spec_hbm()] * 2,
        [spec_hbm()] * pairs,
        [pltpu.VMEM((pairs, 2, message, z.ax), F32), pltpu.SemaphoreType.DMA((pairs, 2))],
        0,
        4 * 4 * pairs * message * z.ax,
    )(keep, got)


def gate_call(held, after):
    def kernel(*refs):
        pass

    return call(
        kernel,
        "gate",
        [f32(*array.shape) for array in held],
        [spec_hbm()] * len(held) + [spec_any()] * len(after),
        [spec_hbm()] * len(held),
        [],
        0,
        0,
        {n: n for n in range(len(held))},
    )(*held, *after)


def open_call(z, one, me, own, received_one, received_first):
    radial = z.segments * z.rows
    tall = z.nodes * radial
    operand_shape = (z.segments, 2 * z.pad, z.cols)
    low, high = one
    pairs = z.segments // 2
    message = received_first[0].shape[1]

    def kernel(me_ref, own_ref, one_ref, *refs):
        first_refs, refs = refs[:pairs], refs[pairs:]
        out_ref, operand_ref, own_buf, one_buf, first_buf, stage, one_sem, first_sem, own_sem, out_sem = refs
        first_copies = load_pairs(z, me_ref[0], first_refs, first_buf, first_sem)
        one_copies = [pltpu.make_async_copy(one_ref.at[e], one_buf.at[e], one_sem.at[e]) for e in range(z.segments)]
        own_copy = pltpu.make_async_copy(own_ref, own_buf, own_sem)
        for copy in first_copies + [own_copy] + one_copies:
            copy.start()
        for copy in first_copies:
            copy.wait()
        sends = []

        def put(i, e, value):
            for j in range(z.rows):
                rows = pl.ds(e * z.rows + j, z.nodes, stride=radial)
                stage[i, rows, :] = value[: z.nodes, j * z.ax : (j + 1) * z.ax]

        def send(i):
            copy = pltpu.make_async_copy(stage.at[i], out_ref.at[i], out_sem.at[i])
            copy.start()
            sends.append(copy)

        for e in range(z.segments):
            field = read_exact(z, first_buf, (e,), 0)
            empty = jnp.zeros((z.pad - z.nodes, z.cols), F32)
            operand_ref[e] = operand_right(jnp.concatenate([field, empty], axis=0))
            put(0, e, field)
        send(0)
        own_copy.wait()
        for copy in one_copies:
            copy.wait()
        for i in range(low, high):
            matrix = operand_left(own_buf[i])
            for e in range(z.segments):
                value = product(matrix, operand_ref[e])[: z.nodes]
                put(i, e, value + read_exact(z, one_buf, (e,), (i - low) * z.height))
            send(i)
        for copy in sends:
            copy.wait()

    return call(
        kernel,
        "finish_0",
        [f32(z.steps, tall, z.ax), jax.ShapeDtypeStruct(operand_shape, BF16)],
        [spec_smem()] + [spec_hbm()] * (2 + pairs),
        [spec_hbm(), spec_vmem()],
        [
            pltpu.VMEM((z.steps, z.pad, z.pad), F32),
            pltpu.VMEM(received_one.shape, F32),
            pltpu.VMEM((z.segments, message, z.ax), F32),
            pltpu.VMEM((high, tall, z.ax), F32),
            pltpu.SemaphoreType.DMA((z.segments,)),
            pltpu.SemaphoreType.DMA((z.segments,)),
            pltpu.SemaphoreType.DMA,
            pltpu.SemaphoreType.DMA((high,)),
        ],
        z.flops * (high - 1) * z.segments,
        4 * 2 * high * tall * z.ax,
    )(me, own, received_one, *received_first)


def finish_call(z, chunk, me, own, messages, operands, out):
    low, high = chunk
    count = high - low
    radial = z.segments * z.rows
    tall = z.nodes * radial
    message = messages[0].shape[1]

    def kernel(me_ref, own_ref, operand_ref, *refs):
        message_refs, refs = refs[: len(messages)], refs[len(messages) :]
        _, out_ref, buf, own_buf, operand_buf, stage, sem, in_sem, out_sem = refs
        own_copy = pltpu.make_async_copy(own_ref.at[pl.ds(low, count)], own_buf, in_sem.at[0])
        operand_copy = pltpu.make_async_copy(operand_ref, operand_buf, in_sem.at[1])
        own_copy.start()
        operand_copy.start()
        copies = load_pairs(z, me_ref[0], message_refs, buf, sem)
        for copy in copies:
            copy.start()
        own_copy.wait()
        operand_copy.wait()
        for copy in copies:
            copy.wait()
        sends = []
        for n in range(count):
            matrix = operand_left(own_buf[n])
            for e in range(z.segments):
                value = product(matrix, operand_buf[e])[: z.nodes] + read_exact(z, buf, (e,), n * z.height)
                for j in range(z.rows):
                    rows = pl.ds(e * z.rows + j, z.nodes, stride=radial)
                    stage[n, rows, :] = value[:, j * z.ax : (j + 1) * z.ax]
            copy = pltpu.make_async_copy(stage.at[n], out_ref.at[low + n], out_sem.at[n])
            copy.start()
            sends.append(copy)
        for copy in sends:
            copy.wait()

    inputs = [me, own, operands] + list(messages) + [out]
    return call(
        kernel,
        f"finish_{low}",
        f32(z.steps, tall, z.ax),
        [spec_smem()] + [spec_hbm()] * (len(inputs) - 1),
        spec_hbm(),
        [
            pltpu.VMEM((z.segments, message, z.ax), F32),
            pltpu.VMEM((count, z.pad, z.pad), F32),
            pltpu.VMEM(operands.shape, BF16),
            pltpu.VMEM((count, tall, z.ax), F32),
            pltpu.SemaphoreType.DMA((z.segments,)),
            pltpu.SemaphoreType.DMA((2,)),
            pltpu.SemaphoreType.DMA((count,)),
        ],
        z.flops * count * z.segments,
        4 * 2 * count * tall * z.ax,
        {len(inputs) - 1: 0},
    )(*inputs)


def shift_by(array, axis, by):
    size = lax.axis_size(axis)
    return lax.ppermute(array, axis, [(i, (i + by) % size) for i in range(size)])


def neighbours(head, tail):
    size = lax.axis_size("elem")
    left = lax.ppermute(tail, "elem", [(i, i + 1) for i in range(size - 1)])
    right = lax.ppermute(head, "elem", [(i + 1, i) for i in range(size - 1)])
    return left, right


def spread(messages):
    return lax.all_to_all(messages, "elem", 0, 0, tiled=True)


def spread_pairs(z, keep, give, after):
    got = lax.ppermute(give, "elem", [(i, i ^ 1) for i in range(z.segments)])
    coupled = couple_call(z, keep, got)
    if after:
        coupled = gate_call(coupled, after)
    return [coupled[0]] + [shift_by(coupled[d], "elem", 2 * d) for d in range(1, z.segments // 2)]


def chunks_of(steps):
    middle = 4 if steps >= 8 else 2
    last = steps - 1
    parts = [(middle, last), (last, steps)] if last > middle else [(middle, steps)]
    return (1, middle), (middle, steps), parts


def body(state, rhs, to_modal, viscous_op, sweep_gain, inv_blocks):
    segments = lax.axis_size("elem")
    groups = lax.axis_size("blk")
    z = Sizes(state, segments, groups)
    state = state.reshape(segments, z.steps * z.height, z.ax)
    rhs = rhs.reshape(segments, z.steps * z.height, z.ax)
    gain = jnp.transpose(sweep_gain, (1, 0, 2))
    inverse = jnp.transpose(inv_blocks, (1, 0, 2))
    here = lax.axis_index("elem").astype(jnp.int32)
    me = here.reshape(1)
    places = jnp.stack([here, lax.axis_index("blk").astype(jnp.int32)])
    one, two, parts = chunks_of(z.steps)
    sensors, head, tail = sensor_call(z, state, to_modal)
    lefts, rights = neighbours(head, tail)

    def sweep(chunk, parts, ring, carry, after):
        return sweep_call(
            z, chunk, parts, me, state, rhs, viscous_op, gain, inverse, sensors, lefts, rights, ring, carry, after
        )

    messages_one, low, high = sweep(one, [], None, None, [])
    ring = [shift_by(high, "blk", 1), shift_by(low, "blk", -1)]
    own, heads, tails, wholes, prefix, group = maps_call(z, me, gain, [messages_one])
    *pairs, ends, starts = sweep(two, parts, ring, messages_one, [group])
    before, pack = chain_call(z, starts, ends, tails, wholes, group)
    packs = [pack] + [shift_by(pack, "blk", s) for s in range(1, groups)]
    keep_first, give_first = first_call(z, places, packs, before, prefix, heads, starts)
    received_one = spread(messages_one)
    received_first = spread_pairs(z, keep_first, give_first, [])
    out, operands = open_call(z, one, me, own, received_one, received_first)
    after = received_first[1:]
    for n, part in enumerate(parts):
        received = spread_pairs(z, pairs[2 * n], pairs[2 * n + 1], after)
        out = finish_call(z, part, me, own, received, operands, out)
        after = received[1:2]
    return out.reshape(z.steps, z.nodes, segments * z.rows, z.ax)


def solution(mesh):
    in_specs = (
        P("blk", None, "elem", None),
        P("blk", None, "elem", None),
        P(),
        P(),
        P("blk", None, None),
        P("blk", None, None),
    )
    out_specs = P(("blk", "elem"), None, None, None)
    return jax.shard_map(body, mesh=mesh, in_specs=in_specs, out_specs=out_specs, check_vma=False)
```

```python
import functools

import jax
import jax.numpy as jnp
from jax import lax
from jax.experimental import pallas as pl
from jax.experimental.pallas import tpu as pltpu
from jax.sharding import PartitionSpec as P

ORDER = 4
F32 = jnp.float32
BF16 = jnp.bfloat16
MIB = 1024 * 1024
TILE = 8
LANES = 128


def operand_left(a):
    high = a.astype(BF16)
    low = (a - high.astype(F32)).astype(BF16)
    return jnp.concatenate([jnp.concatenate([high, high], axis=1), jnp.concatenate([low, low], axis=1)], axis=0)


def operand_right(x):
    high = x.astype(BF16)
    return jnp.concatenate([high, (x - high.astype(F32)).astype(BF16)], axis=0)


def product(left, right):
    both = jnp.dot(left, right, preferred_element_type=F32)
    half = left.shape[0] // 2
    return both[:half] + both[half:]


def spec_any():
    return pl.BlockSpec(memory_space=pl.ANY)


def spec_hbm():
    return pl.BlockSpec(memory_space=pltpu.HBM)


def spec_vmem():
    return pl.BlockSpec(memory_space=pltpu.VMEM)


def spec_smem():
    return pl.BlockSpec(memory_space=pltpu.SMEM)


def call(kernel, name, outs, in_specs, out_specs, scratch, flops, nbytes, aliases=None, limit=57):
    return pl.pallas_call(
        kernel,
        name=name,
        out_shape=outs,
        in_specs=in_specs,
        out_specs=out_specs,
        scratch_shapes=scratch,
        input_output_aliases=aliases or {},
        compiler_params=pltpu.CompilerParams(vmem_limit_bytes=limit * MIB),
        cost_estimate=pl.CostEstimate(flops=int(flops), bytes_accessed=int(nbytes), transcendentals=0),
    )


def f32(*shape):
    return jax.ShapeDtypeStruct(shape, F32)


def up(value, unit):
    return -(-value // unit) * unit


class Sizes:
    def __init__(self, state, segments, groups):
        count, self.nodes, self.rows, self.ax = state.shape
        self.count = count
        self.segments = segments
        self.groups = groups
        self.steps = count // segments
        self.cols = self.rows * self.ax
        self.height = self.nodes * self.rows
        self.pad = up(self.nodes, LANES)
        self.spill = up((self.pad - self.nodes) * self.rows, TILE)
        self.flops = 2 * 4 * self.pad * self.pad * self.cols

    def window(self, low, high):
        first = low * self.height // TILE * TILE
        return first, up(high * self.height, TILE) - first

    def message(self, count):
        return up(count * self.height, TILE)

    def rows_masked(self, x):
        cut = self.nodes // TILE * TILE
        rest = x[cut:]
        inside = lax.broadcasted_iota(jnp.int32, rest.shape, 0) < self.nodes - cut
        return jnp.concatenate([x[:cut], jnp.where(inside, rest, 0.0)], axis=0)

    def square(self, x):
        x = jnp.concatenate([x, jnp.zeros((self.nodes, self.pad - self.nodes), F32)], axis=1)
        return jnp.concatenate([x, jnp.zeros((self.pad - self.nodes, self.pad), F32)], axis=0)


def read_field(z, ref, lead, offset):
    parts = [ref[lead + (pl.ds(offset + j, z.pad, stride=z.rows), slice(None))] for j in range(z.rows)]
    return z.rows_masked(jnp.concatenate(parts, axis=1))


def read_exact(z, ref, lead, offset):
    parts = [ref[lead + (pl.ds(offset + j, z.nodes, stride=z.rows), slice(None))] for j in range(z.rows)]
    return jnp.concatenate(parts, axis=1)


def write_field(z, ref, lead, offset, value):
    for j in range(z.rows):
        rows = pl.ds(offset + j, z.nodes, stride=z.rows)
        ref[lead + (rows, slice(None))] = value[: z.nodes, j * z.ax : (j + 1) * z.ax]


def read_matrix(z, ref, k):
    return z.square(ref[:, k, :])


def send_pair(z, mine, e, stage, keep_ref, give_ref, sem):
    pairs = z.segments // 2
    place = lax.rem(e // 2 - mine // 2 + pairs, pairs)
    own = lax.rem(mine, 2) == e % 2

    @pl.when(own)
    def _():
        pltpu.make_async_copy(stage.at[e], keep_ref.at[place], sem.at[e]).start()

    @pl.when(jnp.logical_not(own))
    def _():
        pltpu.make_async_copy(stage.at[e], give_ref.at[place], sem.at[e]).start()

    return pltpu.make_async_copy(stage.at[e], keep_ref.at[place], sem.at[e])


def load_pairs(z, mine, sources, buf, sem):
    pairs = z.segments // 2
    side = lax.rem(mine, 2)
    copies = []
    for d in range(pairs):
        pair = lax.rem(mine // 2 - d + pairs, pairs) * 2
        for n in range(2):
            e = pair + (side if n == 0 else 1 - side)
            copies.append(pltpu.make_async_copy(sources[d].at[n], buf.at[e], sem.at[2 * d + n]))
    return copies


def sensor_call(z, state, to_modal):
    batch = 4 if z.segments % 4 == 0 else 1
    tall = z.steps * z.height

    def kernel(state_ref, modal_ref, sensor_ref, head_ref, tail_ref, buf, modal_buf, sem, modal_sem):
        modal_copy = pltpu.make_async_copy(modal_ref, modal_buf, modal_sem)
        modal_copy.start()
        copies = [
            pltpu.make_async_copy(state_ref.at[e], buf.at[e, pl.ds(0, tall)], sem.at[e]) for e in range(z.segments)
        ]
        for copy in copies:
            copy.start()
        modal_copy.wait()
        matrix = operand_left(z.square(modal_buf[...]))
        for e0 in range(0, z.segments, batch):
            for e in range(e0, e0 + batch):
                copies[e].wait()
            for e in range(e0, e0 + batch):
                for i in range(z.steps):
                    modal = product(matrix, operand_right(read_field(z, buf, (e,), i * z.height)))
                    squares = modal * modal
                    lower = jnp.sum(squares[: ORDER**3], axis=0, keepdims=True)
                    upper = jnp.sum(squares[ORDER**3 :], axis=0, keepdims=True)
                    sensor = (upper / z.nodes) / ((lower + upper) / z.nodes + 1e-6)
                    sensor_ref[i, e : e + 1, :] = sensor
                    head_ref[i, e : e + 1, :] = sensor[:, : z.ax]
                    tail_ref[i, e : e + 1, :] = sensor[:, z.cols - z.ax :]

    outs = [f32(z.steps, z.segments, z.cols)] + [f32(z.steps, z.segments, z.ax)] * 2
    return call(
        kernel,
        "sensor",
        outs,
        [spec_hbm()] * 2,
        [spec_vmem()] * 3,
        [
            pltpu.VMEM((z.segments, tall + z.spill, z.ax), F32),
            pltpu.VMEM((z.nodes, z.nodes), F32),
            pltpu.SemaphoreType.DMA((z.segments,)),
            pltpu.SemaphoreType.DMA,
        ],
        z.flops * z.steps * z.segments,
        4 * z.segments * tall * z.ax,
        limit=57,
    )(state, to_modal)


def smoothed(z, sensor, before, after, left, right):
    inner = sensor[:, : z.cols - z.ax]
    outer = sensor[:, z.ax :]
    from_left = jnp.concatenate([left, inner], axis=1)
    from_right = jnp.concatenate([outer, right], axis=1)
    return (4.0 * sensor + before + after + from_left + from_right) / 8.0


def sweep_call(z, chunk, parts, me, state, rhs, viscous, gain, inverse, sensors, lefts, rights, ring, carry, after):
    low, high = chunk
    opened = high == z.steps
    first, size = z.window(low, high)
    count = high - low
    first0, size0 = z.window(0, 1)
    steps = list(range(low, high)) + ([0] if opened else [])
    has_carry = carry is not None
    gains = list(range(low if has_carry else low + 1, high))
    messages = [z.message(stop - start) for start, stop in parts or [chunk]]
    edge_outs = low == 1
    pairs = z.segments // 2
    last, last_size = z.window(low - 2, low - 1)
    batch = next(n for n in (4, 8, z.segments) if z.segments % n == 0 and n * z.steps % TILE == 0)
    narrow = low == 1
    cuts = list(range(0, z.segments + 1, batch))
    if narrow:
        cuts[1:1] = [2]
    batches = list(zip(cuts[:-1], cuts[1:]))

    if parts:
        outs = [f32(pairs, message, z.ax) for message in messages for _ in range(2)]
    else:
        outs = [f32(z.segments, messages[0], z.ax)]

    def kernel(*refs):
        me_ref, state_ref, rhs_ref, viscous_ref, inverse_ref, gain_ref, sensor_ref, left_ref, right_ref = refs[:9]
        refs = refs[9:]
        if opened:
            before_ref, behind_ref, refs = refs[0], refs[1], refs[2:]
        if has_carry:
            carry_ref, refs = refs[0], refs[1:]
        refs = refs[len(after) :]
        out_refs, refs = refs[: len(outs)], refs[len(outs) :]
        if opened:
            end_ref, start_ref, refs = refs[0], refs[1], refs[2:]
        if edge_outs:
            low_ref, high_ref, refs = refs[0], refs[1], refs[2:]
        state_buf, rhs_buf, inverse_buf, gain_buf, viscous_buf, smooth_buf, sem, matrix_sem, out_sem = refs[:9]
        stages, refs = refs[9 : 9 + len(messages)], refs[9 + len(messages) :]
        if opened:
            state0, rhs0, refs = refs[0], refs[1], refs[2:]
        if has_carry:
            carry_buf = refs[0]
        viscous_copy = pltpu.make_async_copy(viscous_ref, viscous_buf, out_sem.at[0, 0])
        viscous_copy.start()
        copies = [[] for _ in range(z.segments)]
        for s0, s1 in batches:
            for s in range(s0, s1):
                moves = [
                    (state_ref.at[s, pl.ds(first, size)], state_buf.at[s, pl.ds(0, size)]),
                    (rhs_ref.at[s, pl.ds(first, size)], rhs_buf.at[s, pl.ds(0, size)]),
                ]
                if opened:
                    moves.append((state_ref.at[s, pl.ds(first0, size0)], state0.at[s, pl.ds(0, size0)]))
                    moves.append((rhs_ref.at[s, pl.ds(first0, size0)], rhs0.at[s, pl.ds(0, size0)]))
                if has_carry:
                    moves.append((carry_ref.at[s, pl.ds(last, last_size)], carry_buf.at[s, pl.ds(0, last_size)]))
                if narrow:
                    for source, target, needed in ((inverse_ref, inverse_buf, steps), (gain_ref, gain_buf, gains)):
                        if needed:
                            part = pl.ds(s * z.steps + needed[0], len(needed))
                            moves.append((source.at[:, part], target.at[:, part]))
                for n, (source, target) in enumerate(moves):
                    copies[s].append(pltpu.make_async_copy(source, target, sem.at[s, n]))
            if not narrow:
                part = pl.ds(s0 * z.steps, (s1 - s0) * z.steps)
                for n, (source, target) in enumerate(((inverse_ref, inverse_buf), (gain_ref, gain_buf))):
                    copy = pltpu.make_async_copy(source.at[:, part], target.at[:, part], matrix_sem.at[s0, n])
                    copies[s0].append(copy)
            for s in range(s0, s1):
                for copy in copies[s]:
                    copy.start()
        for n, i in enumerate(steps):
            before = sensor_ref[(i - 1) % z.steps]
            later = sensor_ref[(i + 1) % z.steps]
            if i == 0:
                before = jnp.concatenate([before_ref[...], before[: z.segments - 1]], axis=0)
            if i == z.steps - 1:
                later = jnp.concatenate([later[1:], behind_ref[...]], axis=0)
            smooth_buf[n] = smoothed(z, sensor_ref[i], before, later, left_ref[i], right_ref[i])
        if edge_outs:
            low_ref[...] = sensor_ref[0, :1]
            high_ref[...] = sensor_ref[z.steps - 1, z.segments - 1 :]
        viscous_copy.wait()
        operator = operand_left(z.square(viscous_buf[...]))
        sends = []

        for s0, s1 in batches:
            group = range(s0, s1)
            for s in group:
                for copy in copies[s]:
                    copy.wait()
            sources = []
            for n, i in enumerate(steps):
                bufs = (state0, rhs0, -first0) if i == 0 else (state_buf, rhs_buf, i * z.height - first)
                moved = [product(operator, operand_right(read_field(z, bufs[0], (s,), bufs[2]))) for s in group]
                forces = [
                    operand_right(read_field(z, bufs[1], (s,), bufs[2]) + smooth_buf[n, s : s + 1, :] * value)
                    for s, value in zip(group, moved)
                ]
                sources.append(forces)
            for n, i in enumerate(steps):
                sources[n] = [
                    product(operand_left(read_matrix(z, inverse_buf, s * z.steps + i)), force)
                    for s, force in zip(group, sources[n])
                ]
            fields = None
            if has_carry:
                fields = [read_field(z, carry_buf, (s,), (low - 2) * z.height - last) for s in group]
            for n, i in enumerate(steps):
                values = sources[n]
                if i == 0:
                    for s, value in zip(group, values):
                        start_ref[s] = value
                    continue
                if fields is not None:
                    swept = [
                        product(operand_left(read_matrix(z, gain_buf, s * z.steps + i)), operand_right(field))
                        for s, field in zip(group, fields)
                    ]
                    values = [value + more for value, more in zip(values, swept)]
                fields = values
                for s, value in zip(group, values):
                    for (start, stop), stage in zip(parts or [chunk], stages):
                        if start <= i < stop:
                            write_field(z, stage, (s,), (i - start) * z.height, value)
            for s, value in zip(group, fields):
                if opened:
                    end_ref[s] = value
                if not parts:
                    copy = pltpu.make_async_copy(stages[0].at[s], out_refs[0].at[s], out_sem.at[0, s])
                    copy.start()
                    sends.append(copy)
            for p, stage in enumerate(stages if parts else []):
                for s in group:
                    keep_ref, give_ref = out_refs[2 * p], out_refs[2 * p + 1]
                    sends.append(send_pair(z, me_ref[0], s, stage, keep_ref, give_ref, out_sem.at[p]))
        for copy in sends:
            copy.wait()

    field = f32(z.segments, z.pad, z.cols)
    out_specs = [spec_hbm()] * len(outs)
    more = [field] * (2 if opened else 0) + ([f32(1, z.cols)] * 2 if edge_outs else [])
    operands = [me, state, rhs, viscous, inverse, gain, sensors, lefts, rights]
    in_specs = [spec_smem()] + [spec_hbm()] * 5 + [spec_vmem()] * 3
    extra = list(ring) if opened else []
    extra_specs = [spec_vmem()] * len(extra)
    if has_carry:
        extra.append(carry)
        extra_specs.append(spec_hbm())
    scratch = [
        pltpu.VMEM((z.segments, size + z.spill, z.ax), F32),
        pltpu.VMEM((z.segments, size + z.spill, z.ax), F32),
        pltpu.VMEM(inverse.shape, F32),
        pltpu.VMEM(gain.shape, F32),
        pltpu.VMEM(viscous.shape, F32),
        pltpu.VMEM((len(steps), z.segments, z.cols), F32),
        pltpu.SemaphoreType.DMA((z.segments, 7)),
        pltpu.SemaphoreType.DMA((z.segments, 2)),
        pltpu.SemaphoreType.DMA((len(messages), z.segments)),
    ]
    scratch += [pltpu.VMEM((z.segments, message, z.ax), F32) for message in messages]
    if opened:
        scratch += [pltpu.VMEM((z.segments, size0 + z.spill, z.ax), F32)] * 2
    if has_carry:
        scratch.append(pltpu.VMEM((z.segments, last_size + z.spill, z.ax), F32))
    return call(
        kernel,
        f"sweep_{low}",
        outs + more,
        in_specs + extra_specs + [spec_any()] * len(after),
        out_specs + [spec_vmem()] * len(more),
        scratch,
        z.flops * len(steps) * z.segments * 3,
        4 * z.segments * size * z.ax * 4,
        limit=52,
    )(*operands, *extra, *after)


def maps_call(z, me, gain, after):
    def kernel(me_ref, gain_ref, *refs):
        own_ref, head_ref, tail_ref, whole_ref, prefix_ref, group_ref, gain_buf, kept, sem = refs[len(after) :]
        copy = pltpu.make_async_copy(gain_ref, gain_buf, sem)
        copy.start()
        copy.wait()

        def times(a, b):
            return product(operand_left(a), operand_right(b))

        values = [read_matrix(z, gain_buf, e * z.steps + 1) for e in range(z.segments)]
        for i in range(1, z.steps):
            if i > 1:
                values = [
                    times(read_matrix(z, gain_buf, e * z.steps + i), values[e]) for e in range(z.segments)
                ]
            for e in range(z.segments):
                kept[e, i] = values[e]
        heads = [read_matrix(z, gain_buf, e * z.steps) for e in range(z.segments)]
        for e in range(z.segments):
            kept[e, 0] = heads[e]
            head_ref[e] = heads[e]
            tail_ref[e] = values[e]
            whole_ref[e] = times(values[e], heads[e])
        own_ref[...] = kept[me_ref[0]]
        value = whole_ref[0]
        prefix_ref[0] = value
        for e in range(1, z.segments):
            prefix_ref[e] = value
            value = times(whole_ref[e], value)
        group_ref[...] = value

    square = (z.pad, z.pad)
    outs = [f32(z.steps, *square)] + [f32(z.segments, *square)] * 4 + [f32(*square)]
    return call(
        kernel,
        "maps",
        outs,
        [spec_smem(), spec_hbm()] + [spec_any()] * len(after),
        [spec_vmem()] * 6,
        [
            pltpu.VMEM(gain.shape, F32),
            pltpu.VMEM((z.segments, z.steps) + square, F32),
            pltpu.SemaphoreType.DMA,
        ],
        z.flops * z.segments * (z.steps + 1) // 2,
        4 * z.segments * z.steps * z.pad * z.pad,
    )(me, gain, *after)


def chain_call(z, starts, ends, tails, wholes, group):
    def kernel(start_ref, end_ref, tail_ref, whole_ref, group_ref, before_ref, pack_ref):
        value = None
        for e in range(z.segments):
            shift = end_ref[e] + product(operand_left(tail_ref[e]), operand_right(start_ref[e]))
            if e > 0:
                before_ref[e] = value
                shift = shift + product(operand_left(whole_ref[e]), operand_right(value))
            else:
                before_ref[0] = jnp.zeros_like(shift)
            value = shift
        pack_ref[:, : z.cols] = value
        pack_ref[:, z.cols :] = group_ref[...]

    return call(
        kernel,
        "chain",
        [f32(z.segments, z.pad, z.cols), f32(z.pad, z.cols + z.pad)],
        [spec_vmem()] * 5,
        [spec_vmem()] * 2,
        [],
        z.flops * z.segments * 2,
        4 * z.segments * z.pad * z.cols * 4,
    )(starts, ends, tails, wholes, group)


def first_call(z, places, packs, before, prefix, heads, starts):
    rows = z.message(1)
    pairs = z.segments // 2

    def kernel(*refs):
        places_ref, refs = refs[0], refs[1:]
        pack_refs, refs = refs[: z.groups], refs[z.groups :]
        before_ref, prefix_ref, head_ref, start_ref, keep_ref, give_ref, stage, sem = refs
        mine = places_ref[0]
        group = places_ref[1]
        value = jnp.zeros((z.pad, z.cols), F32)
        matrices = [operand_left(ref[:, z.cols :]) for ref in pack_refs]
        for t in range(2 * z.groups - 1, 0, -1):
            n = t % z.groups
            moved = product(matrices[n], operand_right(value)) + pack_refs[n][:, : z.cols]
            value = jnp.where(t <= z.groups + group, moved, 0.0)
        incoming = operand_right(value)
        arriving = [value] + [
            before_ref[e] + product(operand_left(prefix_ref[e]), incoming) for e in range(1, z.segments)
        ]
        solved = [
            start_ref[e] + product(operand_left(head_ref[e]), operand_right(arriving[e])) for e in range(z.segments)
        ]
        for e in range(z.segments):
            write_field(z, stage, (e,), 0, solved[e])
        sends = [send_pair(z, mine, e, stage, keep_ref, give_ref, sem) for e in range(z.segments)]
        for copy in sends:
            copy.wait()

    return call(
        kernel,
        "first",
        [f32(pairs, rows, z.ax)] * 2,
        [spec_smem()] + [spec_vmem()] * (z.groups + 4),
        [spec_hbm()] * 2,
        [pltpu.VMEM((z.segments, rows, z.ax), F32), pltpu.SemaphoreType.DMA((z.segments,))],
        z.flops * (z.segments * 2 + 2 * z.groups),
        4 * z.segments * z.pad * z.cols * 4,
    )(places, *packs, before, prefix, heads, starts)


def couple_call(z, keep, got):
    pairs, message, _ = keep.shape

    def kernel(*refs):
        sources, refs = refs[:2], refs[2:]
        outs, buf, sem = refs[:pairs], refs[pairs], refs[pairs + 1]
        loads = [
            [pltpu.make_async_copy(sources[n].at[d], buf.at[d, n], sem.at[d, n]) for n in range(2)]
            for d in range(pairs)
        ]
        for load in loads:
            for copy in load:
                copy.start()
        stores = []
        for d in range(pairs):
            for copy in loads[d]:
                copy.wait()
            copy = pltpu.make_async_copy(buf.at[d], outs[d], sem.at[d, 0])
            copy.start()
            stores.append(copy)
        for copy in stores:
            copy.wait()

    return call(
        kernel,
        "couple",
        [f32(2, message, z.ax)] * pairs,
        [spec_hbm()] * 2,
        [spec_hbm()] * pairs,
        [pltpu.VMEM((pairs, 2, message, z.ax), F32), pltpu.SemaphoreType.DMA((pairs, 2))],
        0,
        4 * 4 * pairs * message * z.ax,
    )(keep, got)


def gate_call(held, after):
    def kernel(*refs):
        pass

    return call(
        kernel,
        "gate",
        f32(*held.shape),
        [spec_hbm(), spec_any()],
        spec_hbm(),
        [],
        0,
        0,
        {0: 0},
    )(held, after)


def open_call(z, one, me, own, received_one, received_first):
    radial = z.segments * z.rows
    tall = z.nodes * radial
    operand_shape = (z.segments, 2 * z.pad, z.cols)
    low, high = one
    pairs = z.segments // 2
    message = received_first[0].shape[1]

    def kernel(me_ref, own_ref, one_ref, *refs):
        first_refs, refs = refs[:pairs], refs[pairs:]
        out_ref, operand_ref, own_buf, one_buf, first_buf, stage, one_sem, first_sem, own_sem, out_sem = refs
        first_copies = load_pairs(z, me_ref[0], first_refs, first_buf, first_sem)
        one_copies = [pltpu.make_async_copy(one_ref.at[e], one_buf.at[e], one_sem.at[e]) for e in range(z.segments)]
        own_copy = pltpu.make_async_copy(own_ref, own_buf, own_sem)
        for copy in first_copies + [own_copy] + one_copies:
            copy.start()
        for copy in first_copies:
            copy.wait()
        sends = []

        def put(i, e, value):
            for j in range(z.rows):
                rows = pl.ds(e * z.rows + j, z.nodes, stride=radial)
                stage[i, rows, :] = value[: z.nodes, j * z.ax : (j + 1) * z.ax]

        def send(i):
            copy = pltpu.make_async_copy(stage.at[i], out_ref.at[i], out_sem.at[i])
            copy.start()
            sends.append(copy)

        for e in range(z.segments):
            field = read_exact(z, first_buf, (e,), 0)
            empty = jnp.zeros((z.pad - z.nodes, z.cols), F32)
            operand_ref[e] = operand_right(jnp.concatenate([field, empty], axis=0))
            put(0, e, field)
        send(0)
        own_copy.wait()
        for copy in one_copies:
            copy.wait()
        for i in range(low, high):
            matrix = operand_left(own_buf[i])
            for e in range(z.segments):
                value = product(matrix, operand_ref[e])[: z.nodes]
                put(i, e, value + read_exact(z, one_buf, (e,), (i - low) * z.height))
            send(i)
        for copy in sends:
            copy.wait()

    return call(
        kernel,
        "finish_0",
        [f32(z.steps, tall, z.ax), jax.ShapeDtypeStruct(operand_shape, BF16)],
        [spec_smem()] + [spec_hbm()] * (2 + pairs),
        [spec_hbm(), spec_vmem()],
        [
            pltpu.VMEM((z.steps, z.pad, z.pad), F32),
            pltpu.VMEM(received_one.shape, F32),
            pltpu.VMEM((z.segments, message, z.ax), F32),
            pltpu.VMEM((high, tall, z.ax), F32),
            pltpu.SemaphoreType.DMA((z.segments,)),
            pltpu.SemaphoreType.DMA((z.segments,)),
            pltpu.SemaphoreType.DMA,
            pltpu.SemaphoreType.DMA((high,)),
        ],
        z.flops * (high - 1) * z.segments,
        4 * 2 * high * tall * z.ax,
    )(me, own, received_one, *received_first)


def finish_call(z, chunk, me, own, messages, operands, out):
    low, high = chunk
    count = high - low
    radial = z.segments * z.rows
    tall = z.nodes * radial
    message = messages[0].shape[1]

    def kernel(me_ref, own_ref, operand_ref, *refs):
        message_refs, refs = refs[: len(messages)], refs[len(messages) :]
        _, out_ref, buf, own_buf, operand_buf, stage, sem, in_sem, out_sem = refs
        own_copy = pltpu.make_async_copy(own_ref.at[pl.ds(low, count)], own_buf, in_sem.at[0])
        operand_copy = pltpu.make_async_copy(operand_ref, operand_buf, in_sem.at[1])
        own_copy.start()
        operand_copy.start()
        copies = load_pairs(z, me_ref[0], message_refs, buf, sem)
        for copy in copies:
            copy.start()
        own_copy.wait()
        operand_copy.wait()
        for copy in copies:
            copy.wait()
        sends = []
        for n in range(count):
            matrix = operand_left(own_buf[n])
            for e in range(z.segments):
                value = product(matrix, operand_buf[e])[: z.nodes] + read_exact(z, buf, (e,), n * z.height)
                for j in range(z.rows):
                    rows = pl.ds(e * z.rows + j, z.nodes, stride=radial)
                    stage[n, rows, :] = value[:, j * z.ax : (j + 1) * z.ax]
            copy = pltpu.make_async_copy(stage.at[n], out_ref.at[low + n], out_sem.at[n])
            copy.start()
            sends.append(copy)
        for copy in sends:
            copy.wait()

    inputs = [me, own, operands] + list(messages) + [out]
    return call(
        kernel,
        f"finish_{low}",
        f32(z.steps, tall, z.ax),
        [spec_smem()] + [spec_hbm()] * (len(inputs) - 1),
        spec_hbm(),
        [
            pltpu.VMEM((z.segments, message, z.ax), F32),
            pltpu.VMEM((count, z.pad, z.pad), F32),
            pltpu.VMEM(operands.shape, BF16),
            pltpu.VMEM((count, tall, z.ax), F32),
            pltpu.SemaphoreType.DMA((z.segments,)),
            pltpu.SemaphoreType.DMA((2,)),
            pltpu.SemaphoreType.DMA((count,)),
        ],
        z.flops * count * z.segments,
        4 * 2 * count * tall * z.ax,
        {len(inputs) - 1: 0},
        limit=57 if count > 1 else 40,
    )(*inputs)


def shift_by(array, axis, by):
    size = lax.axis_size(axis)
    return lax.ppermute(array, axis, [(i, (i + by) % size) for i in range(size)])


def neighbours(head, tail):
    size = lax.axis_size("elem")
    left = lax.ppermute(tail, "elem", [(i, i + 1) for i in range(size - 1)])
    right = lax.ppermute(head, "elem", [(i + 1, i) for i in range(size - 1)])
    return left, right


def spread(messages):
    return lax.all_to_all(messages, "elem", 0, 0, tiled=True)


def spread_pairs(z, keep, give, after):
    got = lax.ppermute(give, "elem", [(i, i ^ 1) for i in range(z.segments)])
    coupled = couple_call(z, keep, got)
    moved = [coupled[0]]
    for d in range(1, z.segments // 2):
        held = coupled[d] if after is None else gate_call(coupled[d], after[d])
        moved.append(shift_by(held, "elem", 2 * d))
    return moved


def chunks_of(steps):
    middle = 4 if steps >= 8 else 2
    last = steps - 1
    parts = [(middle, last), (last, steps)] if last > middle else [(middle, steps)]
    return (1, middle), (middle, steps), parts


def body(state, rhs, to_modal, viscous_op, sweep_gain, inv_blocks):
    segments = lax.axis_size("elem")
    groups = lax.axis_size("blk")
    z = Sizes(state, segments, groups)
    state = state.reshape(segments, z.steps * z.height, z.ax)
    rhs = rhs.reshape(segments, z.steps * z.height, z.ax)
    gain = jnp.transpose(sweep_gain, (1, 0, 2))
    inverse = jnp.transpose(inv_blocks, (1, 0, 2))
    here = lax.axis_index("elem").astype(jnp.int32)
    me = here.reshape(1)
    places = jnp.stack([here, lax.axis_index("blk").astype(jnp.int32)])
    one, two, parts = chunks_of(z.steps)
    sensors, head, tail = sensor_call(z, state, to_modal)
    lefts, rights = neighbours(head, tail)

    def sweep(chunk, parts, ring, carry, after):
        return sweep_call(
            z, chunk, parts, me, state, rhs, viscous_op, gain, inverse, sensors, lefts, rights, ring, carry, after
        )

    messages_one, low, high = sweep(one, [], None, None, [])
    ring = [shift_by(high, "blk", 1), shift_by(low, "blk", -1)]
    own, heads, tails, wholes, prefix, group = maps_call(z, me, gain, [messages_one])
    *pairs, ends, starts = sweep(two, parts, ring, messages_one, [group])
    before, pack = chain_call(z, starts, ends, tails, wholes, group)
    packs = [pack] + [shift_by(pack, "blk", s) for s in range(1, groups)]
    keep_first, give_first = first_call(z, places, packs, before, prefix, heads, starts)
    received_one = spread(messages_one)
    received_first = spread_pairs(z, keep_first, give_first, None)
    out, operands = open_call(z, one, me, own, received_one, received_first)
    after = received_first
    for n, part in enumerate(parts):
        received = spread_pairs(z, pairs[2 * n], pairs[2 * n + 1], after)
        out = finish_call(z, part, me, own, received, operands, out)
        after = [received[1]] * len(received)
    return out.reshape(z.steps, z.nodes, segments * z.rows, z.ax)


def solution(mesh):
    in_specs = (
        P("blk", None, "elem", None),
        P("blk", None, "elem", None),
        P(),
        P(),
        P("blk", None, None),
        P("blk", None, None),
    )
    out_specs = P(("blk", "elem"), None, None, None)
    return jax.shard_map(body, mesh=mesh, in_specs=in_specs, out_specs=out_specs, check_vma=False)
```

```python
import functools

import jax
import jax.numpy as jnp
from jax import lax
from jax.experimental import pallas as pl
from jax.experimental.pallas import tpu as pltpu
from jax.sharding import PartitionSpec as P

ORDER = 4
F32 = jnp.float32
BF16 = jnp.bfloat16
MIB = 1024 * 1024
TILE = 8
LANES = 128


def operand_left(a):
    high = a.astype(BF16)
    low = (a - high.astype(F32)).astype(BF16)
    return jnp.concatenate([jnp.concatenate([high, high], axis=1), jnp.concatenate([low, low], axis=1)], axis=0)


def operand_right(x):
    high = x.astype(BF16)
    return jnp.concatenate([high, (x - high.astype(F32)).astype(BF16)], axis=0)


def product(left, right):
    both = jnp.dot(left, right, preferred_element_type=F32)
    half = left.shape[0] // 2
    return both[:half] + both[half:]


def spec_any():
    return pl.BlockSpec(memory_space=pl.ANY)


def spec_hbm():
    return pl.BlockSpec(memory_space=pltpu.HBM)


def spec_vmem():
    return pl.BlockSpec(memory_space=pltpu.VMEM)


def spec_smem():
    return pl.BlockSpec(memory_space=pltpu.SMEM)


def call(kernel, name, outs, in_specs, out_specs, scratch, flops, nbytes, aliases=None, limit=57):
    return pl.pallas_call(
        kernel,
        name=name,
        out_shape=outs,
        in_specs=in_specs,
        out_specs=out_specs,
        scratch_shapes=scratch,
        input_output_aliases=aliases or {},
        compiler_params=pltpu.CompilerParams(vmem_limit_bytes=limit * MIB),
        cost_estimate=pl.CostEstimate(flops=int(flops), bytes_accessed=int(nbytes), transcendentals=0),
    )


def f32(*shape):
    return jax.ShapeDtypeStruct(shape, F32)


def up(value, unit):
    return -(-value // unit) * unit


class Sizes:
    def __init__(self, state, segments, groups):
        count, self.nodes, self.rows, self.ax = state.shape
        self.count = count
        self.segments = segments
        self.groups = groups
        self.steps = count // segments
        self.cols = self.rows * self.ax
        self.height = self.nodes * self.rows
        self.pad = up(self.nodes, LANES)
        self.spill = up((self.pad - self.nodes) * self.rows, TILE)
        self.flops = 2 * 4 * self.pad * self.pad * self.cols

    def window(self, low, high):
        first = low * self.height // TILE * TILE
        return first, up(high * self.height, TILE) - first

    def message(self, count):
        return up(count * self.height, TILE)

    def rows_masked(self, x):
        cut = self.nodes // TILE * TILE
        rest = x[cut:]
        inside = lax.broadcasted_iota(jnp.int32, rest.shape, 0) < self.nodes - cut
        return jnp.concatenate([x[:cut], jnp.where(inside, rest, 0.0)], axis=0)

    def square(self, x):
        x = jnp.concatenate([x, jnp.zeros((self.nodes, self.pad - self.nodes), F32)], axis=1)
        return jnp.concatenate([x, jnp.zeros((self.pad - self.nodes, self.pad), F32)], axis=0)


def read_field(z, ref, lead, offset):
    parts = [ref[lead + (pl.ds(offset + j, z.pad, stride=z.rows), slice(None))] for j in range(z.rows)]
    return z.rows_masked(jnp.concatenate(parts, axis=1))


def read_exact(z, ref, lead, offset):
    parts = [ref[lead + (pl.ds(offset + j, z.nodes, stride=z.rows), slice(None))] for j in range(z.rows)]
    return jnp.concatenate(parts, axis=1)


def write_field(z, ref, lead, offset, value):
    for j in range(z.rows):
        rows = pl.ds(offset + j, z.nodes, stride=z.rows)
        ref[lead + (rows, slice(None))] = value[: z.nodes, j * z.ax : (j + 1) * z.ax]


def read_matrix(z, ref, k):
    return z.square(ref[:, k, :])


def send_pair(z, mine, e, stage, keep_ref, give_ref, sem):
    pairs = z.segments // 2
    place = lax.rem(e // 2 - mine // 2 + pairs, pairs)
    own = lax.rem(mine, 2) == e % 2

    @pl.when(own)
    def _():
        pltpu.make_async_copy(stage.at[e], keep_ref.at[place], sem.at[e]).start()

    @pl.when(jnp.logical_not(own))
    def _():
        pltpu.make_async_copy(stage.at[e], give_ref.at[place], sem.at[e]).start()

    return pltpu.make_async_copy(stage.at[e], keep_ref.at[place], sem.at[e])


def load_pairs(z, mine, sources, buf, sem):
    pairs = z.segments // 2
    side = lax.rem(mine, 2)
    copies = []
    for d in range(pairs):
        pair = lax.rem(mine // 2 - d + pairs, pairs) * 2
        for n in range(2):
            e = pair + (side if n == 0 else 1 - side)
            copies.append(pltpu.make_async_copy(sources[d].at[n], buf.at[e], sem.at[2 * d + n]))
    return copies


def sensor_call(z, state, to_modal):
    batch = 4 if z.segments % 4 == 0 else 1
    tall = z.steps * z.height

    def kernel(state_ref, modal_ref, sensor_ref, head_ref, tail_ref, buf, modal_buf, sem, modal_sem):
        modal_copy = pltpu.make_async_copy(modal_ref, modal_buf, modal_sem)
        modal_copy.start()
        copies = [
            pltpu.make_async_copy(state_ref.at[e], buf.at[e, pl.ds(0, tall)], sem.at[e]) for e in range(z.segments)
        ]
        for copy in copies:
            copy.start()
        modal_copy.wait()
        matrix = operand_left(z.square(modal_buf[...]))
        for e0 in range(0, z.segments, batch):
            for e in range(e0, e0 + batch):
                copies[e].wait()
            for e in range(e0, e0 + batch):
                for i in range(z.steps):
                    modal = product(matrix, operand_right(read_field(z, buf, (e,), i * z.height)))
                    squares = modal * modal
                    lower = jnp.sum(squares[: ORDER**3], axis=0, keepdims=True)
                    upper = jnp.sum(squares[ORDER**3 :], axis=0, keepdims=True)
                    sensor = (upper / z.nodes) / ((lower + upper) / z.nodes + 1e-6)
                    sensor_ref[i, e : e + 1, :] = sensor
                    head_ref[i, e : e + 1, :] = sensor[:, : z.ax]
                    tail_ref[i, e : e + 1, :] = sensor[:, z.cols - z.ax :]

    outs = [f32(z.steps, z.segments, z.cols)] + [f32(z.steps, z.segments, z.ax)] * 2
    return call(
        kernel,
        "sensor",
        outs,
        [spec_hbm()] * 2,
        [spec_vmem()] * 3,
        [
            pltpu.VMEM((z.segments, tall + z.spill, z.ax), F32),
            pltpu.VMEM((z.nodes, z.nodes), F32),
            pltpu.SemaphoreType.DMA((z.segments,)),
            pltpu.SemaphoreType.DMA,
        ],
        z.flops * z.steps * z.segments,
        4 * z.segments * tall * z.ax,
        limit=52,
    )(state, to_modal)


def smoothed(z, sensor, before, after, left, right):
    inner = sensor[:, : z.cols - z.ax]
    outer = sensor[:, z.ax :]
    from_left = jnp.concatenate([left, inner], axis=1)
    from_right = jnp.concatenate([outer, right], axis=1)
    return (4.0 * sensor + before + after + from_left + from_right) / 8.0


def sweep_call(z, chunk, parts, me, state, rhs, viscous, gain, inverse, sensors, lefts, rights, ring, carry, after):
    low, high = chunk
    opened = high == z.steps
    first, size = z.window(low, high)
    count = high - low
    first0, size0 = z.window(0, 1)
    steps = list(range(low, high)) + ([0] if opened else [])
    has_carry = carry is not None
    gains = list(range(low if has_carry else low + 1, high))
    messages = [z.message(stop - start) for start, stop in parts or [chunk]]
    edge_outs = low == 1
    pairs = z.segments // 2
    last, last_size = z.window(low - 2, low - 1)
    batch = next(n for n in (4, 8, z.segments) if z.segments % n == 0 and n * z.steps % TILE == 0)
    narrow = low == 1
    cuts = list(range(0, z.segments + 1, batch))
    if narrow:
        cuts[1:1] = [2]
    batches = list(zip(cuts[:-1], cuts[1:]))

    if parts:
        outs = [f32(pairs, message, z.ax) for message in messages for _ in range(2)]
    else:
        outs = [f32(z.segments, messages[0], z.ax)]

    def kernel(*refs):
        me_ref, state_ref, rhs_ref, viscous_ref, inverse_ref, gain_ref, sensor_ref, left_ref, right_ref = refs[:9]
        refs = refs[9:]
        if opened:
            before_ref, behind_ref, refs = refs[0], refs[1], refs[2:]
        if has_carry:
            carry_ref, refs = refs[0], refs[1:]
        refs = refs[len(after) :]
        out_refs, refs = refs[: len(outs)], refs[len(outs) :]
        if opened:
            end_ref, start_ref, refs = refs[0], refs[1], refs[2:]
        if edge_outs:
            low_ref, high_ref, refs = refs[0], refs[1], refs[2:]
        state_buf, rhs_buf, inverse_buf, gain_buf, viscous_buf, smooth_buf, sem, matrix_sem, out_sem = refs[:9]
        stages, refs = refs[9 : 9 + len(messages)], refs[9 + len(messages) :]
        if opened:
            state0, rhs0, refs = refs[0], refs[1], refs[2:]
        if has_carry:
            carry_buf = refs[0]
        viscous_copy = pltpu.make_async_copy(viscous_ref, viscous_buf, out_sem.at[0, 0])
        viscous_copy.start()
        copies = [[] for _ in range(z.segments)]
        for s0, s1 in batches:
            for s in range(s0, s1):
                moves = [
                    (state_ref.at[s, pl.ds(first, size)], state_buf.at[s, pl.ds(0, size)]),
                    (rhs_ref.at[s, pl.ds(first, size)], rhs_buf.at[s, pl.ds(0, size)]),
                ]
                if opened:
                    moves.append((state_ref.at[s, pl.ds(first0, size0)], state0.at[s, pl.ds(0, size0)]))
                    moves.append((rhs_ref.at[s, pl.ds(first0, size0)], rhs0.at[s, pl.ds(0, size0)]))
                if has_carry:
                    moves.append((carry_ref.at[s, pl.ds(last, last_size)], carry_buf.at[s, pl.ds(0, last_size)]))
                if narrow:
                    for source, target, needed in ((inverse_ref, inverse_buf, steps), (gain_ref, gain_buf, gains)):
                        if needed:
                            part = pl.ds(s * z.steps + needed[0], len(needed))
                            moves.append((source.at[:, part], target.at[:, part]))
                for n, (source, target) in enumerate(moves):
                    copies[s].append(pltpu.make_async_copy(source, target, sem.at[s, n]))
            if not narrow:
                part = pl.ds(s0 * z.steps, (s1 - s0) * z.steps)
                for n, (source, target) in enumerate(((inverse_ref, inverse_buf), (gain_ref, gain_buf))):
                    copy = pltpu.make_async_copy(source.at[:, part], target.at[:, part], matrix_sem.at[s0, n])
                    copies[s0].append(copy)
            for s in range(s0, s1):
                for copy in copies[s]:
                    copy.start()
        for n, i in enumerate(steps):
            before = sensor_ref[(i - 1) % z.steps]
            later = sensor_ref[(i + 1) % z.steps]
            if i == 0:
                before = jnp.concatenate([before_ref[...], before[: z.segments - 1]], axis=0)
            if i == z.steps - 1:
                later = jnp.concatenate([later[1:], behind_ref[...]], axis=0)
            smooth_buf[n] = smoothed(z, sensor_ref[i], before, later, left_ref[i], right_ref[i])
        if edge_outs:
            low_ref[...] = sensor_ref[0, :1]
            high_ref[...] = sensor_ref[z.steps - 1, z.segments - 1 :]
        viscous_copy.wait()
        operator = operand_left(z.square(viscous_buf[...]))
        sends = []

        for s0, s1 in batches:
            group = range(s0, s1)
            for s in group:
                for copy in copies[s]:
                    copy.wait()
            sources = []
            for n, i in enumerate(steps):
                bufs = (state0, rhs0, -first0) if i == 0 else (state_buf, rhs_buf, i * z.height - first)
                moved = [product(operator, operand_right(read_field(z, bufs[0], (s,), bufs[2]))) for s in group]
                forces = [
                    operand_right(read_field(z, bufs[1], (s,), bufs[2]) + smooth_buf[n, s : s + 1, :] * value)
                    for s, value in zip(group, moved)
                ]
                sources.append(forces)
            for n, i in enumerate(steps):
                sources[n] = [
                    product(operand_left(read_matrix(z, inverse_buf, s * z.steps + i)), force)
                    for s, force in zip(group, sources[n])
                ]
            fields = None
            if has_carry:
                fields = [read_field(z, carry_buf, (s,), (low - 2) * z.height - last) for s in group]
            for n, i in enumerate(steps):
                values = sources[n]
                if i == 0:
                    for s, value in zip(group, values):
                        start_ref[s] = value
                    continue
                if fields is not None:
                    swept = [
                        product(operand_left(read_matrix(z, gain_buf, s * z.steps + i)), operand_right(field))
                        for s, field in zip(group, fields)
                    ]
                    values = [value + more for value, more in zip(values, swept)]
                fields = values
                for s, value in zip(group, values):
                    for (start, stop), stage in zip(parts or [chunk], stages):
                        if start <= i < stop:
                            write_field(z, stage, (s,), (i - start) * z.height, value)
            for s, value in zip(group, fields):
                if opened:
                    end_ref[s] = value
                if not parts:
                    copy = pltpu.make_async_copy(stages[0].at[s], out_refs[0].at[s], out_sem.at[0, s])
                    copy.start()
                    sends.append(copy)
            for p, stage in enumerate(stages if parts else []):
                for s in group:
                    keep_ref, give_ref = out_refs[2 * p], out_refs[2 * p + 1]
                    sends.append(send_pair(z, me_ref[0], s, stage, keep_ref, give_ref, out_sem.at[p]))
        for copy in sends:
            copy.wait()

    field = f32(z.segments, z.pad, z.cols)
    out_specs = [spec_hbm()] * len(outs)
    more = [field] * (2 if opened else 0) + ([f32(1, z.cols)] * 2 if edge_outs else [])
    operands = [me, state, rhs, viscous, inverse, gain, sensors, lefts, rights]
    in_specs = [spec_smem()] + [spec_hbm()] * 5 + [spec_vmem()] * 3
    extra = list(ring) if opened else []
    extra_specs = [spec_vmem()] * len(extra)
    if has_carry:
        extra.append(carry)
        extra_specs.append(spec_hbm())
    scratch = [
        pltpu.VMEM((z.segments, size + z.spill, z.ax), F32),
        pltpu.VMEM((z.segments, size + z.spill, z.ax), F32),
        pltpu.VMEM(inverse.shape, F32),
        pltpu.VMEM(gain.shape, F32),
        pltpu.VMEM(viscous.shape, F32),
        pltpu.VMEM((len(steps), z.segments, z.cols), F32),
        pltpu.SemaphoreType.DMA((z.segments, 7)),
        pltpu.SemaphoreType.DMA((z.segments, 2)),
        pltpu.SemaphoreType.DMA((len(messages), z.segments)),
    ]
    scratch += [pltpu.VMEM((z.segments, message, z.ax), F32) for message in messages]
    if opened:
        scratch += [pltpu.VMEM((z.segments, size0 + z.spill, z.ax), F32)] * 2
    if has_carry:
        scratch.append(pltpu.VMEM((z.segments, last_size + z.spill, z.ax), F32))
    return call(
        kernel,
        f"sweep_{low}",
        outs + more,
        in_specs + extra_specs + [spec_any()] * len(after),
        out_specs + [spec_vmem()] * len(more),
        scratch,
        z.flops * len(steps) * z.segments * 3,
        4 * z.segments * size * z.ax * 4,
        limit=52,
    )(*operands, *extra, *after)


def maps_call(z, me, gain, after):
    def kernel(me_ref, gain_ref, *refs):
        own_ref, head_ref, tail_ref, whole_ref, prefix_ref, group_ref, gain_buf, kept, sem = refs[len(after) :]
        copy = pltpu.make_async_copy(gain_ref, gain_buf, sem)
        copy.start()
        copy.wait()

        def times(a, b):
            return product(operand_left(a), operand_right(b))

        values = [read_matrix(z, gain_buf, e * z.steps + 1) for e in range(z.segments)]
        for i in range(1, z.steps):
            if i > 1:
                values = [
                    times(read_matrix(z, gain_buf, e * z.steps + i), values[e]) for e in range(z.segments)
                ]
            for e in range(z.segments):
                kept[e, i] = values[e]
        heads = [read_matrix(z, gain_buf, e * z.steps) for e in range(z.segments)]
        for e in range(z.segments):
            kept[e, 0] = heads[e]
            head_ref[e] = heads[e]
            tail_ref[e] = values[e]
            whole_ref[e] = times(values[e], heads[e])
        own_ref[...] = kept[me_ref[0]]
        value = whole_ref[0]
        prefix_ref[0] = value
        for e in range(1, z.segments):
            prefix_ref[e] = value
            value = times(whole_ref[e], value)
        group_ref[...] = value

    square = (z.pad, z.pad)
    outs = [f32(z.steps, *square)] + [f32(z.segments, *square)] * 4 + [f32(*square)]
    return call(
        kernel,
        "maps",
        outs,
        [spec_smem(), spec_hbm()] + [spec_any()] * len(after),
        [spec_vmem()] * 6,
        [
            pltpu.VMEM(gain.shape, F32),
            pltpu.VMEM((z.segments, z.steps) + square, F32),
            pltpu.SemaphoreType.DMA,
        ],
        z.flops * z.segments * (z.steps + 1) // 2,
        4 * z.segments * z.steps * z.pad * z.pad,
        limit=52,
    )(me, gain, *after)


def chain_call(z, starts, ends, tails, wholes, group):
    def kernel(start_ref, end_ref, tail_ref, whole_ref, group_ref, before_ref, pack_ref):
        value = None
        for e in range(z.segments):
            shift = end_ref[e] + product(operand_left(tail_ref[e]), operand_right(start_ref[e]))
            if e > 0:
                before_ref[e] = value
                shift = shift + product(operand_left(whole_ref[e]), operand_right(value))
            else:
                before_ref[0] = jnp.zeros_like(shift)
            value = shift
        pack_ref[:, : z.cols] = value
        pack_ref[:, z.cols :] = group_ref[...]

    return call(
        kernel,
        "chain",
        [f32(z.segments, z.pad, z.cols), f32(z.pad, z.cols + z.pad)],
        [spec_vmem()] * 5,
        [spec_vmem()] * 2,
        [],
        z.flops * z.segments * 2,
        4 * z.segments * z.pad * z.cols * 4,
    )(starts, ends, tails, wholes, group)


def first_call(z, places, packs, before, prefix, heads, starts):
    rows = z.message(1)
    pairs = z.segments // 2

    def kernel(*refs):
        places_ref, refs = refs[0], refs[1:]
        pack_refs, refs = refs[: z.groups], refs[z.groups :]
        before_ref, prefix_ref, head_ref, start_ref, keep_ref, give_ref, stage, sem = refs
        mine = places_ref[0]
        group = places_ref[1]
        value = jnp.zeros((z.pad, z.cols), F32)
        matrices = [operand_left(ref[:, z.cols :]) for ref in pack_refs]
        for t in range(2 * z.groups - 1, 0, -1):
            n = t % z.groups
            moved = product(matrices[n], operand_right(value)) + pack_refs[n][:, : z.cols]
            value = jnp.where(t <= z.groups + group, moved, 0.0)
        incoming = operand_right(value)
        arriving = [value] + [
            before_ref[e] + product(operand_left(prefix_ref[e]), incoming) for e in range(1, z.segments)
        ]
        solved = [
            start_ref[e] + product(operand_left(head_ref[e]), operand_right(arriving[e])) for e in range(z.segments)
        ]
        for e in range(z.segments):
            write_field(z, stage, (e,), 0, solved[e])
        sends = [send_pair(z, mine, e, stage, keep_ref, give_ref, sem) for e in range(z.segments)]
        for copy in sends:
            copy.wait()

    return call(
        kernel,
        "first",
        [f32(pairs, rows, z.ax)] * 2,
        [spec_smem()] + [spec_vmem()] * (z.groups + 4),
        [spec_hbm()] * 2,
        [pltpu.VMEM((z.segments, rows, z.ax), F32), pltpu.SemaphoreType.DMA((z.segments,))],
        z.flops * (z.segments * 2 + 2 * z.groups),
        4 * z.segments * z.pad * z.cols * 4,
    )(places, *packs, before, prefix, heads, starts)


def couple_call(z, keep, got):
    pairs, message, _ = keep.shape

    def kernel(*refs):
        sources, refs = refs[:2], refs[2:]
        outs, buf, sem = refs[:pairs], refs[pairs], refs[pairs + 1]
        loads = [
            [pltpu.make_async_copy(sources[n].at[d], buf.at[d, n], sem.at[d, n]) for n in range(2)]
            for d in range(pairs)
        ]
        for load in loads:
            for copy in load:
                copy.start()
        stores = []
        for d in range(pairs):
            for copy in loads[d]:
                copy.wait()
            copy = pltpu.make_async_copy(buf.at[d], outs[d], sem.at[d, 0])
            copy.start()
            stores.append(copy)
        for copy in stores:
            copy.wait()

    return call(
        kernel,
        "couple",
        [f32(2, message, z.ax)] * pairs,
        [spec_hbm()] * 2,
        [spec_hbm()] * pairs,
        [pltpu.VMEM((pairs, 2, message, z.ax), F32), pltpu.SemaphoreType.DMA((pairs, 2))],
        0,
        4 * 4 * pairs * message * z.ax,
    )(keep, got)


def gate_call(held, after):
    def kernel(*refs):
        pass

    return call(
        kernel,
        "gate",
        f32(*held.shape),
        [spec_hbm(), spec_any()],
        spec_hbm(),
        [],
        0,
        0,
        {0: 0},
    )(held, after)


def open_call(z, one, me, own, received_one, received_first):
    radial = z.segments * z.rows
    tall = z.nodes * radial
    operand_shape = (z.segments, 2 * z.pad, z.cols)
    low, high = one
    pairs = z.segments // 2
    message = received_first[0].shape[1]

    def kernel(me_ref, own_ref, one_ref, *refs):
        first_refs, refs = refs[:pairs], refs[pairs:]
        out_ref, operand_ref, own_buf, one_buf, first_buf, stage, one_sem, first_sem, own_sem, out_sem = refs
        first_copies = load_pairs(z, me_ref[0], first_refs, first_buf, first_sem)
        one_copies = [pltpu.make_async_copy(one_ref.at[e], one_buf.at[e], one_sem.at[e]) for e in range(z.segments)]
        own_copy = pltpu.make_async_copy(own_ref, own_buf, own_sem)
        for copy in first_copies + [own_copy] + one_copies:
            copy.start()
        for copy in first_copies:
            copy.wait()
        sends = []

        def put(i, e, value):
            for j in range(z.rows):
                rows = pl.ds(e * z.rows + j, z.nodes, stride=radial)
                stage[i, rows, :] = value[: z.nodes, j * z.ax : (j + 1) * z.ax]

        def send(i):
            copy = pltpu.make_async_copy(stage.at[i], out_ref.at[i], out_sem.at[i])
            copy.start()
            sends.append(copy)

        for e in range(z.segments):
            field = read_exact(z, first_buf, (e,), 0)
            empty = jnp.zeros((z.pad - z.nodes, z.cols), F32)
            operand_ref[e] = operand_right(jnp.concatenate([field, empty], axis=0))
            put(0, e, field)
        send(0)
        own_copy.wait()
        for copy in one_copies:
            copy.wait()
        for i in range(low, high):
            matrix = operand_left(own_buf[i])
            for e in range(z.segments):
                value = product(matrix, operand_ref[e])[: z.nodes]
                put(i, e, value + read_exact(z, one_buf, (e,), (i - low) * z.height))
            send(i)
        for copy in sends:
            copy.wait()

    return call(
        kernel,
        "finish_0",
        [f32(z.steps, tall, z.ax), jax.ShapeDtypeStruct(operand_shape, BF16)],
        [spec_smem()] + [spec_hbm()] * (2 + pairs),
        [spec_hbm(), spec_vmem()],
        [
            pltpu.VMEM((z.steps, z.pad, z.pad), F32),
            pltpu.VMEM(received_one.shape, F32),
            pltpu.VMEM((z.segments, message, z.ax), F32),
            pltpu.VMEM((high, tall, z.ax), F32),
            pltpu.SemaphoreType.DMA((z.segments,)),
            pltpu.SemaphoreType.DMA((z.segments,)),
            pltpu.SemaphoreType.DMA,
            pltpu.SemaphoreType.DMA((high,)),
        ],
        z.flops * (high - 1) * z.segments,
        4 * 2 * high * tall * z.ax,
    )(me, own, received_one, *received_first)


def finish_call(z, chunk, me, own, messages, operands, out):
    low, high = chunk
    count = high - low
    radial = z.segments * z.rows
    tall = z.nodes * radial
    message = messages[0].shape[1]

    def kernel(me_ref, own_ref, operand_ref, *refs):
        message_refs, refs = refs[: len(messages)], refs[len(messages) :]
        _, out_ref, buf, own_buf, operand_buf, stage, sem, in_sem, out_sem = refs
        own_copy = pltpu.make_async_copy(own_ref.at[pl.ds(low, count)], own_buf, in_sem.at[0])
        operand_copy = pltpu.make_async_copy(operand_ref, operand_buf, in_sem.at[1])
        own_copy.start()
        operand_copy.start()
        copies = load_pairs(z, me_ref[0], message_refs, buf, sem)
        for copy in copies:
            copy.start()
        own_copy.wait()
        operand_copy.wait()
        for copy in copies:
            copy.wait()
        sends = []
        for n in range(count):
            matrix = operand_left(own_buf[n])
            for e in range(z.segments):
                value = product(matrix, operand_buf[e])[: z.nodes] + read_exact(z, buf, (e,), n * z.height)
                for j in range(z.rows):
                    rows = pl.ds(e * z.rows + j, z.nodes, stride=radial)
                    stage[n, rows, :] = value[:, j * z.ax : (j + 1) * z.ax]
            copy = pltpu.make_async_copy(stage.at[n], out_ref.at[low + n], out_sem.at[n])
            copy.start()
            sends.append(copy)
        for copy in sends:
            copy.wait()

    inputs = [me, own, operands] + list(messages) + [out]
    return call(
        kernel,
        f"finish_{low}",
        f32(z.steps, tall, z.ax),
        [spec_smem()] + [spec_hbm()] * (len(inputs) - 1),
        spec_hbm(),
        [
            pltpu.VMEM((z.segments, message, z.ax), F32),
            pltpu.VMEM((count, z.pad, z.pad), F32),
            pltpu.VMEM(operands.shape, BF16),
            pltpu.VMEM((count, tall, z.ax), F32),
            pltpu.SemaphoreType.DMA((z.segments,)),
            pltpu.SemaphoreType.DMA((2,)),
            pltpu.SemaphoreType.DMA((count,)),
        ],
        z.flops * count * z.segments,
        4 * 2 * count * tall * z.ax,
        {len(inputs) - 1: 0},
    )(*inputs)


def close_call(z, step, me, own, messages, operands, out):
    radial = z.segments * z.rows
    tall = z.nodes * radial
    pairs = z.segments // 2

    def kernel(me_ref, own_ref, operand_ref, *refs):
        message_refs = refs[:pairs]
        _, out_ref, stage, out_sem = refs[pairs:]
        matrix = operand_left(own_ref[step])
        mine = me_ref[0]
        side = lax.rem(mine, 2)
        for d in range(pairs):
            pair = lax.rem(mine // 2 - d + pairs, pairs) * 2
            for n in range(2):
                e = pair + (side if n == 0 else 1 - side)
                value = product(matrix, operand_ref[e])[: z.nodes] + read_exact(z, message_refs[d], (n,), 0)
                for j in range(z.rows):
                    rows = pl.ds(e * z.rows + j, z.nodes, stride=radial)
                    stage[rows, :] = value[:, j * z.ax : (j + 1) * z.ax]
        copy = pltpu.make_async_copy(stage, out_ref.at[step], out_sem)
        copy.start()
        copy.wait()

    inputs = [me, own, operands] + list(messages) + [out]
    return call(
        kernel,
        f"finish_{step}",
        f32(z.steps, tall, z.ax),
        [spec_smem()] + [spec_vmem()] * (2 + pairs) + [spec_hbm()],
        spec_hbm(),
        [pltpu.VMEM((tall, z.ax), F32), pltpu.SemaphoreType.DMA],
        z.flops * z.segments,
        4 * 2 * tall * z.ax,
        {len(inputs) - 1: 0},
        limit=36,
    )(*inputs)


def shift_by(array, axis, by):
    size = lax.axis_size(axis)
    return lax.ppermute(array, axis, [(i, (i + by) % size) for i in range(size)])


def neighbours(head, tail):
    size = lax.axis_size("elem")
    left = lax.ppermute(tail, "elem", [(i, i + 1) for i in range(size - 1)])
    right = lax.ppermute(head, "elem", [(i + 1, i) for i in range(size - 1)])
    return left, right


def spread(messages):
    return lax.all_to_all(messages, "elem", 0, 0, tiled=True)


def spread_pairs(z, keep, give, after):
    got = lax.ppermute(give, "elem", [(i, i ^ 1) for i in range(z.segments)])
    coupled = couple_call(z, keep, got)
    moved = [coupled[0]]
    for d in range(1, z.segments // 2):
        held = coupled[d] if after is None else gate_call(coupled[d], after[d])
        moved.append(shift_by(held, "elem", 2 * d))
    return moved


def chunks_of(steps):
    middle = 4 if steps >= 8 else 2
    last = steps - 1
    parts = [(middle, last), (last, steps)] if last > middle else [(middle, steps)]
    return (1, middle), (middle, steps), parts


def body(state, rhs, to_modal, viscous_op, sweep_gain, inv_blocks):
    segments = lax.axis_size("elem")
    groups = lax.axis_size("blk")
    z = Sizes(state, segments, groups)
    state = state.reshape(segments, z.steps * z.height, z.ax)
    rhs = rhs.reshape(segments, z.steps * z.height, z.ax)
    gain = jnp.transpose(sweep_gain, (1, 0, 2))
    inverse = jnp.transpose(inv_blocks, (1, 0, 2))
    here = lax.axis_index("elem").astype(jnp.int32)
    me = here.reshape(1)
    places = jnp.stack([here, lax.axis_index("blk").astype(jnp.int32)])
    one, two, parts = chunks_of(z.steps)
    sensors, head, tail = sensor_call(z, state, to_modal)
    lefts, rights = neighbours(head, tail)

    def sweep(chunk, parts, ring, carry, after):
        return sweep_call(
            z, chunk, parts, me, state, rhs, viscous_op, gain, inverse, sensors, lefts, rights, ring, carry, after
        )

    messages_one, low, high = sweep(one, [], None, None, [])
    ring = [shift_by(high, "blk", 1), shift_by(low, "blk", -1)]
    own, heads, tails, wholes, prefix, group = maps_call(z, me, gain, [messages_one])
    *pairs, ends, starts = sweep(two, parts, ring, messages_one, [group])
    before, pack = chain_call(z, starts, ends, tails, wholes, group)
    packs = [pack] + [shift_by(pack, "blk", s) for s in range(1, groups)]
    keep_first, give_first = first_call(z, places, packs, before, prefix, heads, starts)
    received_one = spread(messages_one)
    received_first = spread_pairs(z, keep_first, give_first, None)
    out, operands = open_call(z, one, me, own, received_one, received_first)
    after = received_first
    for n, part in enumerate(parts):
        received = spread_pairs(z, pairs[2 * n], pairs[2 * n + 1], after)
        if part == (z.steps - 1, z.steps):
            out = close_call(z, part[0], me, own, received, operands, out)
        else:
            out = finish_call(z, part, me, own, received, operands, out)
        after = [received[1]] * len(received)
    return out.reshape(z.steps, z.nodes, segments * z.rows, z.ax)


def solution(mesh):
    in_specs = (
        P("blk", None, "elem", None),
        P("blk", None, "elem", None),
        P(),
        P(),
        P("blk", None, None),
        P("blk", None, None),
    )
    out_specs = P(("blk", "elem"), None, None, None)
    return jax.shard_map(body, mesh=mesh, in_specs=in_specs, out_specs=out_specs, check_vma=False)
```

```python
import functools

import jax
import jax.numpy as jnp
from jax import lax
from jax.experimental import pallas as pl
from jax.experimental.pallas import tpu as pltpu
from jax.sharding import PartitionSpec as P

ORDER = 4
F32 = jnp.float32
BF16 = jnp.bfloat16
MIB = 1024 * 1024
TILE = 8
LANES = 128


def operand_left(a):
    high = a.astype(BF16)
    low = (a - high.astype(F32)).astype(BF16)
    return jnp.concatenate([jnp.concatenate([high, high], axis=1), jnp.concatenate([low, low], axis=1)], axis=0)


def operand_right(x):
    high = x.astype(BF16)
    return jnp.concatenate([high, (x - high.astype(F32)).astype(BF16)], axis=0)


def product(left, right):
    both = jnp.dot(left, right, preferred_element_type=F32)
    half = left.shape[0] // 2
    return both[:half] + both[half:]


def spec_any():
    return pl.BlockSpec(memory_space=pl.ANY)


def spec_hbm():
    return pl.BlockSpec(memory_space=pltpu.HBM)


def spec_vmem():
    return pl.BlockSpec(memory_space=pltpu.VMEM)


def spec_smem():
    return pl.BlockSpec(memory_space=pltpu.SMEM)


def call(kernel, name, outs, in_specs, out_specs, scratch, flops, nbytes, aliases=None, limit=57):
    return pl.pallas_call(
        kernel,
        name=name,
        out_shape=outs,
        in_specs=in_specs,
        out_specs=out_specs,
        scratch_shapes=scratch,
        input_output_aliases=aliases or {},
        compiler_params=pltpu.CompilerParams(vmem_limit_bytes=limit * MIB),
        cost_estimate=pl.CostEstimate(flops=int(flops), bytes_accessed=int(nbytes), transcendentals=0),
    )


def f32(*shape):
    return jax.ShapeDtypeStruct(shape, F32)


def up(value, unit):
    return -(-value // unit) * unit


class Sizes:
    def __init__(self, state, segments, groups):
        count, self.nodes, self.rows, self.ax = state.shape
        self.count = count
        self.segments = segments
        self.groups = groups
        self.steps = count // segments
        self.cols = self.rows * self.ax
        self.height = self.nodes * self.rows
        self.pad = up(self.nodes, LANES)
        self.spill = up((self.pad - self.nodes) * self.rows, TILE)
        self.tail = up((self.pad - self.nodes) * segments * self.rows, TILE)
        self.flops = 2 * 4 * self.pad * self.pad * self.cols

    def window(self, low, high):
        first = low * self.height // TILE * TILE
        return first, up(high * self.height, TILE) - first

    def message(self, count):
        return up(count * self.height, TILE)

    def rows_masked(self, x):
        cut = self.nodes // TILE * TILE
        rest = x[cut:]
        inside = lax.broadcasted_iota(jnp.int32, rest.shape, 0) < self.nodes - cut
        return jnp.concatenate([x[:cut], jnp.where(inside, rest, 0.0)], axis=0)

    def square(self, x):
        x = jnp.concatenate([x, jnp.zeros((self.nodes, self.pad - self.nodes), F32)], axis=1)
        return jnp.concatenate([x, jnp.zeros((self.pad - self.nodes, self.pad), F32)], axis=0)


def read_field(z, ref, lead, offset):
    parts = [ref[lead + (pl.ds(offset + j, z.pad, stride=z.rows), slice(None))] for j in range(z.rows)]
    return z.rows_masked(jnp.concatenate(parts, axis=1))


def read_exact(z, ref, lead, offset):
    parts = [ref[lead + (pl.ds(offset + j, z.nodes, stride=z.rows), slice(None))] for j in range(z.rows)]
    return jnp.concatenate(parts, axis=1)


def write_field(z, ref, lead, offset, value):
    for j in range(z.rows):
        rows = pl.ds(offset + j, z.nodes, stride=z.rows)
        ref[lead + (rows, slice(None))] = value[: z.nodes, j * z.ax : (j + 1) * z.ax]


def read_matrix(z, ref, k):
    x = z.rows_masked(ref[:, k, :])
    return jnp.concatenate([x, jnp.zeros((z.pad, z.pad - z.nodes), F32)], axis=1)


def send_pair(z, mine, e, stage, keep_ref, give_ref, sem):
    pairs = z.segments // 2
    place = lax.rem(e // 2 - mine // 2 + pairs, pairs)
    own = lax.rem(mine, 2) == e % 2
    source = stage.at[e, pl.ds(0, keep_ref.shape[1])]

    @pl.when(own)
    def _():
        pltpu.make_async_copy(source, keep_ref.at[place], sem.at[e]).start()

    @pl.when(jnp.logical_not(own))
    def _():
        pltpu.make_async_copy(source, give_ref.at[place], sem.at[e]).start()

    return pltpu.make_async_copy(source, keep_ref.at[place], sem.at[e])


def load_pairs(z, mine, sources, buf, sem):
    pairs = z.segments // 2
    side = lax.rem(mine, 2)
    copies = []
    for d in range(pairs):
        pair = lax.rem(mine // 2 - d + pairs, pairs) * 2
        for n in range(2):
            e = pair + (side if n == 0 else 1 - side)
            target = buf.at[e, pl.ds(0, sources[d].shape[1])]
            copies.append(pltpu.make_async_copy(sources[d].at[n], target, sem.at[2 * d + n]))
    return copies


def sensor_call(z, state, to_modal):
    batch = 4 if z.segments % 4 == 0 else 1
    tall = z.steps * z.height

    def kernel(state_ref, modal_ref, sensor_ref, head_ref, tail_ref, buf, modal_buf, sem, modal_sem):
        modal_copy = pltpu.make_async_copy(modal_ref, modal_buf, modal_sem)
        modal_copy.start()
        copies = [
            pltpu.make_async_copy(state_ref.at[e], buf.at[e, pl.ds(0, tall)], sem.at[e]) for e in range(z.segments)
        ]
        for copy in copies:
            copy.start()
        modal_copy.wait()
        matrix = operand_left(z.square(modal_buf[...]))
        for e0 in range(0, z.segments, batch):
            for e in range(e0, e0 + batch):
                copies[e].wait()
            for e in range(e0, e0 + batch):
                for i in range(z.steps):
                    modal = product(matrix, operand_right(read_field(z, buf, (e,), i * z.height)))
                    squares = modal * modal
                    lower = jnp.sum(squares[: ORDER**3], axis=0, keepdims=True)
                    upper = jnp.sum(squares[ORDER**3 :], axis=0, keepdims=True)
                    sensor = (upper / z.nodes) / ((lower + upper) / z.nodes + 1e-6)
                    sensor_ref[i, e : e + 1, :] = sensor
                    head_ref[i, e : e + 1, :] = sensor[:, : z.ax]
                    tail_ref[i, e : e + 1, :] = sensor[:, z.cols - z.ax :]

    outs = [f32(z.steps, z.segments, z.cols)] + [f32(z.steps, z.segments, z.ax)] * 2
    return call(
        kernel,
        "sensor",
        outs,
        [spec_hbm()] * 2,
        [spec_vmem()] * 3,
        [
            pltpu.VMEM((z.segments, tall + z.spill, z.ax), F32),
            pltpu.VMEM((z.nodes, z.nodes), F32),
            pltpu.SemaphoreType.DMA((z.segments,)),
            pltpu.SemaphoreType.DMA,
        ],
        z.flops * z.steps * z.segments,
        4 * z.segments * tall * z.ax,
        limit=52,
    )(state, to_modal)


def smoothed(z, sensor, before, after, left, right):
    inner = sensor[:, : z.cols - z.ax]
    outer = sensor[:, z.ax :]
    from_left = jnp.concatenate([left, inner], axis=1)
    from_right = jnp.concatenate([outer, right], axis=1)
    return (4.0 * sensor + before + after + from_left + from_right) / 8.0


def sweep_call(z, chunk, parts, me, state, rhs, viscous, gain, inverse, sensors, lefts, rights, ring, carry, after):
    low, high = chunk
    opened = high == z.steps
    first, size = z.window(low, high)
    count = high - low
    first0, size0 = z.window(0, 1)
    steps = list(range(low, high)) + ([0] if opened else [])
    has_carry = carry is not None
    gains = list(range(low if has_carry else low + 1, high))
    messages = [z.message(stop - start) for start, stop in parts or [chunk]]
    edge_outs = low == 1
    pairs = z.segments // 2
    last, last_size = z.window(low - 2, low - 1)
    batch = next(n for n in (4, 8, z.segments) if z.segments % n == 0 and n * z.steps % TILE == 0)
    narrow = low == 1
    cuts = list(range(0, z.segments + 1, batch))
    if narrow:
        cuts[1:1] = [2]
    batches = list(zip(cuts[:-1], cuts[1:]))

    if parts:
        outs = [f32(pairs, message, z.ax) for message in messages for _ in range(2)]
    else:
        outs = [f32(z.segments, messages[0], z.ax)]

    def kernel(*refs):
        me_ref, state_ref, rhs_ref, viscous_ref, inverse_ref, gain_ref, sensor_ref, left_ref, right_ref = refs[:9]
        refs = refs[9:]
        if opened:
            before_ref, behind_ref, refs = refs[0], refs[1], refs[2:]
        if has_carry:
            carry_ref, refs = refs[0], refs[1:]
        refs = refs[len(after) :]
        out_refs, refs = refs[: len(outs)], refs[len(outs) :]
        if opened:
            end_ref, start_ref, refs = refs[0], refs[1], refs[2:]
        if edge_outs:
            low_ref, high_ref, refs = refs[0], refs[1], refs[2:]
        state_buf, rhs_buf, inverse_buf, gain_buf, viscous_buf, smooth_buf, sem, matrix_sem, out_sem = refs[:9]
        stages, refs = refs[9 : 9 + len(messages)], refs[9 + len(messages) :]
        if opened:
            state0, rhs0, refs = refs[0], refs[1], refs[2:]
        if has_carry:
            carry_buf = refs[0]
        viscous_copy = pltpu.make_async_copy(viscous_ref, viscous_buf, out_sem.at[0, 0])
        viscous_copy.start()
        copies = [[] for _ in range(z.segments)]
        for s0, s1 in batches:
            for s in range(s0, s1):
                moves = [
                    (state_ref.at[s, pl.ds(first, size)], state_buf.at[s, pl.ds(0, size)]),
                    (rhs_ref.at[s, pl.ds(first, size)], rhs_buf.at[s, pl.ds(0, size)]),
                ]
                if opened:
                    moves.append((state_ref.at[s, pl.ds(first0, size0)], state0.at[s, pl.ds(0, size0)]))
                    moves.append((rhs_ref.at[s, pl.ds(first0, size0)], rhs0.at[s, pl.ds(0, size0)]))
                if has_carry:
                    moves.append((carry_ref.at[s, pl.ds(last, last_size)], carry_buf.at[s, pl.ds(0, last_size)]))
                if narrow:
                    for source, target, needed in ((inverse_ref, inverse_buf, steps), (gain_ref, gain_buf, gains)):
                        if needed:
                            part = pl.ds(s * z.steps + needed[0], len(needed))
                            moves.append((source.at[:, part], target.at[pl.ds(0, z.nodes), part]))
                for n, (source, target) in enumerate(moves):
                    copies[s].append(pltpu.make_async_copy(source, target, sem.at[s, n]))
            if not narrow:
                part = pl.ds(s0 * z.steps, (s1 - s0) * z.steps)
                for n, (source, target) in enumerate(((inverse_ref, inverse_buf), (gain_ref, gain_buf))):
                    copy = pltpu.make_async_copy(
                        source.at[:, part], target.at[pl.ds(0, z.nodes), part], matrix_sem.at[s0, n]
                    )
                    copies[s0].append(copy)
            for s in range(s0, s1):
                for copy in copies[s]:
                    copy.start()
        for n, i in enumerate(steps):
            before = sensor_ref[(i - 1) % z.steps]
            later = sensor_ref[(i + 1) % z.steps]
            if i == 0:
                before = jnp.concatenate([before_ref[...], before[: z.segments - 1]], axis=0)
            if i == z.steps - 1:
                later = jnp.concatenate([later[1:], behind_ref[...]], axis=0)
            smooth_buf[n] = smoothed(z, sensor_ref[i], before, later, left_ref[i], right_ref[i])
        if edge_outs:
            low_ref[...] = sensor_ref[0, :1]
            high_ref[...] = sensor_ref[z.steps - 1, z.segments - 1 :]
        viscous_copy.wait()
        operator = operand_left(z.square(viscous_buf[...]))
        sends = []

        for s0, s1 in batches:
            group = range(s0, s1)
            for s in group:
                for copy in copies[s]:
                    copy.wait()
            sources = []
            for n, i in enumerate(steps):
                bufs = (state0, rhs0, -first0) if i == 0 else (state_buf, rhs_buf, i * z.height - first)
                moved = [product(operator, operand_right(read_field(z, bufs[0], (s,), bufs[2]))) for s in group]
                forces = [
                    operand_right(read_field(z, bufs[1], (s,), bufs[2]) + smooth_buf[n, s : s + 1, :] * value)
                    for s, value in zip(group, moved)
                ]
                sources.append(forces)
            for n, i in enumerate(steps):
                sources[n] = [
                    product(operand_left(read_matrix(z, inverse_buf, s * z.steps + i)), force)
                    for s, force in zip(group, sources[n])
                ]
            fields = None
            if has_carry:
                fields = [read_field(z, carry_buf, (s,), (low - 2) * z.height - last) for s in group]
            for n, i in enumerate(steps):
                values = sources[n]
                if i == 0:
                    for s, value in zip(group, values):
                        start_ref[s] = value
                    continue
                if fields is not None:
                    swept = [
                        product(operand_left(read_matrix(z, gain_buf, s * z.steps + i)), operand_right(field))
                        for s, field in zip(group, fields)
                    ]
                    values = [value + more for value, more in zip(values, swept)]
                fields = values
                for s, value in zip(group, values):
                    for (start, stop), stage in zip(parts or [chunk], stages):
                        if start <= i < stop:
                            write_field(z, stage, (s,), (i - start) * z.height, value)
            for s, value in zip(group, fields):
                if opened:
                    end_ref[s] = value
                if not parts:
                    copy = pltpu.make_async_copy(
                        stages[0].at[s, pl.ds(0, messages[0])], out_refs[0].at[s], out_sem.at[0, s]
                    )
                    copy.start()
                    sends.append(copy)
            for p, stage in enumerate(stages if parts else []):
                for s in group:
                    keep_ref, give_ref = out_refs[2 * p], out_refs[2 * p + 1]
                    sends.append(send_pair(z, me_ref[0], s, stage, keep_ref, give_ref, out_sem.at[p]))
        for copy in sends:
            copy.wait()

    field = f32(z.segments, z.pad, z.cols)
    out_specs = [spec_hbm()] * len(outs)
    more = [field] * (2 if opened else 0) + ([f32(1, z.cols)] * 2 if edge_outs else [])
    operands = [me, state, rhs, viscous, inverse, gain, sensors, lefts, rights]
    in_specs = [spec_smem()] + [spec_hbm()] * 5 + [spec_vmem()] * 3
    extra = list(ring) if opened else []
    extra_specs = [spec_vmem()] * len(extra)
    if has_carry:
        extra.append(carry)
        extra_specs.append(spec_hbm())
    scratch = [
        pltpu.VMEM((z.segments, size + z.spill, z.ax), F32),
        pltpu.VMEM((z.segments, size + z.spill, z.ax), F32),
        pltpu.VMEM((z.pad,) + inverse.shape[1:], F32),
        pltpu.VMEM((z.pad,) + gain.shape[1:], F32),
        pltpu.VMEM(viscous.shape, F32),
        pltpu.VMEM((len(steps), z.segments, z.cols), F32),
        pltpu.SemaphoreType.DMA((z.segments, 7)),
        pltpu.SemaphoreType.DMA((z.segments, 2)),
        pltpu.SemaphoreType.DMA((len(messages), z.segments)),
    ]
    scratch += [pltpu.VMEM((z.segments, message + z.spill, z.ax), F32) for message in messages]
    if opened:
        scratch += [pltpu.VMEM((z.segments, size0 + z.spill, z.ax), F32)] * 2
    if has_carry:
        scratch.append(pltpu.VMEM((z.segments, last_size + z.spill, z.ax), F32))
    return call(
        kernel,
        f"sweep_{low}",
        outs + more,
        in_specs + extra_specs + [spec_any()] * len(after),
        out_specs + [spec_vmem()] * len(more),
        scratch,
        z.flops * len(steps) * z.segments * 3,
        4 * z.segments * size * z.ax * 4,
        limit=52,
    )(*operands, *extra, *after)


def maps_call(z, me, gain, after):
    def kernel(me_ref, gain_ref, *refs):
        own_ref, head_ref, tail_ref, whole_ref, prefix_ref, group_ref, gain_buf, kept, sem = refs[len(after) :]
        copy = pltpu.make_async_copy(gain_ref, gain_buf.at[pl.ds(0, z.nodes)], sem)
        copy.start()
        copy.wait()

        def times(a, b):
            return product(operand_left(a), operand_right(b))

        values = [read_matrix(z, gain_buf, e * z.steps + 1) for e in range(z.segments)]
        for i in range(1, z.steps):
            if i > 1:
                values = [
                    times(read_matrix(z, gain_buf, e * z.steps + i), values[e]) for e in range(z.segments)
                ]
            for e in range(z.segments):
                kept[e, i] = values[e]
        heads = [read_matrix(z, gain_buf, e * z.steps) for e in range(z.segments)]
        for e in range(z.segments):
            kept[e, 0] = heads[e]
            head_ref[e] = heads[e]
            tail_ref[e] = values[e]
            whole_ref[e] = times(values[e], heads[e])
        own_ref[...] = kept[me_ref[0]]
        value = whole_ref[0]
        prefix_ref[0] = value
        for e in range(1, z.segments):
            prefix_ref[e] = value
            value = times(whole_ref[e], value)
        group_ref[...] = value

    square = (z.pad, z.pad)
    outs = [f32(z.steps, *square)] + [f32(z.segments, *square)] * 4 + [f32(*square)]
    return call(
        kernel,
        "maps",
        outs,
        [spec_smem(), spec_hbm()] + [spec_any()] * len(after),
        [spec_vmem()] * 6,
        [
            pltpu.VMEM((z.pad,) + gain.shape[1:], F32),
            pltpu.VMEM((z.segments, z.steps) + square, F32),
            pltpu.SemaphoreType.DMA,
        ],
        z.flops * z.segments * (z.steps + 1) // 2,
        4 * z.segments * z.steps * z.pad * z.pad,
        limit=52,
    )(me, gain, *after)


def chain_call(z, starts, ends, tails, wholes, group):
    def kernel(start_ref, end_ref, tail_ref, whole_ref, group_ref, before_ref, pack_ref):
        value = None
        for e in range(z.segments):
            shift = end_ref[e] + product(operand_left(tail_ref[e]), operand_right(start_ref[e]))
            if e > 0:
                before_ref[e] = value
                shift = shift + product(operand_left(whole_ref[e]), operand_right(value))
            else:
                before_ref[0] = jnp.zeros_like(shift)
            value = shift
        pack_ref[:, : z.cols] = value
        pack_ref[:, z.cols :] = group_ref[...]

    return call(
        kernel,
        "chain",
        [f32(z.segments, z.pad, z.cols), f32(z.pad, z.cols + z.pad)],
        [spec_vmem()] * 5,
        [spec_vmem()] * 2,
        [],
        z.flops * z.segments * 2,
        4 * z.segments * z.pad * z.cols * 4,
    )(starts, ends, tails, wholes, group)


def first_call(z, places, packs, before, prefix, heads, starts):
    rows = z.message(1)
    pairs = z.segments // 2

    def kernel(*refs):
        places_ref, refs = refs[0], refs[1:]
        pack_refs, refs = refs[: z.groups], refs[z.groups :]
        before_ref, prefix_ref, head_ref, start_ref, keep_ref, give_ref, stage, sem = refs
        mine = places_ref[0]
        group = places_ref[1]
        value = jnp.zeros((z.pad, z.cols), F32)
        matrices = [operand_left(ref[:, z.cols :]) for ref in pack_refs]
        for t in range(2 * z.groups - 1, 0, -1):
            n = t % z.groups
            moved = product(matrices[n], operand_right(value)) + pack_refs[n][:, : z.cols]
            value = jnp.where(t <= z.groups + group, moved, 0.0)
        incoming = operand_right(value)
        arriving = [value] + [
            before_ref[e] + product(operand_left(prefix_ref[e]), incoming) for e in range(1, z.segments)
        ]
        solved = [
            start_ref[e] + product(operand_left(head_ref[e]), operand_right(arriving[e])) for e in range(z.segments)
        ]
        for e in range(z.segments):
            write_field(z, stage, (e,), 0, solved[e])
        sends = [send_pair(z, mine, e, stage, keep_ref, give_ref, sem) for e in range(z.segments)]
        for copy in sends:
            copy.wait()

    return call(
        kernel,
        "first",
        [f32(pairs, rows, z.ax)] * 2,
        [spec_smem()] + [spec_vmem()] * (z.groups + 4),
        [spec_hbm()] * 2,
        [pltpu.VMEM((z.segments, rows + z.spill, z.ax), F32), pltpu.SemaphoreType.DMA((z.segments,))],
        z.flops * (z.segments * 2 + 2 * z.groups),
        4 * z.segments * z.pad * z.cols * 4,
    )(places, *packs, before, prefix, heads, starts)


def couple_call(z, keep, got):
    pairs, message, _ = keep.shape

    def kernel(*refs):
        sources, refs = refs[:2], refs[2:]
        outs, buf, sem = refs[:pairs], refs[pairs], refs[pairs + 1]
        loads = [
            [pltpu.make_async_copy(sources[n].at[d], buf.at[d, n], sem.at[d, n]) for n in range(2)]
            for d in range(pairs)
        ]
        for load in loads:
            for copy in load:
                copy.start()
        stores = []
        for d in range(pairs):
            for copy in loads[d]:
                copy.wait()
            copy = pltpu.make_async_copy(buf.at[d], outs[d], sem.at[d, 0])
            copy.start()
            stores.append(copy)
        for copy in stores:
            copy.wait()

    return call(
        kernel,
        "couple",
        [f32(2, message, z.ax)] * pairs,
        [spec_hbm()] * 2,
        [spec_hbm()] * pairs,
        [pltpu.VMEM((pairs, 2, message, z.ax), F32), pltpu.SemaphoreType.DMA((pairs, 2))],
        0,
        4 * 4 * pairs * message * z.ax,
    )(keep, got)


def gate_call(held, after):
    def kernel(*refs):
        pass

    return call(
        kernel,
        "gate",
        f32(*held.shape),
        [spec_hbm(), spec_any()],
        spec_hbm(),
        [],
        0,
        0,
        {0: 0},
    )(held, after)


def open_call(z, one, me, own, received_one, received_first):
    radial = z.segments * z.rows
    tall = z.nodes * radial
    operand_shape = (z.segments, 2 * z.pad, z.cols)
    low, high = one
    pairs = z.segments // 2
    message = received_first[0].shape[1]

    def kernel(me_ref, own_ref, one_ref, *refs):
        first_refs, refs = refs[:pairs], refs[pairs:]
        out_ref, operand_ref, own_buf, one_buf, first_buf, stage, one_sem, first_sem, own_sem, out_sem = refs
        first_copies = load_pairs(z, me_ref[0], first_refs, first_buf, first_sem)
        one_copies = [
            pltpu.make_async_copy(one_ref.at[e], one_buf.at[e, pl.ds(0, one_ref.shape[1])], one_sem.at[e])
            for e in range(z.segments)
        ]
        own_copy = pltpu.make_async_copy(own_ref, own_buf, own_sem)
        for copy in first_copies + [own_copy] + one_copies:
            copy.start()
        for copy in first_copies:
            copy.wait()
        sends = []

        def put(i, e, value):
            for j in range(z.rows):
                rows = pl.ds(e * z.rows + j, z.nodes, stride=radial)
                stage[i, rows, :] = value[: z.nodes, j * z.ax : (j + 1) * z.ax]

        def send(i):
            copy = pltpu.make_async_copy(stage.at[i, pl.ds(0, tall)], out_ref.at[i], out_sem.at[i])
            copy.start()
            sends.append(copy)

        for e in range(z.segments):
            field = read_exact(z, first_buf, (e,), 0)
            empty = jnp.zeros((z.pad - z.nodes, z.cols), F32)
            operand_ref[e] = operand_right(jnp.concatenate([field, empty], axis=0))
            put(0, e, field)
        send(0)
        own_copy.wait()
        for copy in one_copies:
            copy.wait()
        for i in range(low, high):
            matrix = operand_left(own_buf[i])
            for e in range(z.segments):
                value = product(matrix, operand_ref[e])[: z.nodes]
                put(i, e, value + read_exact(z, one_buf, (e,), (i - low) * z.height))
            send(i)
        for copy in sends:
            copy.wait()

    return call(
        kernel,
        "finish_0",
        [f32(z.steps, tall, z.ax), jax.ShapeDtypeStruct(operand_shape, BF16)],
        [spec_smem()] + [spec_hbm()] * (2 + pairs),
        [spec_hbm(), spec_vmem()],
        [
            pltpu.VMEM((z.steps, z.pad, z.pad), F32),
            pltpu.VMEM((z.segments, received_one.shape[1] + z.spill, z.ax), F32),
            pltpu.VMEM((z.segments, message + z.spill, z.ax), F32),
            pltpu.VMEM((high, tall + z.tail, z.ax), F32),
            pltpu.SemaphoreType.DMA((z.segments,)),
            pltpu.SemaphoreType.DMA((z.segments,)),
            pltpu.SemaphoreType.DMA,
            pltpu.SemaphoreType.DMA((high,)),
        ],
        z.flops * (high - 1) * z.segments,
        4 * 2 * high * tall * z.ax,
    )(me, own, received_one, *received_first)


def finish_call(z, chunk, me, own, messages, operands, out):
    low, high = chunk
    count = high - low
    radial = z.segments * z.rows
    tall = z.nodes * radial
    message = messages[0].shape[1]

    def kernel(me_ref, own_ref, operand_ref, *refs):
        message_refs, refs = refs[: len(messages)], refs[len(messages) :]
        _, out_ref, buf, own_buf, operand_buf, stage, sem, in_sem, out_sem = refs
        own_copy = pltpu.make_async_copy(own_ref.at[pl.ds(low, count)], own_buf, in_sem.at[0])
        operand_copy = pltpu.make_async_copy(operand_ref, operand_buf, in_sem.at[1])
        own_copy.start()
        operand_copy.start()
        copies = load_pairs(z, me_ref[0], message_refs, buf, sem)
        for copy in copies:
            copy.start()
        own_copy.wait()
        operand_copy.wait()
        for copy in copies:
            copy.wait()
        sends = []
        for n in range(count):
            matrix = operand_left(own_buf[n])
            for e in range(z.segments):
                value = product(matrix, operand_buf[e])[: z.nodes] + read_exact(z, buf, (e,), n * z.height)
                for j in range(z.rows):
                    rows = pl.ds(e * z.rows + j, z.nodes, stride=radial)
                    stage[n, rows, :] = value[:, j * z.ax : (j + 1) * z.ax]
            copy = pltpu.make_async_copy(stage.at[n, pl.ds(0, tall)], out_ref.at[low + n], out_sem.at[n])
            copy.start()
            sends.append(copy)
        for copy in sends:
            copy.wait()

    inputs = [me, own, operands] + list(messages) + [out]
    return call(
        kernel,
        f"finish_{low}",
        f32(z.steps, tall, z.ax),
        [spec_smem()] + [spec_hbm()] * (len(inputs) - 1),
        spec_hbm(),
        [
            pltpu.VMEM((z.segments, message + z.spill, z.ax), F32),
            pltpu.VMEM((count, z.pad, z.pad), F32),
            pltpu.VMEM(operands.shape, BF16),
            pltpu.VMEM((count, tall + z.tail, z.ax), F32),
            pltpu.SemaphoreType.DMA((z.segments,)),
            pltpu.SemaphoreType.DMA((2,)),
            pltpu.SemaphoreType.DMA((count,)),
        ],
        z.flops * count * z.segments,
        4 * 2 * count * tall * z.ax,
        {len(inputs) - 1: 0},
    )(*inputs)


def close_call(z, step, me, own, messages, operands, out):
    radial = z.segments * z.rows
    tall = z.nodes * radial
    pairs = z.segments // 2

    def kernel(me_ref, own_ref, operand_ref, *refs):
        message_refs = refs[:pairs]
        _, out_ref, stage, out_sem = refs[pairs:]
        matrix = operand_left(own_ref[step])
        mine = me_ref[0]
        side = lax.rem(mine, 2)
        for d in range(pairs):
            pair = lax.rem(mine // 2 - d + pairs, pairs) * 2
            for n in range(2):
                e = pair + (side if n == 0 else 1 - side)
                value = product(matrix, operand_ref[e])[: z.nodes] + read_exact(z, message_refs[d], (n,), 0)
                for j in range(z.rows):
                    rows = pl.ds(e * z.rows + j, z.nodes, stride=radial)
                    stage[rows, :] = value[:, j * z.ax : (j + 1) * z.ax]
        copy = pltpu.make_async_copy(stage.at[pl.ds(0, tall)], out_ref.at[step], out_sem)
        copy.start()
        copy.wait()

    inputs = [me, own, operands] + list(messages) + [out]
    return call(
        kernel,
        f"finish_{step}",
        f32(z.steps, tall, z.ax),
        [spec_smem()] + [spec_vmem()] * (2 + pairs) + [spec_hbm()],
        spec_hbm(),
        [pltpu.VMEM((tall + z.tail, z.ax), F32), pltpu.SemaphoreType.DMA],
        z.flops * z.segments,
        4 * 2 * tall * z.ax,
        {len(inputs) - 1: 0},
        limit=36,
    )(*inputs)


def shift_by(array, axis, by):
    size = lax.axis_size(axis)
    return lax.ppermute(array, axis, [(i, (i + by) % size) for i in range(size)])


def neighbours(head, tail):
    size = lax.axis_size("elem")
    left = lax.ppermute(tail, "elem", [(i, i + 1) for i in range(size - 1)])
    right = lax.ppermute(head, "elem", [(i + 1, i) for i in range(size - 1)])
    return left, right


def spread(messages):
    return lax.all_to_all(messages, "elem", 0, 0, tiled=True)


def spread_pairs(z, keep, give, after):
    got = lax.ppermute(give, "elem", [(i, i ^ 1) for i in range(z.segments)])
    coupled = couple_call(z, keep, got)
    moved = [coupled[0]]
    for d in range(1, z.segments // 2):
        held = coupled[d] if after is None else gate_call(coupled[d], after[d])
        moved.append(shift_by(held, "elem", 2 * d))
    return moved


def chunks_of(steps):
    middle = 4 if steps >= 8 else 2
    last = steps - 1
    parts = [(middle, last), (last, steps)] if last > middle else [(middle, steps)]
    return (1, middle), (middle, steps), parts


def body(state, rhs, to_modal, viscous_op, sweep_gain, inv_blocks):
    segments = lax.axis_size("elem")
    groups = lax.axis_size("blk")
    z = Sizes(state, segments, groups)
    state = state.reshape(segments, z.steps * z.height, z.ax)
    rhs = rhs.reshape(segments, z.steps * z.height, z.ax)
    gain = jnp.transpose(sweep_gain, (1, 0, 2))
    inverse = jnp.transpose(inv_blocks, (1, 0, 2))
    here = lax.axis_index("elem").astype(jnp.int32)
    me = here.reshape(1)
    places = jnp.stack([here, lax.axis_index("blk").astype(jnp.int32)])
    one, two, parts = chunks_of(z.steps)
    sensors, head, tail = sensor_call(z, state, to_modal)
    lefts, rights = neighbours(head, tail)

    def sweep(chunk, parts, ring, carry, after):
        return sweep_call(
            z, chunk, parts, me, state, rhs, viscous_op, gain, inverse, sensors, lefts, rights, ring, carry, after
        )

    messages_one, low, high = sweep(one, [], None, None, [])
    ring = [shift_by(high, "blk", 1), shift_by(low, "blk", -1)]
    own, heads, tails, wholes, prefix, group = maps_call(z, me, gain, [messages_one])
    *pairs, ends, starts = sweep(two, parts, ring, messages_one, [group])
    before, pack = chain_call(z, starts, ends, tails, wholes, group)
    packs = [pack] + [shift_by(pack, "blk", s) for s in range(1, groups)]
    keep_first, give_first = first_call(z, places, packs, before, prefix, heads, starts)
    received_one = spread(messages_one)
    received_first = spread_pairs(z, keep_first, give_first, None)
    out, operands = open_call(z, one, me, own, received_one, received_first)
    after = received_first
    for n, part in enumerate(parts):
        received = spread_pairs(z, pairs[2 * n], pairs[2 * n + 1], after)
        if part == (z.steps - 1, z.steps):
            out = close_call(z, part[0], me, own, received, operands, out)
        else:
            out = finish_call(z, part, me, own, received, operands, out)
        after = [received[1]] * len(received)
    return out.reshape(z.steps, z.nodes, segments * z.rows, z.ax)


def solution(mesh):
    in_specs = (
        P("blk", None, "elem", None),
        P("blk", None, "elem", None),
        P(),
        P(),
        P("blk", None, None),
        P("blk", None, None),
    )
    out_specs = P(("blk", "elem"), None, None, None)
    return jax.shard_map(body, mesh=mesh, in_specs=in_specs, out_specs=out_specs, check_vma=False)
```

```python
import functools

import jax
import jax.numpy as jnp
from jax import lax
from jax.experimental import pallas as pl
from jax.experimental.pallas import tpu as pltpu
from jax.sharding import PartitionSpec as P

ORDER = 4
F32 = jnp.float32
BF16 = jnp.bfloat16
MIB = 1024 * 1024
TILE = 8
LANES = 128


def operand_left(a):
    high = a.astype(BF16)
    low = (a - high.astype(F32)).astype(BF16)
    return jnp.concatenate([jnp.concatenate([high, high], axis=1), jnp.concatenate([low, low], axis=1)], axis=0)


def operand_right(x):
    high = x.astype(BF16)
    return jnp.concatenate([high, (x - high.astype(F32)).astype(BF16)], axis=0)


def product(left, right):
    both = jnp.dot(left, right, preferred_element_type=F32)
    half = left.shape[0] // 2
    return both[:half] + both[half:]


def spec_any():
    return pl.BlockSpec(memory_space=pl.ANY)


def spec_hbm():
    return pl.BlockSpec(memory_space=pltpu.HBM)


def spec_vmem():
    return pl.BlockSpec(memory_space=pltpu.VMEM)


def spec_smem():
    return pl.BlockSpec(memory_space=pltpu.SMEM)


def call(kernel, name, outs, in_specs, out_specs, scratch, flops, nbytes, aliases=None, limit=57):
    return pl.pallas_call(
        kernel,
        name=name,
        out_shape=outs,
        in_specs=in_specs,
        out_specs=out_specs,
        scratch_shapes=scratch,
        input_output_aliases=aliases or {},
        compiler_params=pltpu.CompilerParams(vmem_limit_bytes=limit * MIB),
        cost_estimate=pl.CostEstimate(flops=int(flops), bytes_accessed=int(nbytes), transcendentals=0),
    )


def f32(*shape):
    return jax.ShapeDtypeStruct(shape, F32)


def up(value, unit):
    return -(-value // unit) * unit


class Sizes:
    def __init__(self, state, segments, groups):
        count, self.nodes, self.rows, self.ax = state.shape
        self.count = count
        self.segments = segments
        self.groups = groups
        self.steps = count // segments
        self.cols = self.rows * self.ax
        self.height = self.nodes * self.rows
        self.pad = up(self.nodes, LANES)
        self.spill = up((self.pad - self.nodes) * self.rows, TILE)
        self.tail = up((self.pad - self.nodes) * segments * self.rows, TILE)
        self.flops = 2 * 4 * self.pad * self.pad * self.cols

    def window(self, low, high):
        first = low * self.height // TILE * TILE
        return first, up(high * self.height, TILE) - first

    def message(self, count):
        return up(count * self.height, TILE)

    def rows_masked(self, x):
        cut = self.nodes // TILE * TILE
        rest = x[cut:]
        inside = lax.broadcasted_iota(jnp.int32, rest.shape, 0) < self.nodes - cut
        return jnp.concatenate([x[:cut], jnp.where(inside, rest, 0.0)], axis=0)

    def square(self, x):
        x = jnp.concatenate([x, jnp.zeros((self.nodes, self.pad - self.nodes), F32)], axis=1)
        return jnp.concatenate([x, jnp.zeros((self.pad - self.nodes, self.pad), F32)], axis=0)


def read_field(z, ref, lead, offset):
    parts = [ref[lead + (pl.ds(offset + j, z.pad, stride=z.rows), slice(None))] for j in range(z.rows)]
    return z.rows_masked(jnp.concatenate(parts, axis=1))


def read_exact(z, ref, lead, offset):
    parts = [ref[lead + (pl.ds(offset + j, z.nodes, stride=z.rows), slice(None))] for j in range(z.rows)]
    return jnp.concatenate(parts, axis=1)


def write_field(z, ref, lead, offset, value):
    for j in range(z.rows):
        rows = pl.ds(offset + j, z.nodes, stride=z.rows)
        ref[lead + (rows, slice(None))] = value[: z.nodes, j * z.ax : (j + 1) * z.ax]


def read_matrix(z, ref, k):
    x = z.rows_masked(ref[:, k, :])
    return jnp.concatenate([x, jnp.zeros((z.pad, z.pad - z.nodes), F32)], axis=1)


def send_pair(z, mine, e, stage, keep_ref, give_ref, sem):
    pairs = z.segments // 2
    place = lax.rem(e // 2 - mine // 2 + pairs, pairs)
    own = lax.rem(mine, 2) == e % 2
    source = stage.at[e, pl.ds(0, keep_ref.shape[1])]

    @pl.when(own)
    def _():
        pltpu.make_async_copy(source, keep_ref.at[place], sem.at[e]).start()

    @pl.when(jnp.logical_not(own))
    def _():
        pltpu.make_async_copy(source, give_ref.at[place], sem.at[e]).start()

    return pltpu.make_async_copy(source, keep_ref.at[place], sem.at[e])


def load_pairs(z, mine, sources, buf, sem):
    pairs = z.segments // 2
    side = lax.rem(mine, 2)
    copies = []
    for d in range(pairs):
        pair = lax.rem(mine // 2 - d + pairs, pairs) * 2
        for n in range(2):
            e = pair + (side if n == 0 else 1 - side)
            target = buf.at[e, pl.ds(0, sources[d].shape[1])]
            copies.append(pltpu.make_async_copy(sources[d].at[n], target, sem.at[2 * d + n]))
    return copies


def sensor_call(z, state, to_modal):
    batch = 4 if z.segments % 4 == 0 else 1
    tall = z.steps * z.height

    def kernel(state_ref, modal_ref, sensor_ref, head_ref, tail_ref, buf, modal_buf, sem, modal_sem):
        modal_copy = pltpu.make_async_copy(modal_ref, modal_buf, modal_sem)
        modal_copy.start()
        copies = [
            pltpu.make_async_copy(state_ref.at[e], buf.at[e, pl.ds(0, tall)], sem.at[e]) for e in range(z.segments)
        ]
        for copy in copies:
            copy.start()
        modal_copy.wait()
        matrix = operand_left(z.square(modal_buf[...]))
        for e0 in range(0, z.segments, batch):
            for e in range(e0, e0 + batch):
                copies[e].wait()
            for e in range(e0, e0 + batch):
                for i in range(z.steps):
                    modal = product(matrix, operand_right(read_field(z, buf, (e,), i * z.height)))
                    squares = modal * modal
                    lower = jnp.sum(squares[: ORDER**3], axis=0, keepdims=True)
                    upper = jnp.sum(squares[ORDER**3 :], axis=0, keepdims=True)
                    sensor = (upper / z.nodes) / ((lower + upper) / z.nodes + 1e-6)
                    sensor_ref[i, e : e + 1, :] = sensor
                    head_ref[i, e : e + 1, :] = sensor[:, : z.ax]
                    tail_ref[i, e : e + 1, :] = sensor[:, z.cols - z.ax :]

    outs = [f32(z.steps, z.segments, z.cols)] + [f32(z.steps, z.segments, z.ax)] * 2
    return call(
        kernel,
        "sensor",
        outs,
        [spec_hbm()] * 2,
        [spec_vmem()] * 3,
        [
            pltpu.VMEM((z.segments, tall + z.spill, z.ax), F32),
            pltpu.VMEM((z.nodes, z.nodes), F32),
            pltpu.SemaphoreType.DMA((z.segments,)),
            pltpu.SemaphoreType.DMA,
        ],
        z.flops * z.steps * z.segments,
        4 * z.segments * tall * z.ax,
        limit=53,
    )(state, to_modal)


def smoothed(z, sensor, before, after, left, right):
    inner = sensor[:, : z.cols - z.ax]
    outer = sensor[:, z.ax :]
    from_left = jnp.concatenate([left, inner], axis=1)
    from_right = jnp.concatenate([outer, right], axis=1)
    return (4.0 * sensor + before + after + from_left + from_right) / 8.0


def sweep_call(z, chunk, parts, me, state, rhs, viscous, gain, inverse, sensors, lefts, rights, ring, carry, after):
    low, high = chunk
    opened = high == z.steps
    first, size = z.window(low, high)
    count = high - low
    first0, size0 = z.window(0, 1)
    steps = list(range(low, high)) + ([0] if opened else [])
    has_carry = carry is not None
    gains = list(range(low if has_carry else low + 1, high))
    messages = [z.message(stop - start) for start, stop in parts or [chunk]]
    edge_outs = low == 1
    pairs = z.segments // 2
    last, last_size = z.window(low - 2, low - 1)
    batch = next(n for n in (4, 8, z.segments) if z.segments % n == 0 and n * z.steps % TILE == 0)
    narrow = low == 1
    cuts = list(range(0, z.segments + 1, batch))
    if narrow:
        cuts[1:1] = [2]
    batches = list(zip(cuts[:-1], cuts[1:]))

    if parts:
        outs = [f32(pairs, message, z.ax) for message in messages for _ in range(2)]
    else:
        outs = [f32(z.segments, messages[0], z.ax)]

    def kernel(*refs):
        me_ref, state_ref, rhs_ref, viscous_ref, inverse_ref, gain_ref, sensor_ref, left_ref, right_ref = refs[:9]
        refs = refs[9:]
        if opened:
            before_ref, behind_ref, refs = refs[0], refs[1], refs[2:]
        if has_carry:
            carry_ref, refs = refs[0], refs[1:]
        refs = refs[len(after) :]
        out_refs, refs = refs[: len(outs)], refs[len(outs) :]
        if opened:
            end_ref, start_ref, refs = refs[0], refs[1], refs[2:]
        if edge_outs:
            low_ref, high_ref, refs = refs[0], refs[1], refs[2:]
        state_buf, rhs_buf, inverse_buf, gain_buf, viscous_buf, smooth_buf, sem, matrix_sem, out_sem = refs[:9]
        stages, refs = refs[9 : 9 + len(messages)], refs[9 + len(messages) :]
        if opened:
            state0, rhs0, refs = refs[0], refs[1], refs[2:]
        if has_carry:
            carry_buf = refs[0]
        viscous_copy = pltpu.make_async_copy(viscous_ref, viscous_buf, out_sem.at[0, 0])
        viscous_copy.start()
        copies = [[] for _ in range(z.segments)]
        for s0, s1 in batches:
            for s in range(s0, s1):
                moves = [
                    (state_ref.at[s, pl.ds(first, size)], state_buf.at[s, pl.ds(0, size)]),
                    (rhs_ref.at[s, pl.ds(first, size)], rhs_buf.at[s, pl.ds(0, size)]),
                ]
                if opened:
                    moves.append((state_ref.at[s, pl.ds(first0, size0)], state0.at[s, pl.ds(0, size0)]))
                    moves.append((rhs_ref.at[s, pl.ds(first0, size0)], rhs0.at[s, pl.ds(0, size0)]))
                if has_carry:
                    moves.append((carry_ref.at[s, pl.ds(last, last_size)], carry_buf.at[s, pl.ds(0, last_size)]))
                if narrow:
                    for source, target, needed in ((inverse_ref, inverse_buf, steps), (gain_ref, gain_buf, gains)):
                        if needed:
                            part = pl.ds(s * z.steps + needed[0], len(needed))
                            moves.append((source.at[:, part], target.at[pl.ds(0, z.nodes), part]))
                for n, (source, target) in enumerate(moves):
                    copies[s].append(pltpu.make_async_copy(source, target, sem.at[s, n]))
            if not narrow:
                part = pl.ds(s0 * z.steps, (s1 - s0) * z.steps)
                for n, (source, target) in enumerate(((inverse_ref, inverse_buf), (gain_ref, gain_buf))):
                    copy = pltpu.make_async_copy(
                        source.at[:, part], target.at[pl.ds(0, z.nodes), part], matrix_sem.at[s0, n]
                    )
                    copies[s0].append(copy)
            for s in range(s0, s1):
                for copy in copies[s]:
                    copy.start()
        for n, i in enumerate(steps):
            before = sensor_ref[(i - 1) % z.steps]
            later = sensor_ref[(i + 1) % z.steps]
            if i == 0:
                before = jnp.concatenate([before_ref[...], before[: z.segments - 1]], axis=0)
            if i == z.steps - 1:
                later = jnp.concatenate([later[1:], behind_ref[...]], axis=0)
            smooth_buf[n] = smoothed(z, sensor_ref[i], before, later, left_ref[i], right_ref[i])
        if edge_outs:
            low_ref[...] = sensor_ref[0, :1]
            high_ref[...] = sensor_ref[z.steps - 1, z.segments - 1 :]
        viscous_copy.wait()
        operator = operand_left(z.square(viscous_buf[...]))
        sends = []

        for s0, s1 in batches:
            group = range(s0, s1)
            for s in group:
                for copy in copies[s]:
                    copy.wait()
            sources = []
            for n, i in enumerate(steps):
                bufs = (state0, rhs0, -first0) if i == 0 else (state_buf, rhs_buf, i * z.height - first)
                moved = [product(operator, operand_right(read_field(z, bufs[0], (s,), bufs[2]))) for s in group]
                forces = [
                    operand_right(read_field(z, bufs[1], (s,), bufs[2]) + smooth_buf[n, s : s + 1, :] * value)
                    for s, value in zip(group, moved)
                ]
                sources.append(forces)
            for n, i in enumerate(steps):
                sources[n] = [
                    product(operand_left(read_matrix(z, inverse_buf, s * z.steps + i)), force)
                    for s, force in zip(group, sources[n])
                ]
            fields = None
            if has_carry:
                fields = [read_field(z, carry_buf, (s,), (low - 2) * z.height - last) for s in group]
            for n, i in enumerate(steps):
                values = sources[n]
                if i == 0:
                    for s, value in zip(group, values):
                        start_ref[s] = value
                    continue
                if fields is not None:
                    swept = [
                        product(operand_left(read_matrix(z, gain_buf, s * z.steps + i)), operand_right(field))
                        for s, field in zip(group, fields)
                    ]
                    values = [value + more for value, more in zip(values, swept)]
                fields = values
                for s, value in zip(group, values):
                    for (start, stop), stage in zip(parts or [chunk], stages):
                        if start <= i < stop:
                            write_field(z, stage, (s,), (i - start) * z.height, value)
            for s, value in zip(group, fields):
                if opened:
                    end_ref[s] = value
                if not parts:
                    copy = pltpu.make_async_copy(
                        stages[0].at[s, pl.ds(0, messages[0])], out_refs[0].at[s], out_sem.at[0, s]
                    )
                    copy.start()
                    sends.append(copy)
            for p, stage in enumerate(stages if parts else []):
                for s in group:
                    keep_ref, give_ref = out_refs[2 * p], out_refs[2 * p + 1]
                    sends.append(send_pair(z, me_ref[0], s, stage, keep_ref, give_ref, out_sem.at[p]))
        for copy in sends:
            copy.wait()

    field = f32(z.segments, z.pad, z.cols)
    out_specs = [spec_hbm()] * len(outs)
    more = [field] * (2 if opened else 0) + ([f32(1, z.cols)] * 2 if edge_outs else [])
    operands = [me, state, rhs, viscous, inverse, gain, sensors, lefts, rights]
    in_specs = [spec_smem()] + [spec_hbm()] * 5 + [spec_vmem()] * 3
    extra = list(ring) if opened else []
    extra_specs = [spec_vmem()] * len(extra)
    if has_carry:
        extra.append(carry)
        extra_specs.append(spec_hbm())
    scratch = [
        pltpu.VMEM((z.segments, size + z.spill, z.ax), F32),
        pltpu.VMEM((z.segments, size + z.spill, z.ax), F32),
        pltpu.VMEM((z.pad,) + inverse.shape[1:], F32),
        pltpu.VMEM((z.pad,) + gain.shape[1:], F32),
        pltpu.VMEM(viscous.shape, F32),
        pltpu.VMEM((len(steps), z.segments, z.cols), F32),
        pltpu.SemaphoreType.DMA((z.segments, 7)),
        pltpu.SemaphoreType.DMA((z.segments, 2)),
        pltpu.SemaphoreType.DMA((len(messages), z.segments)),
    ]
    scratch += [pltpu.VMEM((z.segments, message + z.spill, z.ax), F32) for message in messages]
    if opened:
        scratch += [pltpu.VMEM((z.segments, size0 + z.spill, z.ax), F32)] * 2
    if has_carry:
        scratch.append(pltpu.VMEM((z.segments, last_size + z.spill, z.ax), F32))
    return call(
        kernel,
        f"sweep_{low}",
        outs + more,
        in_specs + extra_specs + [spec_any()] * len(after),
        out_specs + [spec_vmem()] * len(more),
        scratch,
        z.flops * len(steps) * z.segments * 3,
        4 * z.segments * size * z.ax * 4,
        limit=52,
    )(*operands, *extra, *after)


def maps_call(z, me, gain, after):
    def kernel(me_ref, gain_ref, *refs):
        own_ref, head_ref, tail_ref, whole_ref, prefix_ref, group_ref, gain_buf, kept, sem = refs[len(after) :]
        copy = pltpu.make_async_copy(gain_ref, gain_buf.at[pl.ds(0, z.nodes)], sem)
        copy.start()
        copy.wait()

        def times(a, b):
            return product(operand_left(a), operand_right(b))

        values = [read_matrix(z, gain_buf, e * z.steps + 1) for e in range(z.segments)]
        for i in range(1, z.steps):
            if i > 1:
                values = [
                    times(read_matrix(z, gain_buf, e * z.steps + i), values[e]) for e in range(z.segments)
                ]
            for e in range(z.segments):
                kept[e, i] = values[e]
        heads = [read_matrix(z, gain_buf, e * z.steps) for e in range(z.segments)]
        for e in range(z.segments):
            kept[e, 0] = heads[e]
            head_ref[e] = heads[e]
            tail_ref[e] = values[e]
            whole_ref[e] = times(values[e], heads[e])
        own_ref[...] = kept[me_ref[0]]
        value = whole_ref[0]
        prefix_ref[0] = value
        for e in range(1, z.segments):
            prefix_ref[e] = value
            value = times(whole_ref[e], value)
        group_ref[...] = value

    square = (z.pad, z.pad)
    outs = [f32(z.steps, *square)] + [f32(z.segments, *square)] * 4 + [f32(*square)]
    return call(
        kernel,
        "maps",
        outs,
        [spec_smem(), spec_hbm()] + [spec_any()] * len(after),
        [spec_vmem()] * 6,
        [
            pltpu.VMEM((z.pad,) + gain.shape[1:], F32),
            pltpu.VMEM((z.segments, z.steps) + square, F32),
            pltpu.SemaphoreType.DMA,
        ],
        z.flops * z.segments * (z.steps + 1) // 2,
        4 * z.segments * z.steps * z.pad * z.pad,
        limit=52,
    )(me, gain, *after)


def chain_call(z, starts, ends, tails, wholes, group):
    def kernel(start_ref, end_ref, tail_ref, whole_ref, group_ref, before_ref, pack_ref):
        value = None
        for e in range(z.segments):
            shift = end_ref[e] + product(operand_left(tail_ref[e]), operand_right(start_ref[e]))
            if e > 0:
                before_ref[e] = value
                shift = shift + product(operand_left(whole_ref[e]), operand_right(value))
            else:
                before_ref[0] = jnp.zeros_like(shift)
            value = shift
        pack_ref[:, : z.cols] = value
        pack_ref[:, z.cols :] = group_ref[...]

    return call(
        kernel,
        "chain",
        [f32(z.segments, z.pad, z.cols), f32(z.pad, z.cols + z.pad)],
        [spec_vmem()] * 5,
        [spec_vmem()] * 2,
        [],
        z.flops * z.segments * 2,
        4 * z.segments * z.pad * z.cols * 4,
    )(starts, ends, tails, wholes, group)


def first_call(z, places, packs, before, prefix, heads, starts):
    rows = z.message(1)
    pairs = z.segments // 2

    def kernel(*refs):
        places_ref, refs = refs[0], refs[1:]
        pack_refs, refs = refs[: z.groups], refs[z.groups :]
        before_ref, prefix_ref, head_ref, start_ref, keep_ref, give_ref, stage, sem = refs
        mine = places_ref[0]
        group = places_ref[1]
        value = jnp.zeros((z.pad, z.cols), F32)
        matrices = [operand_left(ref[:, z.cols :]) for ref in pack_refs]
        for t in range(2 * z.groups - 1, 0, -1):
            n = t % z.groups
            moved = product(matrices[n], operand_right(value)) + pack_refs[n][:, : z.cols]
            value = jnp.where(t <= z.groups + group, moved, 0.0)
        incoming = operand_right(value)
        arriving = [value] + [
            before_ref[e] + product(operand_left(prefix_ref[e]), incoming) for e in range(1, z.segments)
        ]
        solved = [
            start_ref[e] + product(operand_left(head_ref[e]), operand_right(arriving[e])) for e in range(z.segments)
        ]
        for e in range(z.segments):
            write_field(z, stage, (e,), 0, solved[e])
        sends = [send_pair(z, mine, e, stage, keep_ref, give_ref, sem) for e in range(z.segments)]
        for copy in sends:
            copy.wait()

    return call(
        kernel,
        "first",
        [f32(pairs, rows, z.ax)] * 2,
        [spec_smem()] + [spec_vmem()] * (z.groups + 4),
        [spec_hbm()] * 2,
        [pltpu.VMEM((z.segments, rows + z.spill, z.ax), F32), pltpu.SemaphoreType.DMA((z.segments,))],
        z.flops * (z.segments * 2 + 2 * z.groups),
        4 * z.segments * z.pad * z.cols * 4,
    )(places, *packs, before, prefix, heads, starts)


def couple_call(z, keep, got):
    pairs, message, _ = keep.shape

    def kernel(*refs):
        sources, refs = refs[:2], refs[2:]
        outs, buf, sem = refs[:pairs], refs[pairs], refs[pairs + 1]
        loads = [
            [pltpu.make_async_copy(sources[n].at[d], buf.at[d, n], sem.at[d, n]) for n in range(2)]
            for d in range(pairs)
        ]
        for load in loads:
            for copy in load:
                copy.start()
        stores = []
        for d in range(pairs):
            for copy in loads[d]:
                copy.wait()
            copy = pltpu.make_async_copy(buf.at[d], outs[d], sem.at[d, 0])
            copy.start()
            stores.append(copy)
        for copy in stores:
            copy.wait()

    return call(
        kernel,
        "couple",
        [f32(2, message, z.ax)] * pairs,
        [spec_hbm()] * 2,
        [spec_hbm()] * pairs,
        [pltpu.VMEM((pairs, 2, message, z.ax), F32), pltpu.SemaphoreType.DMA((pairs, 2))],
        0,
        4 * 4 * pairs * message * z.ax,
    )(keep, got)


def gate_call(held, after):
    def kernel(*refs):
        pass

    return call(
        kernel,
        "gate",
        f32(*held.shape),
        [spec_hbm(), spec_any()],
        spec_hbm(),
        [],
        0,
        0,
        {0: 0},
    )(held, after)


def open_call(z, one, me, own, received_one, received_first):
    radial = z.segments * z.rows
    tall = z.nodes * radial
    operand_shape = (z.segments, 2 * z.pad, z.cols)
    low, high = one
    pairs = z.segments // 2
    message = received_first[0].shape[1]

    def kernel(me_ref, own_ref, one_ref, *refs):
        first_refs, refs = refs[:pairs], refs[pairs:]
        out_ref, operand_ref, own_buf, one_buf, first_buf, stage, one_sem, first_sem, own_sem, out_sem = refs
        first_copies = load_pairs(z, me_ref[0], first_refs, first_buf, first_sem)
        one_copies = [
            pltpu.make_async_copy(one_ref.at[e], one_buf.at[e, pl.ds(0, one_ref.shape[1])], one_sem.at[e])
            for e in range(z.segments)
        ]
        own_copy = pltpu.make_async_copy(own_ref, own_buf, own_sem)
        for copy in first_copies + [own_copy] + one_copies:
            copy.start()
        for copy in first_copies:
            copy.wait()
        sends = []

        def put(i, e, value):
            for j in range(z.rows):
                rows = pl.ds(e * z.rows + j, z.nodes, stride=radial)
                stage[i, rows, :] = value[: z.nodes, j * z.ax : (j + 1) * z.ax]

        def send(i):
            copy = pltpu.make_async_copy(stage.at[i, pl.ds(0, tall)], out_ref.at[i], out_sem.at[i])
            copy.start()
            sends.append(copy)

        for e in range(z.segments):
            field = read_exact(z, first_buf, (e,), 0)
            empty = jnp.zeros((z.pad - z.nodes, z.cols), F32)
            operand_ref[e] = operand_right(jnp.concatenate([field, empty], axis=0))
            put(0, e, field)
        send(0)
        own_copy.wait()
        for copy in one_copies:
            copy.wait()
        for i in range(low, high):
            matrix = operand_left(own_buf[i])
            for e in range(z.segments):
                value = product(matrix, operand_ref[e])[: z.nodes]
                put(i, e, value + read_exact(z, one_buf, (e,), (i - low) * z.height))
            send(i)
        for copy in sends:
            copy.wait()

    return call(
        kernel,
        "finish_0",
        [f32(z.steps, tall, z.ax), jax.ShapeDtypeStruct(operand_shape, BF16)],
        [spec_smem()] + [spec_hbm()] * (2 + pairs),
        [spec_hbm(), spec_vmem()],
        [
            pltpu.VMEM((z.steps, z.pad, z.pad), F32),
            pltpu.VMEM((z.segments, received_one.shape[1] + z.spill, z.ax), F32),
            pltpu.VMEM((z.segments, message + z.spill, z.ax), F32),
            pltpu.VMEM((high, tall + z.tail, z.ax), F32),
            pltpu.SemaphoreType.DMA((z.segments,)),
            pltpu.SemaphoreType.DMA((z.segments,)),
            pltpu.SemaphoreType.DMA,
            pltpu.SemaphoreType.DMA((high,)),
        ],
        z.flops * (high - 1) * z.segments,
        4 * 2 * high * tall * z.ax,
    )(me, own, received_one, *received_first)


def finish_call(z, chunk, me, own, messages, operands, out):
    low, high = chunk
    count = high - low
    radial = z.segments * z.rows
    tall = z.nodes * radial
    message = messages[0].shape[1]

    def kernel(me_ref, own_ref, operand_ref, *refs):
        message_refs, refs = refs[: len(messages)], refs[len(messages) :]
        _, out_ref, buf, own_buf, operand_buf, stage, sem, in_sem, out_sem = refs
        own_copy = pltpu.make_async_copy(own_ref.at[pl.ds(low, count)], own_buf, in_sem.at[0])
        operand_copy = pltpu.make_async_copy(operand_ref, operand_buf, in_sem.at[1])
        own_copy.start()
        operand_copy.start()
        copies = load_pairs(z, me_ref[0], message_refs, buf, sem)
        for copy in copies:
            copy.start()
        own_copy.wait()
        operand_copy.wait()
        for copy in copies:
            copy.wait()
        sends = []
        for n in range(count):
            matrix = operand_left(own_buf[n])
            for e in range(z.segments):
                value = product(matrix, operand_buf[e])[: z.nodes] + read_exact(z, buf, (e,), n * z.height)
                for j in range(z.rows):
                    rows = pl.ds(e * z.rows + j, z.nodes, stride=radial)
                    stage[n, rows, :] = value[:, j * z.ax : (j + 1) * z.ax]
            copy = pltpu.make_async_copy(stage.at[n, pl.ds(0, tall)], out_ref.at[low + n], out_sem.at[n])
            copy.start()
            sends.append(copy)
        for copy in sends:
            copy.wait()

    inputs = [me, own, operands] + list(messages) + [out]
    return call(
        kernel,
        f"finish_{low}",
        f32(z.steps, tall, z.ax),
        [spec_smem()] + [spec_hbm()] * (len(inputs) - 1),
        spec_hbm(),
        [
            pltpu.VMEM((z.segments, message + z.spill, z.ax), F32),
            pltpu.VMEM((count, z.pad, z.pad), F32),
            pltpu.VMEM(operands.shape, BF16),
            pltpu.VMEM((count, tall + z.tail, z.ax), F32),
            pltpu.SemaphoreType.DMA((z.segments,)),
            pltpu.SemaphoreType.DMA((2,)),
            pltpu.SemaphoreType.DMA((count,)),
        ],
        z.flops * count * z.segments,
        4 * 2 * count * tall * z.ax,
        {len(inputs) - 1: 0},
    )(*inputs)


def close_call(z, step, me, own, messages, operands, out):
    radial = z.segments * z.rows
    tall = z.nodes * radial
    pairs = z.segments // 2

    def kernel(me_ref, own_ref, operand_ref, *refs):
        message_refs = refs[:pairs]
        _, out_ref, stage, out_sem = refs[pairs:]
        matrix = operand_left(own_ref[step])
        mine = me_ref[0]
        side = lax.rem(mine, 2)
        for d in range(pairs):
            pair = lax.rem(mine // 2 - d + pairs, pairs) * 2
            for n in range(2):
                e = pair + (side if n == 0 else 1 - side)
                value = product(matrix, operand_ref[e])[: z.nodes] + read_exact(z, message_refs[d], (n,), 0)
                for j in range(z.rows):
                    rows = pl.ds(e * z.rows + j, z.nodes, stride=radial)
                    stage[rows, :] = value[:, j * z.ax : (j + 1) * z.ax]
        copy = pltpu.make_async_copy(stage.at[pl.ds(0, tall)], out_ref.at[step], out_sem)
        copy.start()
        copy.wait()

    inputs = [me, own, operands] + list(messages) + [out]
    return call(
        kernel,
        f"finish_{step}",
        f32(z.steps, tall, z.ax),
        [spec_smem()] + [spec_vmem()] * (2 + pairs) + [spec_hbm()],
        spec_hbm(),
        [pltpu.VMEM((tall + z.tail, z.ax), F32), pltpu.SemaphoreType.DMA],
        z.flops * z.segments,
        4 * 2 * tall * z.ax,
        {len(inputs) - 1: 0},
        limit=36,
    )(*inputs)


def shift_by(array, axis, by):
    size = lax.axis_size(axis)
    return lax.ppermute(array, axis, [(i, (i + by) % size) for i in range(size)])


def neighbours(head, tail):
    size = lax.axis_size("elem")
    left = lax.ppermute(tail, "elem", [(i, i + 1) for i in range(size - 1)])
    right = lax.ppermute(head, "elem", [(i + 1, i) for i in range(size - 1)])
    return left, right


def spread(messages):
    return lax.all_to_all(messages, "elem", 0, 0, tiled=True)


def spread_pairs(z, keep, give, after):
    got = lax.ppermute(give, "elem", [(i, i ^ 1) for i in range(z.segments)])
    coupled = couple_call(z, keep, got)
    moved = [coupled[0]]
    for d in range(1, z.segments // 2):
        held = coupled[d] if after is None else gate_call(coupled[d], after[d])
        moved.append(shift_by(held, "elem", 2 * d))
    return moved


def chunks_of(steps):
    middle = 4 if steps >= 8 else 2
    last = steps - 1
    parts = [(middle, last), (last, steps)] if last > middle else [(middle, steps)]
    return (1, middle), (middle, steps), parts


def body(state, rhs, to_modal, viscous_op, sweep_gain, inv_blocks):
    segments = lax.axis_size("elem")
    groups = lax.axis_size("blk")
    z = Sizes(state, segments, groups)
    state = state.reshape(segments, z.steps * z.height, z.ax)
    rhs = rhs.reshape(segments, z.steps * z.height, z.ax)
    gain = jnp.transpose(sweep_gain, (1, 0, 2))
    inverse = jnp.transpose(inv_blocks, (1, 0, 2))
    here = lax.axis_index("elem").astype(jnp.int32)
    me = here.reshape(1)
    places = jnp.stack([here, lax.axis_index("blk").astype(jnp.int32)])
    one, two, parts = chunks_of(z.steps)
    sensors, head, tail = sensor_call(z, state, to_modal)
    lefts, rights = neighbours(head, tail)

    def sweep(chunk, parts, ring, carry, after):
        return sweep_call(
            z, chunk, parts, me, state, rhs, viscous_op, gain, inverse, sensors, lefts, rights, ring, carry, after
        )

    messages_one, low, high = sweep(one, [], None, None, [])
    ring = [shift_by(high, "blk", 1), shift_by(low, "blk", -1)]
    own, heads, tails, wholes, prefix, group = maps_call(z, me, gain, [messages_one])
    *pairs, ends, starts = sweep(two, parts, ring, messages_one, [group])
    before, pack = chain_call(z, starts, ends, tails, wholes, group)
    packs = [pack] + [shift_by(pack, "blk", s) for s in range(1, groups)]
    keep_first, give_first = first_call(z, places, packs, before, prefix, heads, starts)
    received_one = spread(messages_one)
    received_first = spread_pairs(z, keep_first, give_first, None)
    out, operands = open_call(z, one, me, own, received_one, received_first)
    after = received_first
    for n, part in enumerate(parts):
        received = spread_pairs(z, pairs[2 * n], pairs[2 * n + 1], after)
        if part == (z.steps - 1, z.steps):
            out = close_call(z, part[0], me, own, received, operands, out)
        else:
            out = finish_call(z, part, me, own, received, operands, out)
        after = [received[1]] * len(received)
    return out.reshape(z.steps, z.nodes, segments * z.rows, z.ax)


def solution(mesh):
    in_specs = (
        P("blk", None, "elem", None),
        P("blk", None, "elem", None),
        P(),
        P(),
        P("blk", None, None),
        P("blk", None, None),
    )
    out_specs = P(("blk", "elem"), None, None, None)
    return jax.shard_map(body, mesh=mesh, in_specs=in_specs, out_specs=out_specs, check_vma=False)
```
